128 devices in a mesh: lon: 16 (over z, y_lo, core), lat: 8 (over x, y_hi).
Axes of the slice: x: 4, y: 4 (y_hi: 2, y_lo: 2; y = y_hi * 2 + y_lo), z: 4, core: 2. Of those that a mesh axis runs over, the one named last changes fastest.
Arguments:
- east_velocity: float32 [16, 1216, 4096], P(None, 'lat', 'lon'), may hold values from -3 to 3
- north_velocity: float32 [16, 1216, 4096], P(None, 'lat', 'lon'), may hold values from -3 to 3
- heat_anomaly: float32 [16, 1216, 4096], P(None, 'lat', 'lon'), may hold values from -6 to 6
- haline_anomaly: float32 [16, 1216, 4096], P(None, 'lat', 'lon'), may hold values from -6 to 6
- spacing_lengths: float32 [6, 1216, 4096], P(None, 'lat', 'lon'), may hold values from 0.5 to 2
- planetary_spin: float32 [2, 1216, 4096], P(None, 'lat', 'lon'), may hold values from -1.5 to 1.5
- ocean_layer_number: int32 [1216, 4096], P('lat', 'lon'), may hold values from 0 to 16
- seam_partner_index: int32 [4096], replicated, may hold values from 0 to 4095, as said below
Outputs:
- stepped_zonal_speed: float32 [16, 1216, 4096], P(None, 'lat', 'lon')
- meridional_next: float32 [16, 1216, 4096], P(None, 'lat', 'lon')
- stepped_heat: float32 [16, 1216, 4096], P(None, 'lat', 'lon')
The draws below stay inside these ranges and needn't reach their ends.
Inputs may be any that keep to these rules, and one draw needn't show every extreme that they name: `seam_partner_index`: for a column in longitude block b of 256 columns, its partner lies in block 15 - b; every column is the partner of exactly one column.
All inputs are finite; a program needn't handle non-finite values.
Results may differ from the reference program's by a relative error of at most 0.0003.
Values sent between devices are 32-bit elements; how exact they have to be, the bound alone decides.
No kernel may reach another device: no remote copies, remote signals or barrier semaphores. Data moves between devices by JAX's collectives and lax.ppermute only.
A program may use at most 192 MiB of HBM per device.

```python
import math
import jax
import jax.numpy as jnp

COL_DEV = 256
STRATA_NUMBER = 16
HALO = 2
LONGITUDE_SPAN = 4096
LATITUDE_SPAN = 1216


def draw_seam_partner_index(key, part):
    key = jax.random.fold_in(key, 7)
    blocks = LONGITUDE_SPAN // COL_DEV
    keys = jax.random.split(key, blocks)
    local = jax.vmap(lambda single: jax.random.permutation(single, COL_DEV))(keys).astype(jnp.int32)
    base = (blocks - 1 - jnp.arange(blocks, dtype=jnp.int32))[:, None] * COL_DEV
    return (base + local).reshape(-1).astype(jnp.int32)


def place_ends(result, stream_key, low, largest):
    spot = [jax.random.randint(jax.random.fold_in(stream_key, axis), (), 0, length) for axis, length in enumerate(result.shape)]
    main_axis = result.shape.index(max(result.shape))
    next_to = spot[:main_axis] + [(spot[main_axis] + 1) % result.shape[main_axis]] + spot[main_axis + 1:]
    return result.at[tuple(spot)].set(low).at[tuple(next_to)].set(largest)


def steps_of(own_key, extent, cuts, least, top_value):
    def one(dim, blocks):
        heights = jax.random.uniform(jax.random.fold_in(jax.random.fold_in(own_key, 6), dim), (blocks,), jnp.float32, least / len(cuts), top_value / len(cuts))
        return jnp.repeat(jnp.exp(heights), extent[dim] // blocks).reshape((-1,) + (1,) * (len(extent) - dim - 1))

    gain = one(*cuts[0])
    for cut in cuts[1:]:
        gain = gain * one(*cut)
    return gain


def gaussian(key, dims, deviation, limit, pieces=(), held_as=jnp.bfloat16):
    values = jax.random.normal(key, dims, jnp.float32) * deviation
    if len(pieces) > 0:
        values = steps_of(key, dims, pieces, -0.22, 0.18) * values
    return jnp.clip(values, min=-limit, max=limit).astype(held_as)


def setup_inputs(seed: int = 0) -> dict:
    seeds = jax.random.split(jax.random.key(seed), 9)
    east_velocity = gaussian(seeds[0], (STRATA_NUMBER, LATITUDE_SPAN, LONGITUDE_SPAN), 0.5, 3.0, ((1, 8), (2, 16)), jnp.float32)
    north_velocity = gaussian(seeds[1], (STRATA_NUMBER, LATITUDE_SPAN, LONGITUDE_SPAN), 0.5, 3.0, ((1, 8), (2, 16)), jnp.float32)
    heat_anomaly = gaussian(seeds[2], (STRATA_NUMBER, LATITUDE_SPAN, LONGITUDE_SPAN), 1.0, 6.0, ((1, 8), (2, 16)), jnp.float32)
    haline_anomaly = gaussian(seeds[3], (STRATA_NUMBER, LATITUDE_SPAN, LONGITUDE_SPAN), 1.0, 6.0, ((1, 8), (2, 16)), jnp.float32)
    spacing_lengths = jnp.clip(jnp.exp(math.log(2.0) - 1.3862944 * jax.random.uniform(seeds[4], (6, LATITUDE_SPAN, LONGITUDE_SPAN), jnp.float32) ** steps_of(seeds[4], (6, LATITUDE_SPAN, LONGITUDE_SPAN), ((1, 8), (2, 16)), -0.2, 0.2)), 0.5, 2.0)
    planetary_spin = jnp.clip(jax.random.uniform(seeds[5], (2, LATITUDE_SPAN, LONGITUDE_SPAN), jnp.float32, -1.5, 1.5) * steps_of(seeds[5], (2, LATITUDE_SPAN, LONGITUDE_SPAN), ((1, 8), (2, 16)), -0.4, 0.0), -1.5, 1.5)
    ocean_layer_number = place_ends(jax.random.randint(seeds[6], (LATITUDE_SPAN, LONGITUDE_SPAN), 0, STRATA_NUMBER + 1), jax.random.fold_in(seeds[6], 1), 0, STRATA_NUMBER).astype(jnp.int32)
    seam_partner_index = draw_seam_partner_index(jax.random.fold_in(seeds[8], 71), 0)
    return {"east_velocity": east_velocity, "north_velocity": north_velocity, "heat_anomaly": heat_anomaly, "haline_anomaly": haline_anomaly, "spacing_lengths": spacing_lengths, "planetary_spin": planetary_spin, "ocean_layer_number": ocean_layer_number, "seam_partner_index": seam_partner_index}


step_duration = 0.25
viscosity = 0.05
diffusivity = 0.3
expansion_coefficient = 0.6
haline_contraction = 0.8
gravity = 0.1
slope_taper = 1.0


def upward_contribution(field):
    padded = jnp.concatenate([field[:1], field, field[-1:]], axis=0)
    return 0.5 * (padded[2:] - padded[:-2])


def stencil_shape(east_velocity, north_velocity, heat_anomaly, haline_anomaly, spacing_coefficients, latitude_points, longitude_points):
    def stencil_patch(field, latitude_shift, longitude_shift):
        return field[..., HALO + latitude_shift:HALO + latitude_shift + latitude_points, HALO + longitude_shift:HALO + longitude_shift + longitude_points]

    depth_count = east_velocity.shape[0]
    level_index = jnp.arange(depth_count, dtype=jnp.float32)[:, None, None]
    wet_mask = (level_index < spacing_coefficients[8][None]).astype(jnp.float32)
    seawater_mass_per_volume = haline_contraction * haline_anomaly - expansion_coefficient * heat_anomaly
    heat_upward_slope = upward_contribution(heat_anomaly)
    density_z = upward_contribution(seawater_mass_per_volume)
    pressure = gravity * (jnp.cumsum(seawater_mass_per_volume, axis=0) - 0.5 * seawater_mass_per_volume)

    def umask(latitude_shift, longitude_shift):
        return stencil_patch(wet_mask, latitude_shift, longitude_shift) * stencil_patch(wet_mask, latitude_shift, longitude_shift + 1)

    def northward_mask(latitude_shift, longitude_shift):
        return stencil_patch(wet_mask, latitude_shift, longitude_shift) * stencil_patch(wet_mask, latitude_shift + 1, longitude_shift)

    def east_face(latitude_shift, longitude_shift):
        e1u = stencil_patch(spacing_coefficients[2], latitude_shift, longitude_shift)
        e2u = stencil_patch(spacing_coefficients[3], latitude_shift, longitude_shift)
        current_mask = umask(latitude_shift, longitude_shift)
        present_point = stencil_patch(heat_anomaly, latitude_shift, longitude_shift)
        nearby_point = stencil_patch(heat_anomaly, latitude_shift, longitude_shift + 1)
        scalar_interface = (7.0 * (present_point + nearby_point) - (stencil_patch(heat_anomaly, latitude_shift, longitude_shift - 1) + stencil_patch(heat_anomaly, latitude_shift, longitude_shift + 2))) / 12.0
        advect = e2u * stencil_patch(east_velocity, latitude_shift, longitude_shift) * scalar_interface * current_mask
        rz_face = 0.5 * (stencil_patch(density_z, latitude_shift, longitude_shift) + stencil_patch(density_z, latitude_shift, longitude_shift + 1))
        heat_interface = 0.5 * (stencil_patch(heat_upward_slope, latitude_shift, longitude_shift) + stencil_patch(heat_upward_slope, latitude_shift, longitude_shift + 1))
        slope = (stencil_patch(seawater_mass_per_volume, latitude_shift, longitude_shift + 1) - stencil_patch(seawater_mass_per_volume, latitude_shift, longitude_shift)) / e1u * rz_face / (rz_face * rz_face + slope_taper)
        isoflux = diffusivity * current_mask * e2u * ((nearby_point - present_point) / e1u - slope * heat_interface)
        return advect, isoflux

    def north_face(latitude_shift, longitude_shift):
        e1v = stencil_patch(spacing_coefficients[4], latitude_shift, longitude_shift)
        e2v = stencil_patch(spacing_coefficients[5], latitude_shift, longitude_shift)
        current_mask = northward_mask(latitude_shift, longitude_shift)
        present_point = stencil_patch(heat_anomaly, latitude_shift, longitude_shift)
        nearby_point = stencil_patch(heat_anomaly, latitude_shift + 1, longitude_shift)
        scalar_interface = (7.0 * (present_point + nearby_point) - (stencil_patch(heat_anomaly, latitude_shift - 1, longitude_shift) + stencil_patch(heat_anomaly, latitude_shift + 2, longitude_shift))) / 12.0
        advect = e1v * stencil_patch(north_velocity, latitude_shift, longitude_shift) * scalar_interface * current_mask
        rz_face = 0.5 * (stencil_patch(density_z, latitude_shift, longitude_shift) + stencil_patch(density_z, latitude_shift + 1, longitude_shift))
        heat_interface = 0.5 * (stencil_patch(heat_upward_slope, latitude_shift, longitude_shift) + stencil_patch(heat_upward_slope, latitude_shift + 1, longitude_shift))
        slope = (stencil_patch(seawater_mass_per_volume, latitude_shift + 1, longitude_shift) - stencil_patch(seawater_mass_per_volume, latitude_shift, longitude_shift)) / e2v * rz_face / (rz_face * rz_face + slope_taper)
        isoflux = diffusivity * current_mask * e1v * ((nearby_point - present_point) / e2v - slope * heat_interface)
        return advect, isoflux

    adv_east, iso_east = east_face(0, 0)
    adv_west, iso_west = east_face(0, -1)
    adv_north, iso_north = north_face(0, 0)
    adv_south, iso_south = north_face(-1, 0)
    area = stencil_patch(spacing_coefficients[0], 0, 0) * stencil_patch(spacing_coefficients[1], 0, 0)
    scalar_change_rate = stencil_patch(wet_mask, 0, 0) * ((iso_east - iso_west + iso_north - iso_south) - (adv_east - adv_west + adv_north - adv_south)) / area
    stepped_heat = stencil_patch(heat_anomaly, 0, 0) + step_duration * scalar_change_rate

    u_mid = stencil_patch(east_velocity, 0, 0)
    e1u = stencil_patch(spacing_coefficients[2], 0, 0)
    e2u = stencil_patch(spacing_coefficients[3], 0, 0)
    v_mean = 0.25 * (stencil_patch(north_velocity, 0, 0) + stencil_patch(north_velocity, 0, 1) + stencil_patch(north_velocity, -1, 0) + stencil_patch(north_velocity, -1, 1))
    u_east = stencil_patch(east_velocity, 0, 1)
    u_west = stencil_patch(east_velocity, 0, -1)
    u_north = stencil_patch(east_velocity, 1, 0)
    u_south = stencil_patch(east_velocity, -1, 0)
    adv_zonal = u_mid * (u_east - u_west) / (2.0 * e1u) + v_mean * (u_north - u_south) / (2.0 * e2u)
    visc_zonal = viscosity * ((u_east + u_west - 2.0 * u_mid) / (e1u * e1u) + (u_north + u_south - 2.0 * u_mid) / (e2u * e2u))
    grad_zonal = (stencil_patch(pressure, 0, 1) - stencil_patch(pressure, 0, 0)) / e1u
    stepped_zonal_speed = u_mid + step_duration * umask(0, 0) * (stencil_patch(spacing_coefficients[6], 0, 0) * v_mean - adv_zonal + visc_zonal - grad_zonal)

    northward_middle = stencil_patch(north_velocity, 0, 0)
    e1v = stencil_patch(spacing_coefficients[4], 0, 0)
    e2v = stencil_patch(spacing_coefficients[5], 0, 0)
    eastward_average = 0.25 * (stencil_patch(east_velocity, 0, 0) + stencil_patch(east_velocity, 0, -1) + stencil_patch(east_velocity, 1, 0) + stencil_patch(east_velocity, 1, -1))
    v_east = stencil_patch(north_velocity, 0, 1)
    v_west = stencil_patch(north_velocity, 0, -1)
    v_north = stencil_patch(north_velocity, 1, 0)
    v_south = stencil_patch(north_velocity, -1, 0)
    meridional_advection = eastward_average * (v_east - v_west) / (2.0 * e1v) + northward_middle * (v_north - v_south) / (2.0 * e2v)
    meridional_friction = viscosity * ((v_east + v_west - 2.0 * northward_middle) / (e1v * e1v) + (v_north + v_south - 2.0 * northward_middle) / (e2v * e2v))
    meridional_gradient = (stencil_patch(pressure, 1, 0) - stencil_patch(pressure, 0, 0)) / e2v
    poleward_following = northward_middle + step_duration * northward_mask(0, 0) * (-stencil_patch(spacing_coefficients[7], 0, 0) * eastward_average - meridional_advection + meridional_friction - meridional_gradient)
    return stepped_zonal_speed, poleward_following, stepped_heat


def channel_signs(depth_count, channel_count):
    index = jnp.arange(channel_count, dtype=jnp.int32)
    return jnp.where(index < 2 * depth_count, -1.0, 1.0).astype(jnp.float32)


def wall_fill(depth_count, channel_count):
    index = jnp.arange(channel_count, dtype=jnp.int32)
    inside = jnp.logical_and(index >= 4 * depth_count, index < 4 * depth_count + 6)
    return jnp.where(inside, 1.0, 0.0).astype(jnp.float32)


def reference(east_velocity, north_velocity, heat_anomaly, haline_anomaly, spacing_lengths, planetary_spin, ocean_layer_number, seam_partner_index):
    depth_count = east_velocity.shape[0]
    bundled_fields = jnp.concatenate([east_velocity, north_velocity, heat_anomaly, haline_anomaly, spacing_lengths, planetary_spin, ocean_layer_number.astype(jnp.float32)[None]], axis=0)
    channel_count, latitude_points, longitude_points = bundled_fields.shape
    wrapped = jnp.concatenate([bundled_fields[..., -HALO:], bundled_fields, bundled_fields[..., :HALO]], axis=2)
    below = jnp.ones((channel_count, HALO, longitude_points + 2 * HALO), jnp.float32) * wall_fill(depth_count, channel_count)[:, None, None]
    columns = jnp.arange(-HALO, longitude_points + HALO, dtype=jnp.int32) % longitude_points
    source = seam_partner_index[columns]
    top_rows = bundled_fields[:, ::-1][:, :HALO]
    folded = top_rows[..., source] * channel_signs(depth_count, channel_count)[:, None, None]
    extended = jnp.concatenate([below, wrapped, folded], axis=1)
    return stencil_shape(extended[:depth_count], extended[depth_count:2 * depth_count], extended[2 * depth_count:3 * depth_count], extended[3 * depth_count:4 * depth_count], extended[4 * depth_count:], latitude_points, longitude_points)
```

```python
import jax
import jax.numpy as jnp
from jax import lax
from jax.experimental import pallas as pl
from jax.experimental.pallas import tpu as pltpu
from jax.sharding import PartitionSpec as P

LANES = 128
TILE = 8

step_duration = 0.25
viscosity = 0.05
diffusivity = 0.3
expansion_coefficient = 0.6
haline_contraction = 0.8
gravity = 0.1

NEAR, FAR, DENS, ZONAL, MERID = 0, 1, 2, 3, 4
E1V_AT, E2V_AT, WET_AT = 0, 1, 2
E1U_LANE, E2U_LANE, WET_LANE = 80, 81, 82


def density_of(salinity, heat):
    return haline_contraction * salinity - expansion_coefficient * heat


def inverse_of(x):
    r = pl.reciprocal(x, approx=True)
    return r * (2.0 - x * r)


def row_pack(t_lo, t_hi, s_lo, s_hi, u_lo, u_hi, v_lo, v_hi, e_lo, e_hi, n_lo, n_hi, first, second):
    levels = t_lo.shape[0]
    even = lax.rem(lax.axis_index("lat"), 2) == 0

    def put(slot, high, low):
        rows = pl.ds(slot * levels, levels)
        first[rows] = jnp.where(even, high, low)
        second[rows] = jnp.where(even, low, high)

    near_hi, near_lo = t_hi[:, 7, :], t_lo[:, 0, :]
    put(NEAR, near_hi, near_lo)
    put(FAR, t_hi[:, 6, :], t_lo[:, 1, :])
    put(DENS, density_of(s_hi[:, 7, :], near_hi), density_of(s_lo[:, 0, :], near_lo))
    put(ZONAL, u_hi[:, 7, :], u_lo[:, 0, :])
    put(MERID, v_hi[:, 7, :], v_lo[:, 0, :])
    base = 5 * levels
    high = jnp.concatenate([e_hi[4, 7:8], e_hi[5, 7:8], n_hi[7:8].astype(jnp.float32), jnp.zeros((5, e_hi.shape[2]), jnp.float32)], axis=0)
    low = jnp.concatenate([e_lo[4, 0:1], e_lo[5, 0:1], n_lo[0:1].astype(jnp.float32), jnp.zeros((5, e_lo.shape[2]), jnp.float32)], axis=0)
    first[base : base + 8] = jnp.where(even, high, low)
    second[base : base + 8] = jnp.where(even, low, high)


def vertical_span(x):
    return jnp.concatenate([x[1:], x[-1:]], axis=0) - jnp.concatenate([x[:1], x[:-1]], axis=0)


def column_pack(group, t, s, u, v, e, n, mine1, mine2, got1, got2, seam, east_out, west_out, north_out, south_out):
    levels = t.shape[0] * pl.num_programs(0)
    rows = t.shape[1]
    cols = t.shape[2]
    lat, lon = lax.axis_index("lat"), lax.axis_index("lon")
    lats, lons = lax.axis_size("lat"), lax.axis_size("lon")
    even = lax.rem(lat, 2) == 0
    step = pl.program_id(0)
    lane = lax.broadcasted_iota(jnp.int32, (rows, LANES), 1)

    @pl.when(step == 0)
    def _():
        is_top = lat == lats - 1
        is_bottom = lat == 0
        north_rows = got1.shape[0]
        for h in range(cols // LANES):
            span = slice(h * LANES, (h + 1) * LANES)
            pick = seam[pl.ds(lon * (cols // LANES) + h, 1), :] - (lons - 1 - lon) * cols
            pick = jnp.where(is_top, pick, lax.broadcasted_iota(jnp.int32, (1, LANES), 1) + h * LANES)
            pick = jnp.broadcast_to(pick, (TILE, LANES))
            inner = jnp.bitwise_and(pick, LANES - 1)
            for row in range(0, north_rows, TILE):
                total = None
                for g in range(cols // LANES):
                    piece = slice(g * LANES, (g + 1) * LANES)
                    source = jnp.where(even, got1[row : row + TILE, piece], got2[row : row + TILE, piece])
                    taken = jnp.take_along_axis(source, inner, axis=1, mode="promise_in_bounds")
                    taken = jnp.where(pick >= g * LANES, taken, 0.0) if g == 0 else taken
                    total = taken if total is None else jnp.where(pick >= g * LANES, taken, total)
                if ZONAL * levels <= row < (MERID + 1) * levels:
                    total = jnp.where(is_top, -total, total)
                north_out[row : row + TILE, span] = total
        def south(slot):
            part = slice(slot * levels, (slot + 1) * levels)
            return jnp.where(is_bottom, 0.0, jnp.where(even, got2[part], got1[part]))

        def own(slot):
            part = slice(slot * levels, (slot + 1) * levels)
            return jnp.where(even, mine2[part], mine1[part])

        tail = slice(5 * levels, 5 * levels + 8)
        coef = jnp.where(even, got2[tail], got1[tail])
        own_wet = jnp.where(even, mine2[tail], mine1[tail])[WET_AT : WET_AT + 1]
        e1v = jnp.where(is_bottom, 1.0, coef[E1V_AT : E1V_AT + 1])
        e2v = jnp.where(is_bottom, 1.0, coef[E2V_AT : E2V_AT + 1])
        wet = jnp.where(is_bottom, 0.0, coef[WET_AT : WET_AT + 1])
        t_near, t_far, d_near, v_near = south(NEAR), south(FAR), south(DENS), south(MERID)
        t_own, t_next, d_own = own(NEAR), own(FAR), own(DENS)
        t_sum = t_near + t_own
        adv = (e1v / 12.0) * v_near * (7.0 * t_sum - (t_far + t_next))
        d_span = vertical_span(d_near + d_own)
        tilt = (d_own - d_near) * d_span * vertical_span(t_sum) / (d_span * d_span + 16.0)
        iso = (diffusivity * e1v / e2v) * (t_own - t_near - tilt)
        level = lax.broadcasted_iota(jnp.int32, (levels, cols), 0).astype(jnp.float32)
        flux = jnp.where(level < jnp.minimum(wet, own_wet), iso - adv, 0.0)
        south_out[0:levels] = t_near
        south_out[levels : 2 * levels] = flux
        south_out[2 * levels : 3 * levels] = south(ZONAL)
        south_out[3 * levels : 4 * levels] = v_near

        n_f = n[...].astype(jnp.float32)
        last = slice(cols - LANES, cols)
        hi = jnp.where(lane == E1U_LANE, pltpu.roll(e[2, :, last], (E1U_LANE + 1) % LANES, 1), 0.0)
        hi = jnp.where(lane == E2U_LANE, pltpu.roll(e[3, :, last], (E2U_LANE + 1) % LANES, 1), hi)
        hi = jnp.where(lane == WET_LANE, pltpu.roll(n_f[:, last], (WET_LANE + 1) % LANES, 1), hi)
        east_out[0:rows] = hi
        west_out[8 : rows + 8] = jnp.where(lane == WET_LANE, pltpu.roll(n_f[:, :LANES], WET_LANE, 1), 0.0)
        sub16 = lax.broadcasted_iota(jnp.int32, (levels, LANES), 0)
        lane16 = lax.broadcasted_iota(jnp.int32, (levels, LANES), 1)
        u_corner = jnp.broadcast_to(north_out[ZONAL * levels : (ZONAL + 1) * levels, cols - 1 : cols], (levels, LANES))
        u_row = jnp.sum(jnp.where(lane16 == sub16 + ZONAL * levels, u_corner, 0.0), axis=0, keepdims=True)
        v_corner = jnp.broadcast_to(v_near[:, 0:1], (levels, LANES))
        v_row = jnp.sum(jnp.where(lane16 == sub16 + MERID * levels, v_corner, 0.0), axis=0, keepdims=True)
        east_out[rows : rows + 8] = jnp.broadcast_to(u_row, (8, LANES))
        west_out[0:8] = jnp.broadcast_to(v_row, (8, LANES))

    first = slice(0, LANES)
    last = slice(cols - LANES, cols)
    hi = east_out[0:rows]
    lo = west_out[8 : rows + 8]
    for kk in range(group):
        k = step * group + kk
        t_hi, t_lo = t[kk, :, last], t[kk, :, first]
        d_hi, d_lo = density_of(s[kk, :, last], t_hi), density_of(s[kk, :, first], t_lo)
        parts = (
            (NEAR, t_hi, 127, t_lo, 0),
            (FAR, t_hi, 126, t_lo, 1),
            (DENS, d_hi, 127, d_lo, 0),
            (ZONAL, u[kk, :, last], 127, u[kk, :, first], 0),
            (MERID, v[kk, :, last], 127, v[kk, :, first], 0),
        )
        for slot, x_hi, at_hi, x_lo, at_lo in parts:
            place = slot * levels + k
            here = lane == place
            hi = jnp.where(here, pltpu.roll(x_hi, lax.rem(place + (2 * LANES - at_hi), LANES), 1), hi)
            lo = jnp.where(here, pltpu.roll(x_lo, lax.rem(place + (2 * LANES - at_lo), LANES), 1), lo)
    east_out[0:rows] = hi
    west_out[8 : rows + 8] = lo


def step_kernel(
    chunks,
    t_hbm, s_hbm, u_hbm, v_hbm, e_hbm, f_hbm, n_hbm, north, south, own_west, from_east, from_west,
    u_out, v_out, t_out,
    t_s, s_s, u_s, v_s, d_s, g_s, far_s, ue_s, uw_s, ve_s, vw_s,
    e_s, f_s, n_s, nf_s, uo_s, vo_s, to_s, shift_s, in_sem, flat_sem, out_sem,
):
    levels, rows, cols = t_hbm.shape
    tiles = rows // TILE
    halves = cols // LANES
    starts = [sum(chunks[:c]) for c in range(len(chunks))]

    def load(c, field, h):
        hbm, vmem = ((t_hbm, t_s), (s_hbm, s_s), (u_hbm, u_s), (v_hbm, v_s))[field]
        span = pl.ds(starts[c] * TILE, chunks[c] * TILE)
        held = pl.ds(starts[c] * TILE + TILE, chunks[c] * TILE)
        return pltpu.make_async_copy(
            hbm.at[:, span, pl.ds(h * LANES, LANES)], vmem.at[h, :, held, :], in_sem.at[c, field, h]
        )

    def store(c, field):
        vmem, hbm = ((uo_s, u_out), (vo_s, v_out), (to_s, t_out))[field]
        span = pl.ds(starts[c] * TILE, chunks[c] * TILE)
        return pltpu.make_async_copy(vmem.at[:, span, :], hbm.at[:, span, :], out_sem.at[c, field])

    flat = [
        pltpu.make_async_copy(hbm, vmem, flat_sem.at[i])
        for i, (hbm, vmem) in enumerate(((e_hbm, e_s), (f_hbm, f_s), (n_hbm, n_s)))
    ]
    flat[2].start()
    for field in range(4):
        for h in range(halves):
            load(0, field, h).start()
    flat[0].start()
    flat[1].start()
    for c in range(1, len(chunks)):
        for field in range(4):
            for h in range(halves):
                load(c, field, h).start()

    source = lax.broadcasted_iota(jnp.int32, (cols, cols), 0)
    target = lax.broadcasted_iota(jnp.int32, (cols, cols), 1)
    for i, moved in enumerate((source == target + 1, source == target - 1, (source == target - 1) | (source == target + 2))):
        shift_s[i] = jnp.where(moved, 1.0, 0.0).astype(jnp.bfloat16)

    def halves_of(x):
        whole = x.astype(jnp.bfloat16)
        return whole, (x - whole.astype(jnp.float32)).astype(jnp.bfloat16)

    def moved(parts, i):
        weights = shift_s[i]
        return sum(jnp.dot(p, weights, preferred_element_type=jnp.float32) for p in parts)

    low, high = TILE - 1, TILE + rows
    for h in range(halves):
        span = slice(h * LANES, (h + 1) * LANES)
        for k in range(levels):
            t_s[h, k, low : low + 1, :] = south[k : k + 1, span]
            g_s[h, k, low : low + 1, :] = south[levels + k : levels + k + 1, span]
            u_s[h, k, low : low + 1, :] = south[2 * levels + k : 2 * levels + k + 1, span]
            v_s[h, k, low : low + 1, :] = south[3 * levels + k : 3 * levels + k + 1, span]
            t_s[h, k, high : high + 1, :] = north[NEAR * levels + k : NEAR * levels + k + 1, span]
            t_s[h, k, high + 1 : high + 2, :] = north[FAR * levels + k : FAR * levels + k + 1, span]
            d_s[h, k, high : high + 1, :] = north[DENS * levels + k : DENS * levels + k + 1, span]
            u_s[h, k, high : high + 1, :] = north[ZONAL * levels + k : ZONAL * levels + k + 1, span]
            v_s[h, k, high : high + 1, :] = north[MERID * levels + k : MERID * levels + k + 1, span]
        nf_s[h, rows : rows + 1, :] = north[5 * levels + WET_AT : 5 * levels + WET_AT + 1, span]
    flat[2].wait()
    for h in range(halves):
        nf_s[h, 0:rows, :] = n_s[:, h * LANES : (h + 1) * LANES].astype(jnp.float32)
    for field in range(4):
        for h in range(halves):
            load(0, field, h).wait()

    def make_density(r):
        at = pl.ds(pl.multiple_of(r * TILE + TILE, TILE), TILE)
        for h in range(halves):
            for k in range(levels):
                d_s[h, k, at, :] = density_of(s_s[h, k, at, :], t_s[h, k, at, :])

    lane = lax.broadcasted_iota(jnp.int32, (TILE, LANES), 1)
    is_last = lane == LANES - 1
    is_first = lane == 0
    both = range(halves)

    def to_lane(x, source, target):
        return pltpu.roll(x, (target - source) % LANES, 1)

    def east_of(x, halo, source):
        turned = [pltpu.roll(p, LANES - 1, 1) for p in x] + [to_lane(halo, source, LANES - 1)]
        return [jnp.where(is_last, turned[h + 1], turned[h]) for h in both]

    def west_of(x, halo, source):
        turned = [to_lane(halo, source, 0)] + [pltpu.roll(p, 1, 1) for p in x]
        return [jnp.where(is_first, turned[h], turned[h + 1]) for h in both]

    def mix(r):
        row = pl.multiple_of(r * TILE, TILE)
        at = pl.ds(row + TILE, TILE)
        east = from_east[at, :]
        west = from_west[pl.ds(row, TILE), :]
        order = jnp.bitwise_and(lane, 1) * levels + lax.shift_right_logical(lane, 1)
        pair = jnp.take_along_axis(east, order, axis=1, mode="promise_in_bounds")

        def of(ref):
            x = jnp.concatenate([ref[h, :, at, :] for h in both], axis=-1)
            return halves_of(x.reshape(levels * TILE, cols))

        def keep(ref, y, fix):
            for k in range(levels):
                x = [y[k * TILE : (k + 1) * TILE, h * LANES : (h + 1) * LANES] for h in both]
                fix(k, x)
                for h in both:
                    ref[h, k, at, :] = x[h]

        def fix_far(k, x):
            x[0] = x[0] + jnp.where(is_first, to_lane(west, NEAR * levels + k, 0), 0.0)
            x[-1] = x[-1] + jnp.where(lane >= LANES - 2, to_lane(pair, 2 * k, LANES - 2), 0.0)

        def fix_east(slot):
            def fix(k, x):
                x[-1] = jnp.where(is_last, to_lane(east, slot * levels + k, LANES - 1), x[-1])
            return fix

        def fix_west(slot):
            def fix(k, x):
                x[0] = jnp.where(is_first, to_lane(west, slot * levels + k, 0), x[0])
            return fix

        keep(far_s, moved(of(t_s), 2), fix_far)
        parts = of(u_s)
        keep(ue_s, moved(parts, 0), fix_east(ZONAL))
        keep(uw_s, moved(parts, 1), fix_west(ZONAL))
        parts = of(v_s)
        keep(ve_s, moved(parts, 0), fix_east(MERID))
        keep(vw_s, moved(parts, 1), fix_west(MERID))

    sub16 = lax.broadcasted_iota(jnp.int32, (levels, LANES), 0)
    lane16 = lax.broadcasted_iota(jnp.int32, (levels, LANES), 1)

    def corner(line, slot):
        wide = jnp.broadcast_to(line, (levels, LANES))
        return jnp.sum(jnp.where(lane16 == sub16 + slot * levels, wide, 0.0), axis=1, keepdims=True)

    edge = moved(halves_of(north[ZONAL * levels : (ZONAL + 1) * levels, :]), 1)
    first_lanes = jnp.where(lane16 == 0, corner(from_west[rows : rows + 1, :], ZONAL), edge[:, :LANES])
    for k in range(levels):
        uw_s[0, k, high : high + 1, :] = first_lanes[k : k + 1]
        for h in range(1, halves):
            uw_s[h, k, high : high + 1, :] = edge[k : k + 1, h * LANES : (h + 1) * LANES]
    edge = moved(halves_of(south[3 * levels : 4 * levels, :]), 0)
    last_lanes = jnp.where(lane16 == LANES - 1, corner(from_east[TILE - 1 : TILE, :], MERID), edge[:, -LANES:])
    for k in range(levels):
        ve_s[halves - 1, k, low : low + 1, :] = last_lanes[k : k + 1]
        for h in range(halves - 1):
            ve_s[h, k, low : low + 1, :] = edge[k : k + 1, h * LANES : (h + 1) * LANES]

    make_density(0)
    mix(0)
    flat[0].wait()
    flat[1].wait()

    def tile_step(r, carry):
        for c in range(1, len(chunks)):
            @pl.when(r + 1 == starts[c])
            def _():
                for field in range(4):
                    for h in both:
                        load(c, field, h).wait()

        ahead = jnp.minimum(r + 1, tiles - 1)
        make_density(ahead)
        mix(ahead)

        row = pl.multiple_of(r * TILE, TILE)
        flat_at = pl.ds(row, TILE)

        def rows_of(ref, k, shift):
            return [ref[h, k, pl.ds(row + TILE + shift, TILE), :] for h in both]

        east = from_east[pl.ds(row + 8, TILE), :]
        west = from_west[flat_at, :]
        own = own_west[pl.ds(row + 8, TILE), :]

        def span_of(x):
            up = jnp.where(lane < levels - 1, pltpu.roll(x, LANES - 1, 1), x)
            down = jnp.where(lane > 0, pltpu.roll(x, 1, 1), x)
            return up - down

        t_sum = west + own
        d_near, d_own = to_lane(west, DENS * levels, 0), to_lane(own, DENS * levels, 0)
        t_far = to_lane(west, FAR * levels, 0) + to_lane(own, FAR * levels, 0)
        e1 = jnp.broadcast_to(west[:, E1U_LANE : E1U_LANE + 1], (TILE, LANES))
        e2 = jnp.broadcast_to(west[:, E2U_LANE : E2U_LANE + 1], (TILE, LANES))
        wet_w = jnp.broadcast_to(jnp.minimum(west, own)[:, WET_LANE : WET_LANE + 1], (TILE, LANES))
        d_span = span_of(d_near + d_own)
        tilt = (d_own - d_near) * d_span * span_of(t_sum) * inverse_of(d_span * d_span + 16.0)
        flux_w = diffusivity * e2 / e1 * (own - west - tilt) - e2 / 12.0 * to_lane(west, ZONAL * levels, 0) * (7.0 * t_sum - t_far)
        flux_w = jnp.where(lane.astype(jnp.float32) < wet_w, flux_w, 0.0)

        def flat_of(ref, i):
            return [ref[i, flat_at, h * LANES : (h + 1) * LANES] for h in both]

        e1t, e2t, e1u, e2u, e1v, e2v = (flat_of(e_s, i) for i in range(6))
        fu, fv = flat_of(f_s, 0), flat_of(f_s, 1)
        wet = [nf_s[h, flat_at, :] for h in both]
        wet_n = [nf_s[h, pl.ds(row + 1, TILE), :] for h in both]
        wet_e = east_of(wet, east, WET_LANE)
        u_wet = [jnp.minimum(wet[h], wet_e[h]) for h in both]
        v_wet = [jnp.minimum(wet[h], wet_n[h]) for h in both]
        area = [step_duration / (e1t[h] * e2t[h]) for h in both]
        dt = step_duration

        def speeds(along, across, spin, first_inv, second_inv):
            a, b = first_inv, second_inv
            return (
                0.25 * dt * spin,
                0.125 * dt * across,
                0.5 * dt * along,
                dt * viscosity * a * a,
                dt * viscosity * b * b,
                2.0 * dt * viscosity * (a * a + b * b),
            )

        iu1, iu2 = [1.0 / x for x in e1u], [1.0 / x for x in e2u]
        iv1, iv2 = [1.0 / x for x in e1v], [1.0 / x for x in e2v]
        iso_e = [diffusivity * e2u[h] * iu1[h] for h in both]
        adv_e = [e2u[h] * (1.0 / 12.0) for h in both]
        iso_n = [diffusivity * e1v[h] * iv2[h] for h in both]
        adv_n = [e1v[h] * (1.0 / 12.0) for h in both]
        cu = [speeds(iu1[h], iu2[h], fu[h], iu1[h], iu2[h]) for h in both]
        cv = [speeds(iv2[h], iv1[h], -fv[h], iv1[h], iv2[h]) for h in both]
        pu = [0.5 * gravity * dt * iu1[h] for h in both]
        pv = [0.5 * gravity * dt * iv2[h] for h in both]

        run_e = [jnp.zeros((TILE, LANES), jnp.float32) for _ in both]
        run_n = [jnp.zeros((TILE, LANES), jnp.float32) for _ in both]
        store_at = lambda h: (flat_at, pl.ds(h * LANES, LANES))

        def level_parts(k):
            t, tn, ts, tnn = (rows_of(t_s, k, i) for i in (0, 1, -1, 2))
            d, dn = rows_of(d_s, k, 0), rows_of(d_s, k, 1)
            u, un, us = (rows_of(u_s, k, i) for i in (0, 1, -1))
            v, vn, vs = (rows_of(v_s, k, i) for i in (0, 1, -1))
            te = east_of(t, east, NEAR * levels + k)
            far = rows_of(far_s, k, 0)
            de = east_of(d, east, DENS * levels + k)
            ue, uw, uwn = rows_of(ue_s, k, 0), rows_of(uw_s, k, 0), rows_of(uw_s, k, 1)
            ve, vw, ves = rows_of(ve_s, k, 0), rows_of(vw_s, k, 0), rows_of(ve_s, k, -1)
            out = []
            for h in both:
                se, sn = t[h] + te[h], t[h] + tn[h]
                dde, ddn = de[h] - d[h], dn[h] - d[h]
                he = iso_e[h] * (te[h] - t[h]) - adv_e[h] * u[h] * (7.0 * se - far[h])
                hn = iso_n[h] * (tn[h] - t[h]) - adv_n[h] * v[h] * (7.0 * sn - (ts[h] + tnn[h]))
                out.append((se, d[h] + de[h], he, iso_e[h] * dde, sn, d[h] + dn[h], hn, iso_n[h] * ddn))

                pe, pn = run_e[h] + dde, run_n[h] + ddn
                run_e[h], run_n[h] = pe + dde, pn + ddn
                c1, c2, c3, c4, c5, c6 = cu[h]
                vbar = (v[h] + vs[h]) + (ve[h] + ves[h])
                du = (
                    vbar * (c1 - c2 * (un[h] - us[h]))
                    - u[h] * (c3 * (ue[h] - uw[h]) + c6)
                    + c4 * (ue[h] + uw[h])
                    + c5 * (un[h] + us[h])
                    - pu[h] * pe
                )
                uo_s[(k,) + store_at(h)] = u[h] + jnp.where(u_wet[h] > k, du, 0.0)
                c1, c2, c3, c4, c5, c6 = cv[h]
                ubar = (u[h] + un[h]) + (uw[h] + uwn[h])
                dv = (
                    ubar * (c1 - c2 * (ve[h] - vw[h]))
                    - v[h] * (c3 * (vn[h] - vs[h]) + c6)
                    + c4 * (ve[h] + vw[h])
                    + c5 * (vn[h] + vs[h])
                    - pv[h] * pn
                )
                vo_s[(k,) + store_at(h)] = v[h] + jnp.where(v_wet[h] > k, dv, 0.0)
            return out

        def finish(k, below, here, above):
            fe, fn = [], []
            for h in both:
                t_span, d_span = above[h][0] - below[h][0], above[h][1] - below[h][1]
                flux = here[h][2] - here[h][3] * d_span * t_span * inverse_of(d_span * d_span + 16.0)
                fe.append(jnp.where(u_wet[h] > k, flux, 0.0))
                t_span, d_span = above[h][4] - below[h][4], above[h][5] - below[h][5]
                flux = here[h][6] - here[h][7] * d_span * t_span * inverse_of(d_span * d_span + 16.0)
                fn.append(jnp.where(v_wet[h] > k, flux, 0.0))
            for h in both:
                g_s[h, k, pl.ds(row + TILE, TILE), :] = fn[h]
            fw = west_of(fe, flux_w, k)
            fs = rows_of(g_s, k, -1)
            t = rows_of(t_s, k, 0)
            for h in both:
                change = area[h] * ((fe[h] - fw[h]) + (fn[h] - fs[h]))
                to_s[(k,) + store_at(h)] = t[h] + jnp.where(wet[h] > k, change, 0.0)

        below = here = level_parts(0)
        for k in range(1, levels):
            above = level_parts(k)
            finish(k - 1, below, here, above)
            below, here = here, above
        finish(levels - 1, below, here, here)

        for c in range(len(chunks)):
            @pl.when(r + 1 == starts[c] + chunks[c])
            def _():
                for field in range(3):
                    store(c, field).start()

        return carry

    lax.fori_loop(0, tiles, tile_step, 0)
    for c in range(len(chunks)):
        for field in range(3):
            store(c, field).wait()


def chunk_sizes(tiles):
    sizes = []
    size = 2
    while tiles > 0:
        take = min(size, tiles)
        sizes.append(take)
        tiles -= take
        size += 1
    return tuple(sizes)


def body(
    east_velocity,
    north_velocity,
    heat_anomaly,
    haline_anomaly,
    spacing_lengths,
    planetary_spin,
    ocean_layer_number,
    seam_partner_index,
):
    t, s, u, v = heat_anomaly, haline_anomaly, east_velocity, north_velocity
    levels, rows, cols = t.shape
    lats, lons = lax.axis_size("lat"), lax.axis_size("lon")
    f32 = jnp.float32
    top = rows // TILE - 1
    message = 5 * levels + 8

    low3 = pl.BlockSpec((levels, TILE, cols), lambda i: (0, 0, 0))
    high3 = pl.BlockSpec((levels, TILE, cols), lambda i: (0, top, 0))
    whole = pl.BlockSpec((message, cols), lambda i: (0, 0))
    count = spacing_lengths.shape[0]
    first, second = pl.pallas_call(
        row_pack,
        grid=(1,),
        in_specs=[low3, high3] * 4
        + [
            pl.BlockSpec((count, TILE, cols), lambda i: (0, 0, 0)),
            pl.BlockSpec((count, TILE, cols), lambda i: (0, top, 0)),
            pl.BlockSpec((TILE, cols), lambda i: (0, 0)),
            pl.BlockSpec((TILE, cols), lambda i: (top, 0)),
        ],
        out_specs=[whole, whole],
        out_shape=[jax.ShapeDtypeStruct((message, cols), f32)] * 2,
        name="row_pack",
    )(t, t, s, s, u, u, v, v, spacing_lengths, spacing_lengths, ocean_layer_number, ocean_layer_number)

    axes = ("lon", "lat")

    def place(lat, lon):
        return lon * lats + lat

    swap1, swap2 = [], []
    for lon in range(lons):
        for lat in range(0, lats, 2):
            swap1 += [(place(lat, lon), place(lat + 1, lon)), (place(lat + 1, lon), place(lat, lon))]
        for lat in range(1, lats - 1, 2):
            swap2 += [(place(lat, lon), place(lat + 1, lon)), (place(lat + 1, lon), place(lat, lon))]
        swap2.append((place(lats - 1, lon), place(lats - 1, lons - 1 - lon)))
    got1 = lax.ppermute(first, axes, swap1)
    got2 = lax.ppermute(second, axes, swap2)

    group = 4
    seam = seam_partner_index.reshape(-1, LANES)
    slab = pl.BlockSpec((group, rows, cols), lambda i: (i, 0, 0))
    fixed = lambda *shape: pl.BlockSpec(shape, lambda i: (0,) * len(shape))
    to_east, to_west, north, south = pl.pallas_call(
        lambda *refs: column_pack(group, *refs),
        grid=(levels // group,),
        in_specs=[slab] * 4
        + [fixed(count, rows, cols), fixed(rows, cols)]
        + [fixed(message, cols)] * 4
        + [fixed(*seam.shape)],
        out_specs=[fixed(rows + 8, LANES)] * 2 + [fixed(message, cols), fixed(4 * levels, cols)],
        out_shape=[jax.ShapeDtypeStruct((rows + 8, LANES), f32)] * 2
        + [jax.ShapeDtypeStruct((message, cols), f32), jax.ShapeDtypeStruct((4 * levels, cols), f32)],
        compiler_params=pltpu.CompilerParams(vmem_limit_bytes=60 * 2**20),
        name="column_pack",
    )(t, s, u, v, spacing_lengths, ocean_layer_number, first, second, got1, got2, seam)

    from_west = lax.ppermute(to_east, "lon", [(i, (i + 1) % lons) for i in range(lons)])
    from_east = lax.ppermute(to_west, "lon", [((i + 1) % lons, i) for i in range(lons)])

    chunks = chunk_sizes(rows // TILE)
    halves = cols // LANES
    held = (halves, levels, rows + 2 * TILE, LANES)
    anywhere = pl.BlockSpec(memory_space=pl.ANY)
    near = pl.BlockSpec(memory_space=pltpu.VMEM)
    out = jax.ShapeDtypeStruct((levels, rows, cols), f32)
    return pl.pallas_call(
        lambda *refs: step_kernel(chunks, *refs),
        in_specs=[anywhere] * 7 + [near] * 5,
        out_specs=[anywhere] * 3,
        out_shape=[out] * 3,
        scratch_shapes=[pltpu.VMEM(held, f32)] * 11
        + [
            pltpu.VMEM(spacing_lengths.shape, f32),
            pltpu.VMEM(planetary_spin.shape, f32),
            pltpu.VMEM((rows, cols), jnp.int32),
            pltpu.VMEM((halves, rows + TILE, LANES), f32),
        ]
        + [pltpu.VMEM((levels, rows, cols), f32)] * 3
        + [
            pltpu.VMEM((3, cols, cols), jnp.bfloat16),
            pltpu.SemaphoreType.DMA((len(chunks), 4, halves)),
            pltpu.SemaphoreType.DMA((3,)),
            pltpu.SemaphoreType.DMA((len(chunks), 3)),
        ],
        compiler_params=pltpu.CompilerParams(vmem_limit_bytes=60 * 2**20),
        name="ocean_step",
    )(t, s, u, v, spacing_lengths, planetary_spin, ocean_layer_number, north, south, to_west, from_east, from_west)


def solution(mesh):
    in_specs = (
        P(None, "lat", "lon"),
        P(None, "lat", "lon"),
        P(None, "lat", "lon"),
        P(None, "lat", "lon"),
        P(None, "lat", "lon"),
        P(None, "lat", "lon"),
        P("lat", "lon"),
        P(),
    )
    out_specs = (P(None, "lat", "lon"), P(None, "lat", "lon"), P(None, "lat", "lon"))
    return jax.shard_map(body, mesh=mesh, in_specs=in_specs, out_specs=out_specs, check_vma=False)
```

```python
import jax
import jax.numpy as jnp
from jax import lax
from jax.experimental import pallas as pl
from jax.experimental.pallas import tpu as pltpu
from jax.sharding import PartitionSpec as P

LANES = 128
TILE = 8

step_duration = 0.25
viscosity = 0.05
diffusivity = 0.3
expansion_coefficient = 0.6
haline_contraction = 0.8
gravity = 0.1

NEAR, FAR, SALT, ZONAL, MERID = 0, 1, 2, 3, 4
E1V_AT, E2V_AT, WET_AT = 0, 1, 2
HEAT_LANE, SALT_LANE, ZONAL_LANE, MERID_LANE = 0, 40, 56, 72
E1U_LANE, E2U_LANE, WET_LANE = 96, 97, 98


def density_of(salinity, heat):
    return haline_contraction * salinity - expansion_coefficient * heat


def inverse_of(x):
    return pltpu.reciprocal(x, approx=True)


def row_pack(t_lo, t_hi, s_lo, s_hi, u_lo, u_hi, v_lo, v_hi, e_lo, e_hi, n_lo, n_hi, first, second):
    levels = t_lo.shape[0]
    even = lax.rem(lax.axis_index("lat"), 2) == 0

    def put(slot, high, low):
        rows = pl.ds(slot * levels, levels)
        first[rows] = jnp.where(even, high, low)
        second[rows] = jnp.where(even, low, high)

    near_hi, near_lo = t_hi[:, 7, :], t_lo[:, 0, :]
    put(NEAR, near_hi, near_lo)
    put(FAR, t_hi[:, 6, :], t_lo[:, 1, :])
    put(SALT, s_hi[:, 7, :], s_lo[:, 0, :])
    put(ZONAL, u_hi[:, 7, :], u_lo[:, 0, :])
    put(MERID, v_hi[:, 7, :], v_lo[:, 0, :])
    base = 5 * levels
    high = jnp.concatenate([e_hi[4, 7:8], e_hi[5, 7:8], n_hi[7:8].astype(jnp.float32), jnp.zeros((5, e_hi.shape[2]), jnp.float32)], axis=0)
    low = jnp.concatenate([e_lo[4, 0:1], e_lo[5, 0:1], n_lo[0:1].astype(jnp.float32), jnp.zeros((5, e_lo.shape[2]), jnp.float32)], axis=0)
    first[base : base + 8] = jnp.where(even, high, low)
    second[base : base + 8] = jnp.where(even, low, high)


def vertical_span(x):
    return jnp.concatenate([x[1:], x[-1:]], axis=0) - jnp.concatenate([x[:1], x[:-1]], axis=0)


def corners(u1, u2, v1, v2, seam, east_in, west_in, east_out, west_out):
    levels, cols = u1.shape
    lat, lon = lax.axis_index("lat"), lax.axis_index("lon")
    lats, lons = lax.axis_size("lat"), lax.axis_size("lon")
    even = lax.rem(lat, 2) == 0
    is_top = lat == lats - 1
    per = cols // LANES
    pick = seam[pl.ds(lon * per + per - 1, 1), LANES - 1 : LANES] - (lons - 1 - lon) * cols
    pick = jnp.where(is_top, pick, cols - 1)
    u = jnp.where(even, u1[...], u2[...])
    u = jnp.where(is_top, -u, u)
    here = lax.broadcasted_iota(jnp.int32, (levels, cols), 1) == pick
    u = jnp.sum(jnp.where(here, u, 0.0), axis=1, keepdims=True)
    v = jnp.where(lat == 0, 0.0, jnp.where(even, v2[:, 0:1], v1[:, 0:1]))
    sub16 = lax.broadcasted_iota(jnp.int32, (levels, LANES), 0)
    lane16 = lax.broadcasted_iota(jnp.int32, (levels, LANES), 1)

    def line(x, base):
        return jnp.sum(jnp.where(lane16 == sub16 + base, x, 0.0), axis=0, keepdims=True)

    east_out[...] = jnp.broadcast_to(line(u, ZONAL_LANE), (8, LANES))
    west_out[...] = jnp.broadcast_to(line(v, MERID_LANE + 1), (8, LANES))


def halo_rows(mine1, mine2, got1, got2, seam, north_out, south_out):
    levels = (mine1.shape[0] - 8) // 5
    cols = mine1.shape[1]
    lat, lon = lax.axis_index("lat"), lax.axis_index("lon")
    lats, lons = lax.axis_size("lat"), lax.axis_size("lon")
    even = lax.rem(lat, 2) == 0
    is_top = lat == lats - 1
    is_bottom = lat == 0
    north_rows = got1.shape[0]
    for h in range(cols // LANES):
        span = slice(h * LANES, (h + 1) * LANES)
        pick = seam[pl.ds(lon * (cols // LANES) + h, 1), :] - (lons - 1 - lon) * cols
        pick = jnp.where(is_top, pick, lax.broadcasted_iota(jnp.int32, (1, LANES), 1) + h * LANES)
        pick = jnp.broadcast_to(pick, (TILE, LANES))
        inner = jnp.bitwise_and(pick, LANES - 1)
        for row in range(0, north_rows, TILE):
            total = None
            for g in range(cols // LANES):
                piece = slice(g * LANES, (g + 1) * LANES)
                source = jnp.where(even, got1[row : row + TILE, piece], got2[row : row + TILE, piece])
                taken = jnp.take_along_axis(source, inner, axis=1, mode="promise_in_bounds")
                taken = jnp.where(pick >= g * LANES, taken, 0.0) if g == 0 else taken
                total = taken if total is None else jnp.where(pick >= g * LANES, taken, total)
            if ZONAL * levels <= row < (MERID + 1) * levels:
                total = jnp.where(is_top, -total, total)
            north_out[row : row + TILE, span] = total
    def south(slot):
        part = slice(slot * levels, (slot + 1) * levels)
        return jnp.where(is_bottom, 0.0, jnp.where(even, got2[part], got1[part]))

    def own(slot):
        part = slice(slot * levels, (slot + 1) * levels)
        return jnp.where(even, mine2[part], mine1[part])

    tail = slice(5 * levels, 5 * levels + 8)
    coef = jnp.where(even, got2[tail], got1[tail])
    own_wet = jnp.where(even, mine2[tail], mine1[tail])[WET_AT : WET_AT + 1]
    e1v = jnp.where(is_bottom, 1.0, coef[E1V_AT : E1V_AT + 1])
    e2v = jnp.where(is_bottom, 1.0, coef[E2V_AT : E2V_AT + 1])
    wet = jnp.where(is_bottom, 0.0, coef[WET_AT : WET_AT + 1])
    t_near, t_far, v_near = south(NEAR), south(FAR), south(MERID)
    t_own, t_next = own(NEAR), own(FAR)
    d_near, d_own = density_of(south(SALT), t_near), density_of(own(SALT), t_own)
    t_sum = t_near + t_own
    adv = (e1v / 12.0) * v_near * (7.0 * t_sum - (t_far + t_next))
    d_span = vertical_span(d_near + d_own)
    tilt = (d_own - d_near) * d_span * vertical_span(t_sum) / (d_span * d_span + 16.0)
    iso = (diffusivity * e1v / e2v) * (t_own - t_near - tilt)
    level = lax.broadcasted_iota(jnp.int32, (levels, cols), 0).astype(jnp.float32)
    flux = jnp.where(level < jnp.minimum(wet, own_wet), iso - adv, 0.0)
    south_out[0:levels] = t_near
    south_out[levels : 2 * levels] = flux
    south_out[2 * levels : 3 * levels] = south(ZONAL)
    south_out[3 * levels : 4 * levels] = v_near


def column_pack(group, t, s, u, v, e, n, east_out, west_out):
    rows, cols = t.shape[1:]
    step = pl.program_id(0)
    lane = lax.broadcasted_iota(jnp.int32, (rows, LANES), 1)
    pair = lax.shift_right_logical(lane, 1)
    first = slice(0, LANES)
    last = slice(cols - LANES, cols)

    @pl.when(step == 0)
    def _():
        n_f = n[...].astype(jnp.float32)
        hi = jnp.where(lane == E1U_LANE, pltpu.roll(e[0, :, last], (E1U_LANE + 1) % LANES, 1), 0.0)
        hi = jnp.where(lane == E2U_LANE, pltpu.roll(e[1, :, last], (E2U_LANE + 1) % LANES, 1), hi)
        east_out[0:rows] = jnp.where(lane == WET_LANE, pltpu.roll(n_f[:, last], (WET_LANE + 1) % LANES, 1), hi)
        west_out[8 : rows + 8] = jnp.where(lane == WET_LANE, pltpu.roll(n_f[:, first], WET_LANE, 1), 0.0)
        east_out[rows : rows + 8] = jnp.zeros((8, LANES), jnp.float32)
        west_out[0:8] = jnp.zeros((8, LANES), jnp.float32)

    hi = east_out[0:rows]
    lo = west_out[8 : rows + 8]
    for kk in range(group):
        k = step * group + kk
        for field, base in ((t, HEAT_LANE), (s, SALT_LANE), (u, ZONAL_LANE), (v, MERID_LANE)):
            ends = jnp.where(lane < LANES // 2, field[kk, :, first], field[kk, :, last])
            if field is t:
                ends = pltpu.roll(ends, 2 * k + 2, 1)
                hi = jnp.where(pair == k, ends, hi)
                lo = jnp.where(pair == k + 1, ends, lo)
            else:
                ends = pltpu.roll(ends, base + 1 + k, 1)
                hi = jnp.where(lane == base + k, ends, hi)
                lo = jnp.where(lane == base + 1 + k, ends, lo)
    east_out[0:rows] = hi
    west_out[8 : rows + 8] = lo


def step_kernel(
    t_hbm, s_hbm, u_hbm, v_hbm, e_hbm, f_hbm, n_hbm, north_hbm, south_hbm, own_hbm, from_east_hbm, from_west_hbm,
    u_out, v_out, t_out,
    north, south, own_west, from_east, from_west, t_s, s_s, u_s, v_s, d_s, g_s, mixed_a, uw_a, ve_a, mixed_b, uw_b, ve_b, e_s, f_s, n_s, nf_s, uo_s, vo_s, to_s, move_s, rim_s, mask_s,
    in_sem, flat_sem, out_sem,
):
    levels, rows, cols = t_hbm.shape
    tiles = rows // TILE
    halves = cols // LANES
    both = range(halves)
    pairs = (tiles - 1) // 2
    assert tiles == 2 * pairs + 1

    fields = ((t_hbm, t_s), (s_hbm, s_s), (u_hbm, u_s), (v_hbm, v_s))

    def load(first, count, unit):
        span = pl.ds(first * TILE, count * TILE)
        held = pl.ds(first * TILE + TILE, count * TILE)
        for hbm, vmem in fields:
            for h in both:
                pltpu.make_async_copy(
                    hbm.at[:, span, pl.ds(h * LANES, LANES)], vmem.at[h, :, held, :], in_sem.at[unit]
                ).start()

    def loaded(count, unit):
        span = pl.ds(0, len(fields) * halves * count * TILE)
        pltpu.make_async_copy(t_hbm.at[:, span, pl.ds(0, LANES)], t_s.at[0, :, span, :], in_sem.at[unit]).wait()

    outs = ((uo_s, u_out), (vo_s, v_out), (to_s, t_out))

    def store(row, count):
        span = pl.ds(row, count * TILE)
        for i, (vmem, hbm) in enumerate(outs):
            pltpu.make_async_copy(vmem.at[:, span, :], hbm.at[:, span, :], out_sem.at[i]).start()

    flat = [
        pltpu.make_async_copy(hbm, vmem, flat_sem.at[i])
        for i, (hbm, vmem) in enumerate(
            (
                (e_hbm, e_s),
                (f_hbm, f_s),
                (n_hbm, n_s),
                (north_hbm, north),
                (south_hbm, south),
                (own_hbm, own_west),
                (from_east_hbm, from_east),
                (from_west_hbm, from_west),
            )
        )
    ]
    for copy in flat[2:]:
        copy.start()
    load(0, 1, 0)
    load(1, 2, 1)
    flat[0].start()
    flat[1].start()
    for unit in range(2, pairs + 1):
        load(2 * unit - 1, 2, unit)

    source = lax.broadcasted_iota(jnp.int32, (cols, cols), 0)
    target = lax.broadcasted_iota(jnp.int32, (cols, cols), 1)
    apart = source - target

    def matrix(*terms):
        total = jnp.zeros((cols, cols), jnp.float32)
        for where, value in terms:
            total = jnp.where(where, value, total)
        return total.astype(jnp.bfloat16)

    at = [apart == i for i in range(-1, 3)]
    move_s[0] = matrix((at[0], -1.0), (at[1], 7.0), (at[2], 7.0), (at[3], -1.0))
    move_s[1] = matrix((at[0], 1.0))
    move_s[2] = matrix((at[2], 1.0))
    origin = jnp.bitwise_and(source, LANES - 1)
    odd = jnp.bitwise_and(origin, 1) == 1
    west_end, east_end = target == 0, target == cols - 1
    heat_east, heat_west = origin < 32, (origin >= 32) & (origin < 64) & odd
    rim_s[0] = matrix(
        (heat_east & ~odd & (target == cols - 2), -1.0),
        (heat_east & ~odd & east_end, 7.0),
        (heat_east & odd & east_end, -1.0),
        (heat_west & west_end, -1.0),
    )
    western = jnp.bitwise_and(origin, 16) == 16
    rim_s[1] = matrix(((origin >= 64) & western & west_end, 1.0))
    rim_s[2] = matrix(
        ((origin >= 64) & ~western & east_end, 1.0),
        (heat_east & ~odd & east_end, 1.0),
        ((origin >= 32) & (origin < 64) & ~odd & east_end, 1.0),
    )

    for copy in flat[2:]:
        copy.wait()
    low, high = TILE - 1, TILE + rows
    north_density = density_of(
        north[SALT * levels : (SALT + 1) * levels, :], north[NEAR * levels : (NEAR + 1) * levels, :]
    )
    for h in both:
        span = slice(h * LANES, (h + 1) * LANES)
        for k in range(levels):
            t_s[h, k, low : low + 1, :] = south[k : k + 1, span]
            g_s[h, k, low : low + 1, :] = south[levels + k : levels + k + 1, span]
            u_s[h, k, low : low + 1, :] = south[2 * levels + k : 2 * levels + k + 1, span]
            v_s[h, k, low : low + 1, :] = south[3 * levels + k : 3 * levels + k + 1, span]
            t_s[h, k, high : high + 1, :] = north[NEAR * levels + k : NEAR * levels + k + 1, span]
            t_s[h, k, high + 1 : high + 2, :] = north[FAR * levels + k : FAR * levels + k + 1, span]
            d_s[h, k, high : high + 1, :] = north_density[k : k + 1, span]
            u_s[h, k, high : high + 1, :] = north[ZONAL * levels + k : ZONAL * levels + k + 1, span]
            v_s[h, k, high : high + 1, :] = north[MERID * levels + k : MERID * levels + k + 1, span]
        nf_s[h, rows : rows + 1, :] = north[5 * levels + WET_AT : 5 * levels + WET_AT + 1, span]
    for h in both:
        nf_s[h, 0:rows, :] = n_s[:, h * LANES : (h + 1) * LANES].astype(jnp.float32)
    loaded(1, 0)
    loaded(2, 1)

    lane = lax.broadcasted_iota(jnp.int32, (TILE, LANES), 1)
    is_last = lane == LANES - 1
    is_first = lane == 0
    from_rim_west = ((lane >= 32) & (lane < 64)) | ((lane >= 80) & (lane < 96)) | (lane >= 112)
    rim_source = jnp.where(
        lane < 32,
        lane + 2,
        jnp.where(
            lane < 64,
            lane - 32,
            jnp.where(
                lane < 80,
                lane - 64 + ZONAL_LANE + 1,
                jnp.where(
                    lane < 96,
                    lane - 80 + ZONAL_LANE,
                    jnp.where(lane < 112, lane - 96 + MERID_LANE + 1, lane - 112 + MERID_LANE),
                ),
            ),
        ),
    )
    lane2 = lax.broadcasted_iota(jnp.int32, (2 * TILE, LANES), 1)
    second = lax.broadcasted_iota(jnp.int32, (2 * TILE, LANES), 0) >= TILE
    level2 = jnp.where(lane2 < 64, lax.shift_right_logical(jnp.bitwise_and(lane2, 31), 1), jnp.bitwise_and(lane2, 15))
    level2 = level2 - jnp.where(second, 1, 0)
    for_density = (lane2 >= 32) & (lane2 < 64) & (jnp.bitwise_and(lane2, 1) == 0)
    kinds = ((lane2 < 64) & ~for_density, (lane2 >= 64) & (lane2 < 96), lane2 >= 96, for_density)
    for i, kind in enumerate(kinds):
        for p in range(levels // 2):
            mask_s[i, p] = jnp.where(kind & (level2 == 2 * p), 1.0, 0.0).astype(jnp.bfloat16)
    density_lane = (lane >= 32) & (lane < 64) & (jnp.bitwise_and(lane, 1) == 0)
    salt_source = jnp.bitwise_and(SALT_LANE + 1 + lax.shift_right_logical(lane - 32, 1), LANES - 1)
    heat_source = jnp.bitwise_and(lane - 30, LANES - 1)

    def to_lane(x, source, target):
        return pltpu.roll(x, (target - source) % LANES, 1)

    def east_of(x, halo, source):
        turned = [pltpu.roll(p, LANES - 1, 1) for p in x] + [to_lane(halo, source, LANES - 1)]
        return [jnp.where(is_last, turned[h + 1], turned[h]) for h in both]

    def west_of(x, halo, source):
        turned = [to_lane(halo, source, 0)] + [pltpu.roll(p, 1, 1) for p in x]
        return [jnp.where(is_first, turned[h], turned[h + 1]) for h in both]

    def two_parts(x):
        high_part = x.astype(jnp.bfloat16)
        return [high_part, (x - high_part.astype(jnp.float32)).astype(jnp.bfloat16)]

    def moved(parts, edges, i):
        y = jnp.dot(edges, rim_s[i], preferred_element_type=jnp.float32) if edges is not None else 0.0
        for p in parts:
            y = y + jnp.dot(p, move_s[i], preferred_element_type=jnp.float32)
        return y

    def mix(r, kept, previous):
        mixed, uw_s, ve_s = kept
        row = pl.multiple_of(r * TILE, TILE)

        def turned(x, order):
            return jnp.take_along_axis(x, order, axis=1, mode="promise_in_bounds")

        east = from_east[pl.ds(row + TILE, TILE), :]
        x = jnp.where(from_rim_west, turned(from_west[pl.ds(row, TILE), :], rim_source), turned(east, rim_source))
        x = jnp.where(density_lane, density_of(turned(east, salt_source), turned(east, heat_source)), x)
        twice = [jnp.concatenate([p, p], axis=0) for p in two_parts(x)]

        def spread(kind):
            split = [[p * mask_s[kind, i] for i in range(levels // 2)] for p in twice]
            return jnp.concatenate([jnp.concatenate(q, axis=0) for q in split], axis=1)

        rim_t, rim_u, rim_v, rim_d = (spread(kind) for kind in range(4))

        def of(values):
            return two_parts(jnp.concatenate(values, axis=-1).reshape(levels * TILE, cols))

        def held_in(ref):
            return [ref[h, :, pl.ds(row + TILE, TILE), :] for h in both]

        def piece(y, i, h):
            count = levels * TILE
            return y[i * count : (i + 1) * count, h * LANES : (h + 1) * LANES].reshape(levels, TILE, LANES)

        d = [density_of(salt, heat) for salt, heat in zip(held_in(s_s), held_in(t_s))]
        for h in both:
            d_s[h, :, pl.ds(row + TILE, TILE), :] = d[h]
        parts = [of(held_in(u_s)), of(held_in(v_s)), of(held_in(t_s)), of(d)]
        y = moved([jnp.concatenate(p, axis=0) for p in zip(*parts)], jnp.concatenate([rim_u, rim_v, rim_t, rim_d], axis=0), 2)
        for h in both:
            mixed[0, h] = piece(y, 0, h)
            ve_s[h, :, TILE : 2 * TILE, :] = piece(y, 1, h)
            mixed[3, h] = piece(y, 2, h)
            mixed[4, h] = piece(y, 3, h)
        y = moved(parts[2], rim_t, 0)
        for h in both:
            mixed[2, h] = piece(y, 0, h)
        y = moved([jnp.concatenate(p, axis=0) for p in zip(*parts[:2])], jnp.concatenate([rim_u, rim_v], axis=0), 1)
        for h in both:
            uw = piece(y, 0, h)
            uw_s[h, :, 0:TILE, :] = uw
            previous[1][h, :, TILE : TILE + 1, :] = uw[:, 0:1, :]
            mixed[1, h] = piece(y, 1, h)

    sub16 = lax.broadcasted_iota(jnp.int32, (levels, LANES), 0)
    lane16 = lax.broadcasted_iota(jnp.int32, (levels, LANES), 1)

    def corner(line, base):
        wide = jnp.broadcast_to(line, (levels, LANES))
        return jnp.sum(jnp.where(lane16 == sub16 + base, wide, 0.0), axis=1, keepdims=True)

    edge = moved(two_parts(south[3 * levels : 4 * levels, :]), None, 2)
    edge = [edge[:, h * LANES : (h + 1) * LANES] for h in both]
    edge[-1] = jnp.where(lane16 == LANES - 1, corner(from_east[TILE - 1 : TILE, :], MERID_LANE + 1), edge[-1])
    for h in both:
        for k in range(levels):
            ve_a[h, k, TILE - 1 : TILE, :] = edge[h][k : k + 1]

    def advance(r, kept, following):
        mixed, uw_s, ve_s = kept
        for h in both:
            following[2][h, :, TILE - 1 : TILE, :] = ve_s[h, :, 2 * TILE - 1 : 2 * TILE, :]
        row = pl.multiple_of(r * TILE, TILE)
        flat_at = pl.ds(row, TILE)

        def rows_of(ref, k, shift):
            return [ref[h, k, pl.ds(row + TILE + shift, TILE), :] for h in both]

        east = from_east[pl.ds(row + TILE, TILE), :]
        west = from_west[flat_at, :]
        own = own_west[pl.ds(row + TILE, TILE), :]

        def span_of(x):
            up = jnp.where(lane < levels - 1, pltpu.roll(x, LANES - 1, 1), x)
            down = jnp.where(lane > 0, pltpu.roll(x, 1, 1), x)
            return up - down

        def heat_lane(x, offset):
            order = jnp.bitwise_and(2 * lane + offset, LANES - 1)
            return jnp.take_along_axis(x, order, axis=1, mode="promise_in_bounds")

        t_near, t_own = heat_lane(west, 1), heat_lane(own, 2)
        t_sum, t_far = t_near + t_own, heat_lane(west, 0) + heat_lane(own, 3)
        d_near = density_of(to_lane(west, SALT_LANE, 0), t_near)
        d_own = density_of(to_lane(own, SALT_LANE + 1, 0), t_own)
        e1 = jnp.broadcast_to(west[:, E1U_LANE : E1U_LANE + 1], (TILE, LANES))
        e2 = jnp.broadcast_to(west[:, E2U_LANE : E2U_LANE + 1], (TILE, LANES))
        wet_w = jnp.broadcast_to(jnp.minimum(west, own)[:, WET_LANE : WET_LANE + 1], (TILE, LANES))
        d_span = span_of(d_near + d_own)
        tilt = (d_own - d_near) * d_span * span_of(t_sum) * inverse_of(d_span * d_span + 16.0)
        flux_w = diffusivity * e2 * inverse_of(e1) * (t_own - t_near - tilt)
        flux_w = flux_w - e2 * (1.0 / 12.0) * to_lane(west, ZONAL_LANE, 0) * (7.0 * t_sum - t_far)
        flux_w = jnp.where(lane.astype(jnp.float32) < wet_w, flux_w, 0.0)

        def flat_of(ref, i):
            return [ref[i, flat_at, h * LANES : (h + 1) * LANES] for h in both]

        e1t, e2t, e1u, e2u, e1v, e2v = (flat_of(e_s, i) for i in range(6))
        fu, fv = flat_of(f_s, 0), flat_of(f_s, 1)
        wet = [nf_s[h, flat_at, :] for h in both]
        wet_n = [nf_s[h, pl.ds(row + 1, TILE), :] for h in both]
        wet_e = east_of(wet, east, WET_LANE)
        u_wet = [jnp.minimum(wet[h], wet_e[h]) for h in both]
        v_wet = [jnp.minimum(wet[h], wet_n[h]) for h in both]
        dt = step_duration
        area = [dt * inverse_of(e1t[h] * e2t[h]) for h in both]

        def speeds(spin, along, across, a, b):
            c4, c5 = dt * viscosity * a * a, dt * viscosity * b * b
            return 0.25 * dt * spin, 0.125 * dt * across, 0.5 * dt * along, c4, c5, 2.0 * (c4 + c5)

        iu1, iu2 = [inverse_of(x) for x in e1u], [inverse_of(x) for x in e2u]
        iv1, iv2 = [inverse_of(x) for x in e1v], [inverse_of(x) for x in e2v]
        iso_e = [diffusivity * e2u[h] * iu1[h] for h in both]
        adv_e = [e2u[h] * (1.0 / 12.0) for h in both]
        iso_n = [diffusivity * e1v[h] * iv2[h] for h in both]
        adv_n = [e1v[h] * (1.0 / 12.0) for h in both]
        cu = [speeds(fu[h], iu1[h], iu2[h], iu1[h], iu2[h]) for h in both]
        cv = [speeds(-fv[h], iv2[h], iv1[h], iv1[h], iv2[h]) for h in both]
        pu = [0.5 * gravity * dt * iu1[h] for h in both]
        pv = [0.5 * gravity * dt * iv2[h] for h in both]

        store_at = lambda h: (flat_at, pl.ds(h * LANES, LANES))
        zero = jnp.zeros((TILE, LANES), jnp.float32)

        run = [zero for _ in both]

        def east_parts(k):
            t, d, u = rows_of(t_s, k, 0), rows_of(d_s, k, 0), rows_of(u_s, k, 0)
            un, us = rows_of(u_s, k, 1), rows_of(u_s, k, -1)
            ue, wide, te, de = ([mixed[i, h, k] for h in both] for i in (0, 2, 3, 4))
            uw = [uw_s[h, k, 0:TILE, :] for h in both]
            v, vs = rows_of(v_s, k, 0), rows_of(v_s, k, -1)
            vbar = [
                (v[h] + vs[h]) + (ve_s[h, k, TILE : 2 * TILE, :] + ve_s[h, k, TILE - 1 : 2 * TILE - 1, :]) for h in both
            ]
            out = []
            for h in both:
                rise = de[h] - d[h]
                direct = iso_e[h] * (te[h] - t[h]) - adv_e[h] * u[h] * wide[h]
                out.append((t[h] + te[h], d[h] + de[h], direct, iso_e[h] * rise))
                press = run[h] + rise
                run[h] = press + rise
                c1, c2, c3, c4, c5, c6 = cu[h]
                du = (
                    vbar[h] * (c1 - c2 * (un[h] - us[h]))
                    - u[h] * (c3 * (ue[h] - uw[h]) + c6)
                    + c4 * (ue[h] + uw[h])
                    + c5 * (un[h] + us[h])
                    - pu[h] * press
                )
                uo_s[(k,) + store_at(h)] = u[h] + jnp.where(u_wet[h] > k, du, 0.0)
            return out

        def flux_of(below, here, above, open_face):
            t_span, d_span = above[0] - below[0], above[1] - below[1]
            flux = here[2] - here[3] * d_span * t_span * inverse_of(d_span * d_span + 16.0)
            return jnp.where(open_face, flux, 0.0)

        def east_finish(k, below, here, above):
            fe = [flux_of(below[h], here[h], above[h], u_wet[h] > k) for h in both]
            fw = west_of(fe, flux_w, k)
            for h in both:
                to_s[(k,) + store_at(h)] = fe[h] - fw[h]

        below = here = east_parts(0)
        for k in range(1, levels):
            above = east_parts(k)
            east_finish(k - 1, below, here, above)
            below, here = here, above
        east_finish(levels - 1, below, here, here)

        run = [zero for _ in both]

        def north_parts(k):
            t, tn, ts, tnn = (rows_of(t_s, k, i) for i in (0, 1, -1, 2))
            d, dn = rows_of(d_s, k, 0), rows_of(d_s, k, 1)
            v, vn, vs = (rows_of(v_s, k, i) for i in (0, 1, -1))
            ve, vw = [ve_s[h, k, TILE : 2 * TILE, :] for h in both], [mixed[1, h, k] for h in both]
            u, un = rows_of(u_s, k, 0), rows_of(u_s, k, 1)
            ubar = [(u[h] + un[h]) + (uw_s[h, k, 0:TILE, :] + uw_s[h, k, 1 : TILE + 1, :]) for h in both]
            out = []
            for h in both:
                rise, pair = dn[h] - d[h], t[h] + tn[h]
                direct = iso_n[h] * (tn[h] - t[h]) - adv_n[h] * v[h] * (7.0 * pair - (ts[h] + tnn[h]))
                out.append((pair, d[h] + dn[h], direct, iso_n[h] * rise))
                press = run[h] + rise
                run[h] = press + rise
                c1, c2, c3, c4, c5, c6 = cv[h]
                dv = (
                    ubar[h] * (c1 - c2 * (ve[h] - vw[h]))
                    - v[h] * (c3 * (vn[h] - vs[h]) + c6)
                    + c4 * (ve[h] + vw[h])
                    + c5 * (vn[h] + vs[h])
                    - pv[h] * press
                )
                vo_s[(k,) + store_at(h)] = v[h] + jnp.where(v_wet[h] > k, dv, 0.0)
            return out

        def north_finish(k, below, here, above):
            for h in both:
                fn = flux_of(below[h], here[h], above[h], v_wet[h] > k)
                g_s[h, k, pl.ds(row + TILE, TILE), :] = fn
                fs = g_s[h, k, pl.ds(row + TILE - 1, TILE), :]
                at_h = (k,) + store_at(h)
                change = area[h] * (to_s[at_h] + (fn - fs))
                to_s[at_h] = t_s[h, k, pl.ds(row + TILE, TILE), :] + jnp.where(wet[h] > k, change, 0.0)

        below = here = north_parts(0)
        for k in range(1, levels):
            above = north_parts(k)
            north_finish(k - 1, below, here, above)
            below, here = here, above
        north_finish(levels - 1, below, here, here)

    set_a, set_b = (mixed_a, uw_a, ve_a), (mixed_b, uw_b, ve_b)
    mix(0, set_a, set_b)
    flat[0].wait()
    flat[1].wait()

    def two_tiles(i, carry):
        @pl.when(i + 2 <= pairs)
        def _():
            loaded(2, i + 2)

        mix(2 * i + 1, set_b, set_a)
        advance(2 * i, set_a, set_b)
        mix(2 * i + 2, set_a, set_b)
        advance(2 * i + 1, set_b, set_a)
        store(pl.multiple_of(i * 2 * TILE, 2 * TILE), 2)
        return carry

    lax.fori_loop(0, pairs, two_tiles, 0)
    edge = moved(two_parts(north[ZONAL * levels : (ZONAL + 1) * levels, :]), None, 1)
    edge = [edge[:, h * LANES : (h + 1) * LANES] for h in both]
    edge[0] = jnp.where(lane16 == 0, corner(from_west[rows : rows + 1, :], ZONAL_LANE), edge[0])
    for h in both:
        for k in range(levels):
            uw_a[h, k, TILE : TILE + 1, :] = edge[h][k : k + 1]
    advance(jnp.int32(2 * pairs), set_a, set_b)
    store(2 * pairs * TILE, 1)
    for i, (vmem, hbm) in enumerate(outs):
        pltpu.make_async_copy(vmem, hbm, out_sem.at[i]).wait()


def body(
    east_velocity,
    north_velocity,
    heat_anomaly,
    haline_anomaly,
    spacing_lengths,
    planetary_spin,
    ocean_layer_number,
    seam_partner_index,
):
    t, s, u, v = heat_anomaly, haline_anomaly, east_velocity, north_velocity
    levels, rows, cols = t.shape
    lats, lons = lax.axis_size("lat"), lax.axis_size("lon")
    f32 = jnp.float32
    top = rows // TILE - 1
    message = 5 * levels + 8

    low3 = pl.BlockSpec((levels, TILE, cols), lambda i: (0, 0, 0))
    high3 = pl.BlockSpec((levels, TILE, cols), lambda i: (0, top, 0))
    whole = pl.BlockSpec((message, cols), lambda i: (0, 0))
    count = spacing_lengths.shape[0]
    first, second = pl.pallas_call(
        row_pack,
        grid=(1,),
        in_specs=[low3, high3] * 4
        + [
            pl.BlockSpec((count, TILE, cols), lambda i: (0, 0, 0)),
            pl.BlockSpec((count, TILE, cols), lambda i: (0, top, 0)),
            pl.BlockSpec((TILE, cols), lambda i: (0, 0)),
            pl.BlockSpec((TILE, cols), lambda i: (top, 0)),
        ],
        out_specs=[whole, whole],
        out_shape=[jax.ShapeDtypeStruct((message, cols), f32)] * 2,
        name="row_pack",
    )(t, t, s, s, u, u, v, v, spacing_lengths, spacing_lengths, ocean_layer_number, ocean_layer_number)

    axes = ("lon", "lat")

    def place(lat, lon):
        return lon * lats + lat

    swap1, swap2 = [], []
    for lon in range(lons):
        for lat in range(0, lats, 2):
            swap1 += [(place(lat, lon), place(lat + 1, lon)), (place(lat + 1, lon), place(lat, lon))]
        for lat in range(1, lats - 1, 2):
            swap2 += [(place(lat, lon), place(lat + 1, lon)), (place(lat + 1, lon), place(lat, lon))]
        swap2.append((place(lats - 1, lon), place(lats - 1, lons - 1 - lon)))
    got1 = lax.ppermute(first, axes, swap1)
    got2 = lax.ppermute(second, axes, swap2)

    group = 8
    slab = pl.BlockSpec((group, rows, cols), lambda i: (i, 0, 0))
    message_out = jax.ShapeDtypeStruct((rows + 8, LANES), f32)
    to_east, to_west = pl.pallas_call(
        lambda *refs: column_pack(group, *refs),
        grid=(levels // group,),
        in_specs=[slab] * 4
        + [pl.BlockSpec((2, rows, cols), lambda i: (1, 0, 0)), pl.BlockSpec((rows, cols), lambda i: (0, 0))],
        out_specs=[pl.BlockSpec((rows + 8, LANES), lambda i: (0, 0))] * 2,
        out_shape=[message_out] * 2,
        compiler_params=pltpu.CompilerParams(vmem_limit_bytes=60 * 2**20),
        cost_estimate=pl.CostEstimate(flops=20 * t.size, bytes_accessed=16 * t.size, transcendentals=0),
        name="column_pack",
    )(t, s, u, v, spacing_lengths, ocean_layer_number)

    seam = seam_partner_index.reshape(-1, LANES)
    fixed = lambda *shape: pl.BlockSpec(shape, lambda i: (0,) * len(shape))
    high_edge = pl.BlockSpec((8, LANES), lambda i: (rows // 8, 0))
    low_edge = pl.BlockSpec((8, LANES), lambda i: (0, 0))
    tight = pltpu.CompilerParams(vmem_limit_bytes=60 * 2**20)
    u_rows = pl.BlockSpec((levels, cols), lambda i: (ZONAL, 0))
    v_rows = pl.BlockSpec((levels, cols), lambda i: (MERID, 0))
    to_east, to_west = pl.pallas_call(
        corners,
        grid=(1,),
        in_specs=[u_rows, u_rows, v_rows, v_rows, fixed(*seam.shape), high_edge, low_edge],
        out_specs=[high_edge, low_edge],
        out_shape=[message_out] * 2,
        input_output_aliases={5: 0, 6: 1},
        compiler_params=tight,
        name="corners",
    )(got1, got2, got1, got2, seam, to_east, to_west)

    from_west = lax.ppermute(to_east, "lon", [(i, (i + 1) % lons) for i in range(lons)])
    from_east = lax.ppermute(to_west, "lon", [((i + 1) % lons, i) for i in range(lons)])

    north, south = pl.pallas_call(
        halo_rows,
        grid=(1,),
        in_specs=[fixed(message, cols)] * 4 + [fixed(*seam.shape)],
        out_specs=[fixed(message, cols), fixed(4 * levels, cols)],
        out_shape=[jax.ShapeDtypeStruct((message, cols), f32), jax.ShapeDtypeStruct((4 * levels, cols), f32)],
        compiler_params=tight,
        cost_estimate=pl.CostEstimate(flops=4 * t.size, bytes_accessed=2 * t.size, transcendentals=0),
        name="halo_rows",
    )(first, second, got1, got2, seam)

    halves = cols // LANES
    held = (halves, levels, rows + 2 * TILE, LANES)
    anywhere = pl.BlockSpec(memory_space=pl.ANY)
    out = jax.ShapeDtypeStruct((levels, rows, cols), f32)
    return pl.pallas_call(
        step_kernel,
        in_specs=[anywhere] * 12,
        out_specs=[anywhere] * 3,
        out_shape=[out] * 3,
        scratch_shapes=[
            pltpu.VMEM((message, cols), f32),
            pltpu.VMEM((4 * levels, cols), f32),
        ]
        + [pltpu.VMEM((rows + 8, LANES), f32)] * 3
        + [pltpu.VMEM(held, f32)] * 6
        + [
            pltpu.VMEM((5, halves, levels, TILE, LANES), f32),
            pltpu.VMEM((halves, levels, 2 * TILE, LANES), f32),
            pltpu.VMEM((halves, levels, 2 * TILE, LANES), f32),
        ]
        * 2
        + [
            pltpu.VMEM(spacing_lengths.shape, f32),
            pltpu.VMEM(planetary_spin.shape, f32),
            pltpu.VMEM((rows, cols), jnp.int32),
            pltpu.VMEM((halves, rows + TILE, LANES), f32),
        ]
        + [pltpu.VMEM((levels, rows, cols), f32)] * 3
        + [
            pltpu.VMEM((3, cols, cols), jnp.bfloat16),
            pltpu.VMEM((3, cols, cols), jnp.bfloat16),
            pltpu.VMEM((4, levels // 2, 2 * TILE, LANES), jnp.bfloat16),
            pltpu.SemaphoreType.DMA((rows // TILE // 2 + 1,)),
            pltpu.SemaphoreType.DMA((8,)),
            pltpu.SemaphoreType.DMA((3,)),
        ],
        compiler_params=pltpu.CompilerParams(vmem_limit_bytes=60 * 2**20),
        name="ocean_step",
    )(t, s, u, v, spacing_lengths, planetary_spin, ocean_layer_number, north, south, to_west, from_east, from_west)


def solution(mesh):
    in_specs = (
        P(None, "lat", "lon"),
        P(None, "lat", "lon"),
        P(None, "lat", "lon"),
        P(None, "lat", "lon"),
        P(None, "lat", "lon"),
        P(None, "lat", "lon"),
        P("lat", "lon"),
        P(),
    )
    out_specs = (P(None, "lat", "lon"), P(None, "lat", "lon"), P(None, "lat", "lon"))
    return jax.shard_map(body, mesh=mesh, in_specs=in_specs, out_specs=out_specs, check_vma=False)
```

```python
import jax
import jax.numpy as jnp
from jax import lax
from jax.experimental import pallas as pl
from jax.experimental.pallas import tpu as pltpu
from jax.sharding import PartitionSpec as P

LANES = 128
TILE = 8

step_duration = 0.25
viscosity = 0.05
diffusivity = 0.3
expansion_coefficient = 0.6
haline_contraction = 0.8
gravity = 0.1

NEAR, FAR, SALT, ZONAL, MERID = 0, 1, 2, 3, 4
E1V_AT, E2V_AT, WET_AT = 0, 1, 2
HEAT_LANE, SALT_LANE, ZONAL_LANE, MERID_LANE = 0, 40, 56, 72
E1U_LANE, E2U_LANE, WET_LANE = 96, 97, 98


def density_of(salinity, heat):
    return haline_contraction * salinity - expansion_coefficient * heat


def inverse_of(x):
    return pltpu.reciprocal(x, approx=True)


def row_pack(t_lo, t_hi, s_lo, s_hi, u_lo, u_hi, v_lo, v_hi, e_lo, e_hi, n_lo, n_hi, first, second):
    levels = t_lo.shape[0]
    even = lax.rem(lax.axis_index("lat"), 2) == 0

    def put(slot, high, low):
        rows = pl.ds(slot * levels, levels)
        first[rows] = jnp.where(even, high, low)
        second[rows] = jnp.where(even, low, high)

    near_hi, near_lo = t_hi[:, 7, :], t_lo[:, 0, :]
    put(NEAR, near_hi, near_lo)
    put(FAR, t_hi[:, 6, :], t_lo[:, 1, :])
    put(SALT, s_hi[:, 7, :], s_lo[:, 0, :])
    put(ZONAL, u_hi[:, 7, :], u_lo[:, 0, :])
    put(MERID, v_hi[:, 7, :], v_lo[:, 0, :])
    base = 5 * levels
    high = jnp.concatenate([e_hi[4, 7:8], e_hi[5, 7:8], n_hi[7:8].astype(jnp.float32), jnp.zeros((5, e_hi.shape[2]), jnp.float32)], axis=0)
    low = jnp.concatenate([e_lo[4, 0:1], e_lo[5, 0:1], n_lo[0:1].astype(jnp.float32), jnp.zeros((5, e_lo.shape[2]), jnp.float32)], axis=0)
    first[base : base + 8] = jnp.where(even, high, low)
    second[base : base + 8] = jnp.where(even, low, high)


def vertical_span(x):
    return jnp.concatenate([x[1:], x[-1:]], axis=0) - jnp.concatenate([x[:1], x[:-1]], axis=0)


def corners(u1, u2, v1, v2, seam, east_in, west_in, east_out, west_out):
    levels, cols = u1.shape
    lat, lon = lax.axis_index("lat"), lax.axis_index("lon")
    lats, lons = lax.axis_size("lat"), lax.axis_size("lon")
    even = lax.rem(lat, 2) == 0
    is_top = lat == lats - 1
    per = cols // LANES
    pick = seam[pl.ds(lon * per + per - 1, 1), LANES - 1 : LANES] - (lons - 1 - lon) * cols
    pick = jnp.where(is_top, pick, cols - 1)
    u = jnp.where(even, u1[...], u2[...])
    u = jnp.where(is_top, -u, u)
    here = lax.broadcasted_iota(jnp.int32, (levels, cols), 1) == pick
    u = jnp.sum(jnp.where(here, u, 0.0), axis=1, keepdims=True)
    v = jnp.where(lat == 0, 0.0, jnp.where(even, v2[:, 0:1], v1[:, 0:1]))
    sub16 = lax.broadcasted_iota(jnp.int32, (levels, LANES), 0)
    lane16 = lax.broadcasted_iota(jnp.int32, (levels, LANES), 1)

    def line(x, base):
        return jnp.sum(jnp.where(lane16 == sub16 + base, x, 0.0), axis=0, keepdims=True)

    east_out[...] = jnp.broadcast_to(line(u, ZONAL_LANE), (8, LANES))
    west_out[...] = jnp.broadcast_to(line(v, MERID_LANE + 1), (8, LANES))


def halo_rows(mine1, mine2, got1, got2, seam, north_out, south_out):
    levels = (mine1.shape[0] - 8) // 5
    cols = mine1.shape[1]
    lat, lon = lax.axis_index("lat"), lax.axis_index("lon")
    lats, lons = lax.axis_size("lat"), lax.axis_size("lon")
    even = lax.rem(lat, 2) == 0
    is_top = lat == lats - 1
    is_bottom = lat == 0
    north_rows = got1.shape[0]
    for h in range(cols // LANES):
        span = slice(h * LANES, (h + 1) * LANES)
        pick = seam[pl.ds(lon * (cols // LANES) + h, 1), :] - (lons - 1 - lon) * cols
        pick = jnp.where(is_top, pick, lax.broadcasted_iota(jnp.int32, (1, LANES), 1) + h * LANES)
        pick = jnp.broadcast_to(pick, (TILE, LANES))
        inner = jnp.bitwise_and(pick, LANES - 1)
        for row in range(0, north_rows, TILE):
            total = None
            for g in range(cols // LANES):
                piece = slice(g * LANES, (g + 1) * LANES)
                source = jnp.where(even, got1[row : row + TILE, piece], got2[row : row + TILE, piece])
                taken = jnp.take_along_axis(source, inner, axis=1, mode="promise_in_bounds")
                taken = jnp.where(pick >= g * LANES, taken, 0.0) if g == 0 else taken
                total = taken if total is None else jnp.where(pick >= g * LANES, taken, total)
            if ZONAL * levels <= row < (MERID + 1) * levels:
                total = jnp.where(is_top, -total, total)
            north_out[row : row + TILE, span] = total
    def south(slot):
        part = slice(slot * levels, (slot + 1) * levels)
        return jnp.where(is_bottom, 0.0, jnp.where(even, got2[part], got1[part]))

    def own(slot):
        part = slice(slot * levels, (slot + 1) * levels)
        return jnp.where(even, mine2[part], mine1[part])

    tail = slice(5 * levels, 5 * levels + 8)
    coef = jnp.where(even, got2[tail], got1[tail])
    own_wet = jnp.where(even, mine2[tail], mine1[tail])[WET_AT : WET_AT + 1]
    e1v = jnp.where(is_bottom, 1.0, coef[E1V_AT : E1V_AT + 1])
    e2v = jnp.where(is_bottom, 1.0, coef[E2V_AT : E2V_AT + 1])
    wet = jnp.where(is_bottom, 0.0, coef[WET_AT : WET_AT + 1])
    t_near, t_far, v_near = south(NEAR), south(FAR), south(MERID)
    t_own, t_next = own(NEAR), own(FAR)
    d_near, d_own = density_of(south(SALT), t_near), density_of(own(SALT), t_own)
    t_sum = t_near + t_own
    adv = (e1v / 12.0) * v_near * (7.0 * t_sum - (t_far + t_next))
    d_span = vertical_span(d_near + d_own)
    tilt = (d_own - d_near) * d_span * vertical_span(t_sum) / (d_span * d_span + 16.0)
    iso = (diffusivity * e1v / e2v) * (t_own - t_near - tilt)
    level = lax.broadcasted_iota(jnp.int32, (levels, cols), 0).astype(jnp.float32)
    flux = jnp.where(level < jnp.minimum(wet, own_wet), iso - adv, 0.0)
    south_out[0:levels] = t_near
    south_out[levels : 2 * levels] = flux
    south_out[2 * levels : 3 * levels] = south(ZONAL)
    south_out[3 * levels : 4 * levels] = v_near


def column_pack(group, t, s, u, v, e, n, east_out, west_out):
    rows, cols = t.shape[1:]
    step = pl.program_id(0)
    lane = lax.broadcasted_iota(jnp.int32, (rows, LANES), 1)
    pair = lax.shift_right_logical(lane, 1)
    first = slice(0, LANES)
    last = slice(cols - LANES, cols)

    @pl.when(step == 0)
    def _():
        n_f = n[...].astype(jnp.float32)
        hi = jnp.where(lane == E1U_LANE, pltpu.roll(e[0, :, last], (E1U_LANE + 1) % LANES, 1), 0.0)
        hi = jnp.where(lane == E2U_LANE, pltpu.roll(e[1, :, last], (E2U_LANE + 1) % LANES, 1), hi)
        east_out[0:rows] = jnp.where(lane == WET_LANE, pltpu.roll(n_f[:, last], (WET_LANE + 1) % LANES, 1), hi)
        west_out[8 : rows + 8] = jnp.where(lane == WET_LANE, pltpu.roll(n_f[:, first], WET_LANE, 1), 0.0)
        east_out[rows : rows + 8] = jnp.zeros((8, LANES), jnp.float32)
        west_out[0:8] = jnp.zeros((8, LANES), jnp.float32)

    hi = east_out[0:rows]
    lo = west_out[8 : rows + 8]
    for kk in range(group):
        k = step * group + kk
        for field, base in ((t, HEAT_LANE), (s, SALT_LANE), (u, ZONAL_LANE), (v, MERID_LANE)):
            ends = jnp.where(lane < LANES // 2, field[kk, :, first], field[kk, :, last])
            if field is t:
                ends = pltpu.roll(ends, 2 * k + 2, 1)
                hi = jnp.where(pair == k, ends, hi)
                lo = jnp.where(pair == k + 1, ends, lo)
            else:
                ends = pltpu.roll(ends, base + 1 + k, 1)
                hi = jnp.where(lane == base + k, ends, hi)
                lo = jnp.where(lane == base + 1 + k, ends, lo)
    east_out[0:rows] = hi
    west_out[8 : rows + 8] = lo


def step_kernel(
    t_hbm, s_hbm, u_hbm, v_hbm, e_hbm, f_hbm, n_hbm, north_hbm, south_hbm, own_hbm, from_east_hbm, from_west_hbm,
    u_out, v_out, t_out,
    north, south, own_west, from_east, from_west, t_s, s_s, u_s, v_s, d_s, g_s, mixed_a, uw_a, ve_a, mixed_b, uw_b, ve_b, e_s, f_s, n_s, nf_s, uo_s, vo_s, to_s, move_s, rim_s, mask_s, coef_s,
    in_sem, flat_sem, out_sem,
):
    levels, rows, cols = t_hbm.shape
    tiles = rows // TILE
    halves = cols // LANES
    both = range(halves)
    pairs = (tiles - 1) // 2
    assert tiles == 2 * pairs + 1

    fields = ((t_hbm, t_s), (s_hbm, s_s), (u_hbm, u_s), (v_hbm, v_s))

    def load(first, count, unit):
        span = pl.ds(first * TILE, count * TILE)
        held = pl.ds(first * TILE + TILE, count * TILE)
        for hbm, vmem in fields:
            for h in both:
                pltpu.make_async_copy(
                    hbm.at[:, span, pl.ds(h * LANES, LANES)], vmem.at[h, :, held, :], in_sem.at[unit]
                ).start()

    def loaded(count, unit):
        span = pl.ds(0, len(fields) * halves * count * TILE)
        pltpu.make_async_copy(t_hbm.at[:, span, pl.ds(0, LANES)], t_s.at[0, :, span, :], in_sem.at[unit]).wait()

    outs = ((uo_s, u_out), (vo_s, v_out), (to_s, t_out))

    def store(row, count):
        span = pl.ds(row, count * TILE)
        for i, (vmem, hbm) in enumerate(outs):
            pltpu.make_async_copy(vmem.at[:, span, :], hbm.at[:, span, :], out_sem.at[i]).start()

    flat = [
        pltpu.make_async_copy(hbm, vmem, flat_sem.at[i])
        for i, (hbm, vmem) in enumerate(
            (
                (e_hbm, e_s),
                (f_hbm, f_s),
                (n_hbm, n_s),
                (north_hbm, north),
                (south_hbm, south),
                (own_hbm, own_west),
                (from_east_hbm, from_east),
                (from_west_hbm, from_west),
            )
        )
    ]
    for copy in flat[2:]:
        copy.start()
    load(0, 1, 0)
    for copy in flat[:2]:
        copy.start()
    load(1, 2, 1)
    for unit in range(2, pairs + 1):
        load(2 * unit - 1, 2, unit)

    source = lax.broadcasted_iota(jnp.int32, (cols, cols), 0)
    target = lax.broadcasted_iota(jnp.int32, (cols, cols), 1)
    apart = source - target

    def matrix(*terms):
        total = jnp.zeros((cols, cols), jnp.float32)
        for where, value in terms:
            total = jnp.where(where, value, total)
        return total.astype(jnp.bfloat16)

    at = [apart == i for i in range(-1, 3)]
    move_s[0] = matrix((at[0], -1.0), (at[1], 7.0), (at[2], 7.0), (at[3], -1.0))
    move_s[1] = matrix((at[0], 1.0))
    move_s[2] = matrix((at[2], 1.0))
    origin = jnp.bitwise_and(source, LANES - 1)
    odd = jnp.bitwise_and(origin, 1) == 1
    west_end, east_end = target == 0, target == cols - 1
    heat_east, heat_west = origin < 32, (origin >= 32) & (origin < 64) & odd
    rim_s[0] = matrix(
        (heat_east & ~odd & (target == cols - 2), -1.0),
        (heat_east & ~odd & east_end, 7.0),
        (heat_east & odd & east_end, -1.0),
        (heat_west & west_end, -1.0),
    )
    western = jnp.bitwise_and(origin, 16) == 16
    rim_s[1] = matrix(((origin >= 64) & western & west_end, 1.0))
    rim_s[2] = matrix(
        ((origin >= 64) & ~western & east_end, 1.0),
        (heat_east & ~odd & east_end, 1.0),
        ((origin >= 32) & (origin < 64) & ~odd & east_end, 1.0),
    )

    for copy in flat[2:]:
        copy.wait()
    low, high = TILE - 1, TILE + rows
    north_density = density_of(
        north[SALT * levels : (SALT + 1) * levels, :], north[NEAR * levels : (NEAR + 1) * levels, :]
    )
    for h in both:
        span = slice(h * LANES, (h + 1) * LANES)
        for k in range(levels):
            t_s[h, k, low : low + 1, :] = south[k : k + 1, span]
            g_s[h, k, low : low + 1, :] = south[levels + k : levels + k + 1, span]
            u_s[h, k, low : low + 1, :] = south[2 * levels + k : 2 * levels + k + 1, span]
            v_s[h, k, low : low + 1, :] = south[3 * levels + k : 3 * levels + k + 1, span]
            t_s[h, k, high : high + 1, :] = north[NEAR * levels + k : NEAR * levels + k + 1, span]
            t_s[h, k, high + 1 : high + 2, :] = north[FAR * levels + k : FAR * levels + k + 1, span]
            d_s[h, k, high : high + 1, :] = north_density[k : k + 1, span]
            u_s[h, k, high : high + 1, :] = north[ZONAL * levels + k : ZONAL * levels + k + 1, span]
            v_s[h, k, high : high + 1, :] = north[MERID * levels + k : MERID * levels + k + 1, span]
        nf_s[h, rows : rows + 1, :] = north[5 * levels + WET_AT : 5 * levels + WET_AT + 1, span]
    for h in both:
        nf_s[h, 0:rows, :] = n_s[:, h * LANES : (h + 1) * LANES].astype(jnp.float32)

    lane = lax.broadcasted_iota(jnp.int32, (TILE, LANES), 1)
    is_last = lane == LANES - 1
    is_first = lane == 0
    from_rim_west = ((lane >= 32) & (lane < 64)) | ((lane >= 80) & (lane < 96)) | (lane >= 112)
    rim_source = jnp.where(
        lane < 32,
        lane + 2,
        jnp.where(
            lane < 64,
            lane - 32,
            jnp.where(
                lane < 80,
                lane - 64 + ZONAL_LANE + 1,
                jnp.where(
                    lane < 96,
                    lane - 80 + ZONAL_LANE,
                    jnp.where(lane < 112, lane - 96 + MERID_LANE + 1, lane - 112 + MERID_LANE),
                ),
            ),
        ),
    )
    lane2 = lax.broadcasted_iota(jnp.int32, (2 * TILE, LANES), 1)
    second = lax.broadcasted_iota(jnp.int32, (2 * TILE, LANES), 0) >= TILE
    level2 = jnp.where(lane2 < 64, lax.shift_right_logical(jnp.bitwise_and(lane2, 31), 1), jnp.bitwise_and(lane2, 15))
    level2 = level2 - jnp.where(second, 1, 0)
    for_density = (lane2 >= 32) & (lane2 < 64) & (jnp.bitwise_and(lane2, 1) == 0)
    kinds = ((lane2 < 64) & ~for_density, (lane2 >= 64) & (lane2 < 96), lane2 >= 96, for_density)
    for i, kind in enumerate(kinds):
        for p in range(levels // 2):
            mask_s[i, p] = jnp.where(kind & (level2 == 2 * p), 1.0, 0.0).astype(jnp.bfloat16)
    density_lane = (lane >= 32) & (lane < 64) & (jnp.bitwise_and(lane, 1) == 0)
    salt_source = jnp.bitwise_and(SALT_LANE + 1 + lax.shift_right_logical(lane - 32, 1), LANES - 1)
    heat_source = jnp.bitwise_and(lane - 30, LANES - 1)

    def to_lane(x, source, target):
        return pltpu.roll(x, (target - source) % LANES, 1)

    def east_of(x, halo, source):
        turned = [pltpu.roll(p, LANES - 1, 1) for p in x] + [to_lane(halo, source, LANES - 1)]
        return [jnp.where(is_last, turned[h + 1], turned[h]) for h in both]

    def west_of(x, halo, source):
        turned = [to_lane(halo, source, 0)] + [pltpu.roll(p, 1, 1) for p in x]
        return [jnp.where(is_first, turned[h], turned[h + 1]) for h in both]

    def two_parts(x):
        high_part = x.astype(jnp.bfloat16)
        return [high_part, (x - high_part.astype(jnp.float32)).astype(jnp.bfloat16)]

    def moved(parts, edges, i):
        y = jnp.dot(edges, rim_s[i], preferred_element_type=jnp.float32) if edges is not None else 0.0
        for p in parts:
            y = y + jnp.dot(p, move_s[i], preferred_element_type=jnp.float32)
        return y

    def prepare(r):
        flat_at = pl.ds(pl.multiple_of(r * TILE, TILE), TILE)
        dt = step_duration
        wet = [nf_s[h, flat_at, :] for h in both]
        wet_e = east_of(wet, from_east[pl.ds(pl.multiple_of(r * TILE, TILE) + TILE, TILE), :], WET_LANE)
        for h in both:
            e1t, e2t, e1u, e2u, e1v, e2v = (e_s[i, flat_at, h * LANES : (h + 1) * LANES] for i in range(6))
            fu, fv = (f_s[i, flat_at, h * LANES : (h + 1) * LANES] for i in range(2))
            wet_n = nf_s[h, pl.ds(pl.multiple_of(r * TILE, TILE) + 1, TILE), :]
            iu1, iu2, iv1, iv2 = (inverse_of(x) for x in (e1u, e2u, e1v, e2v))

            def speeds(spin, along, across, a, b):
                c4, c5 = dt * viscosity * a * a, dt * viscosity * b * b
                return 0.25 * dt * spin, 0.125 * dt * across, 0.5 * dt * along, c4, c5, 2.0 * (c4 + c5)

            values = speeds(fu, iu1, iu2, iu1, iu2) + (0.5 * gravity * dt * iu1, diffusivity * e2u * iu1, e2u * (1.0 / 12.0))
            values += speeds(-fv, iv2, iv1, iv1, iv2) + (0.5 * gravity * dt * iv2, diffusivity * e1v * iv2, e1v * (1.0 / 12.0))
            values += (dt * inverse_of(e1t * e2t), jnp.minimum(wet[h], wet_e[h]), jnp.minimum(wet[h], wet_n))
            for i, value in enumerate(values):
                coef_s[i, h, flat_at, :] = value

    def mix(r, kept, previous):
        mixed, uw_s, ve_s = kept
        row = pl.multiple_of(r * TILE, TILE)
        prepare(r)

        def turned(x, order):
            return jnp.take_along_axis(x, order, axis=1, mode="promise_in_bounds")

        east = from_east[pl.ds(row + TILE, TILE), :]
        x = jnp.where(from_rim_west, turned(from_west[pl.ds(row, TILE), :], rim_source), turned(east, rim_source))
        x = jnp.where(density_lane, density_of(turned(east, salt_source), turned(east, heat_source)), x)
        twice = [jnp.concatenate([p, p], axis=0) for p in two_parts(x)]

        def spread(kind):
            split = [[p * mask_s[kind, i] for i in range(levels // 2)] for p in twice]
            return jnp.concatenate([jnp.concatenate(q, axis=0) for q in split], axis=1)

        rim_t, rim_u, rim_v, rim_d = (spread(kind) for kind in range(4))

        def of(values):
            return two_parts(jnp.concatenate(values, axis=-1).reshape(levels * TILE, cols))

        def held_in(ref):
            return [ref[h, :, pl.ds(row + TILE, TILE), :] for h in both]

        def piece(y, i, h):
            count = levels * TILE
            return y[i * count : (i + 1) * count, h * LANES : (h + 1) * LANES].reshape(levels, TILE, LANES)

        d = [density_of(salt, heat) for salt, heat in zip(held_in(s_s), held_in(t_s))]
        for h in both:
            d_s[h, :, pl.ds(row + TILE, TILE), :] = d[h]
        parts = [of(held_in(u_s)), of(held_in(v_s)), of(held_in(t_s)), of(d)]
        y = moved([jnp.concatenate(p, axis=0) for p in zip(*parts)], jnp.concatenate([rim_u, rim_v, rim_t, rim_d], axis=0), 2)
        for h in both:
            mixed[0, h] = piece(y, 0, h)
            ve_s[h, :, TILE : 2 * TILE, :] = piece(y, 1, h)
            mixed[3, h] = piece(y, 2, h)
            mixed[4, h] = piece(y, 3, h)
        y = moved(parts[2], rim_t, 0)
        for h in both:
            mixed[2, h] = piece(y, 0, h)
        y = moved([jnp.concatenate(p, axis=0) for p in zip(*parts[:2])], jnp.concatenate([rim_u, rim_v], axis=0), 1)
        for h in both:
            uw = piece(y, 0, h)
            uw_s[h, :, 0:TILE, :] = uw
            previous[1][h, :, TILE : TILE + 1, :] = uw[:, 0:1, :]
            mixed[1, h] = piece(y, 1, h)

    sub16 = lax.broadcasted_iota(jnp.int32, (levels, LANES), 0)
    lane16 = lax.broadcasted_iota(jnp.int32, (levels, LANES), 1)

    def corner(line, base):
        wide = jnp.broadcast_to(line, (levels, LANES))
        return jnp.sum(jnp.where(lane16 == sub16 + base, wide, 0.0), axis=1, keepdims=True)

    edge = moved(two_parts(south[3 * levels : 4 * levels, :]), None, 2)
    edge = [edge[:, h * LANES : (h + 1) * LANES] for h in both]
    edge[-1] = jnp.where(lane16 == LANES - 1, corner(from_east[TILE - 1 : TILE, :], MERID_LANE + 1), edge[-1])
    for h in both:
        for k in range(levels):
            ve_a[h, k, TILE - 1 : TILE, :] = edge[h][k : k + 1]

    def advance(r, kept, following):
        mixed, uw_s, ve_s = kept
        for h in both:
            following[2][h, :, TILE - 1 : TILE, :] = ve_s[h, :, 2 * TILE - 1 : 2 * TILE, :]
        row = pl.multiple_of(r * TILE, TILE)
        flat_at = pl.ds(row, TILE)

        def rows_of(ref, k, shift):
            return [ref[h, k, pl.ds(row + TILE + shift, TILE), :] for h in both]

        east = from_east[pl.ds(row + TILE, TILE), :]
        west = from_west[flat_at, :]
        own = own_west[pl.ds(row + TILE, TILE), :]

        def span_of(x):
            up = jnp.where(lane < levels - 1, pltpu.roll(x, LANES - 1, 1), x)
            down = jnp.where(lane > 0, pltpu.roll(x, 1, 1), x)
            return up - down

        def heat_lane(x, offset):
            order = jnp.bitwise_and(2 * lane + offset, LANES - 1)
            return jnp.take_along_axis(x, order, axis=1, mode="promise_in_bounds")

        t_near, t_own = heat_lane(west, 1), heat_lane(own, 2)
        t_sum, t_far = t_near + t_own, heat_lane(west, 0) + heat_lane(own, 3)
        d_near = density_of(to_lane(west, SALT_LANE, 0), t_near)
        d_own = density_of(to_lane(own, SALT_LANE + 1, 0), t_own)
        e1 = jnp.broadcast_to(west[:, E1U_LANE : E1U_LANE + 1], (TILE, LANES))
        e2 = jnp.broadcast_to(west[:, E2U_LANE : E2U_LANE + 1], (TILE, LANES))
        wet_w = jnp.broadcast_to(jnp.minimum(west, own)[:, WET_LANE : WET_LANE + 1], (TILE, LANES))
        d_span = span_of(d_near + d_own)
        tilt = (d_own - d_near) * d_span * span_of(t_sum) * inverse_of(d_span * d_span + 16.0)
        flux_w = diffusivity * e2 * inverse_of(e1) * (t_own - t_near - tilt)
        flux_w = flux_w - e2 * (1.0 / 12.0) * to_lane(west, ZONAL_LANE, 0) * (7.0 * t_sum - t_far)
        flux_w = jnp.where(lane.astype(jnp.float32) < wet_w, flux_w, 0.0)

        def coefficient(i):
            return [coef_s[i, h, flat_at, :] for h in both]

        store_at = lambda h: (flat_at, pl.ds(h * LANES, LANES))
        zero = jnp.zeros((TILE, LANES), jnp.float32)

        run = [zero for _ in both]

        def east_parts(k):
            t, d, u = rows_of(t_s, k, 0), rows_of(d_s, k, 0), rows_of(u_s, k, 0)
            un, us = rows_of(u_s, k, 1), rows_of(u_s, k, -1)
            ue, wide, te, de = ([mixed[i, h, k] for h in both] for i in (0, 2, 3, 4))
            uw = [uw_s[h, k, 0:TILE, :] for h in both]
            v, vs = rows_of(v_s, k, 0), rows_of(v_s, k, -1)
            vbar = [
                (v[h] + vs[h]) + (ve_s[h, k, TILE : 2 * TILE, :] + ve_s[h, k, TILE - 1 : 2 * TILE - 1, :]) for h in both
            ]
            c1, c2, c3, c4, c5, c6, pu, iso_e, adv_e = (coefficient(i) for i in range(9))
            u_wet = coefficient(19)
            out = []
            for h in both:
                rise = de[h] - d[h]
                direct = iso_e[h] * (te[h] - t[h]) - adv_e[h] * u[h] * wide[h]
                out.append((t[h] + te[h], d[h] + de[h], direct, iso_e[h] * rise))
                press = run[h] + rise
                run[h] = press + rise
                du = (
                    vbar[h] * (c1[h] - c2[h] * (un[h] - us[h]))
                    - u[h] * (c3[h] * (ue[h] - uw[h]) + c6[h])
                    + c4[h] * (ue[h] + uw[h])
                    + c5[h] * (un[h] + us[h])
                    - pu[h] * press
                )
                uo_s[(k,) + store_at(h)] = u[h] + jnp.where(u_wet[h] > k, du, 0.0)
            return out

        def flux_of(below, here, above, open_face):
            t_span, d_span = above[0] - below[0], above[1] - below[1]
            flux = here[2] - here[3] * d_span * t_span * inverse_of(d_span * d_span + 16.0)
            return jnp.where(open_face, flux, 0.0)

        def east_finish(k, below, here, above):
            u_wet = coefficient(19)
            fe = [flux_of(below[h], here[h], above[h], u_wet[h] > k) for h in both]
            fw = west_of(fe, flux_w, k)
            for h in both:
                to_s[(k,) + store_at(h)] = fe[h] - fw[h]

        below = here = east_parts(0)
        for k in range(1, levels):
            above = east_parts(k)
            east_finish(k - 1, below, here, above)
            below, here = here, above
        east_finish(levels - 1, below, here, here)

        run = [zero for _ in both]

        def north_parts(k):
            t, tn, ts, tnn = (rows_of(t_s, k, i) for i in (0, 1, -1, 2))
            d, dn = rows_of(d_s, k, 0), rows_of(d_s, k, 1)
            v, vn, vs = (rows_of(v_s, k, i) for i in (0, 1, -1))
            ve, vw = [ve_s[h, k, TILE : 2 * TILE, :] for h in both], [mixed[1, h, k] for h in both]
            u, un = rows_of(u_s, k, 0), rows_of(u_s, k, 1)
            ubar = [(u[h] + un[h]) + (uw_s[h, k, 0:TILE, :] + uw_s[h, k, 1 : TILE + 1, :]) for h in both]
            c1, c2, c3, c4, c5, c6, pv, iso_n, adv_n = (coefficient(i) for i in range(9, 18))
            v_wet = coefficient(20)
            out = []
            for h in both:
                rise, pair = dn[h] - d[h], t[h] + tn[h]
                direct = iso_n[h] * (tn[h] - t[h]) - adv_n[h] * v[h] * (7.0 * pair - (ts[h] + tnn[h]))
                out.append((pair, d[h] + dn[h], direct, iso_n[h] * rise))
                press = run[h] + rise
                run[h] = press + rise
                dv = (
                    ubar[h] * (c1[h] - c2[h] * (ve[h] - vw[h]))
                    - v[h] * (c3[h] * (vn[h] - vs[h]) + c6[h])
                    + c4[h] * (ve[h] + vw[h])
                    + c5[h] * (vn[h] + vs[h])
                    - pv[h] * press
                )
                vo_s[(k,) + store_at(h)] = v[h] + jnp.where(v_wet[h] > k, dv, 0.0)
            return out

        def north_finish(k, below, here, above):
            area, v_wet, wet = coefficient(18), coefficient(20), [nf_s[h, flat_at, :] for h in both]
            for h in both:
                fn = flux_of(below[h], here[h], above[h], v_wet[h] > k)
                g_s[h, k, pl.ds(row + TILE, TILE), :] = fn
                fs = g_s[h, k, pl.ds(row + TILE - 1, TILE), :]
                at_h = (k,) + store_at(h)
                change = area[h] * (to_s[at_h] + (fn - fs))
                to_s[at_h] = t_s[h, k, pl.ds(row + TILE, TILE), :] + jnp.where(wet[h] > k, change, 0.0)

        below = here = north_parts(0)
        for k in range(1, levels):
            above = north_parts(k)
            north_finish(k - 1, below, here, above)
            below, here = here, above
        north_finish(levels - 1, below, here, here)

    set_a, set_b = (mixed_a, uw_a, ve_a), (mixed_b, uw_b, ve_b)
    flat[0].wait()
    flat[1].wait()
    loaded(1, 0)
    loaded(2, 1)
    mix(0, set_a, set_b)

    def two_tiles(i, carry):
        @pl.when(i + 2 <= pairs)
        def _():
            loaded(2, i + 2)

        mix(2 * i + 1, set_b, set_a)
        advance(2 * i, set_a, set_b)
        mix(2 * i + 2, set_a, set_b)
        advance(2 * i + 1, set_b, set_a)
        store(pl.multiple_of(i * 2 * TILE, 2 * TILE), 2)
        return carry

    lax.fori_loop(0, pairs, two_tiles, 0)
    edge = moved(two_parts(north[ZONAL * levels : (ZONAL + 1) * levels, :]), None, 1)
    edge = [edge[:, h * LANES : (h + 1) * LANES] for h in both]
    edge[0] = jnp.where(lane16 == 0, corner(from_west[rows : rows + 1, :], ZONAL_LANE), edge[0])
    for h in both:
        for k in range(levels):
            uw_a[h, k, TILE : TILE + 1, :] = edge[h][k : k + 1]
    advance(jnp.int32(2 * pairs), set_a, set_b)
    store(2 * pairs * TILE, 1)
    for i, (vmem, hbm) in enumerate(outs):
        pltpu.make_async_copy(vmem, hbm, out_sem.at[i]).wait()


def body(
    east_velocity,
    north_velocity,
    heat_anomaly,
    haline_anomaly,
    spacing_lengths,
    planetary_spin,
    ocean_layer_number,
    seam_partner_index,
):
    t, s, u, v = heat_anomaly, haline_anomaly, east_velocity, north_velocity
    levels, rows, cols = t.shape
    lats, lons = lax.axis_size("lat"), lax.axis_size("lon")
    f32 = jnp.float32
    top = rows // TILE - 1
    message = 5 * levels + 8

    low3 = pl.BlockSpec((levels, TILE, cols), lambda i: (0, 0, 0))
    high3 = pl.BlockSpec((levels, TILE, cols), lambda i: (0, top, 0))
    whole = pl.BlockSpec((message, cols), lambda i: (0, 0))
    count = spacing_lengths.shape[0]
    first, second = pl.pallas_call(
        row_pack,
        grid=(1,),
        in_specs=[low3, high3] * 4
        + [
            pl.BlockSpec((count, TILE, cols), lambda i: (0, 0, 0)),
            pl.BlockSpec((count, TILE, cols), lambda i: (0, top, 0)),
            pl.BlockSpec((TILE, cols), lambda i: (0, 0)),
            pl.BlockSpec((TILE, cols), lambda i: (top, 0)),
        ],
        out_specs=[whole, whole],
        out_shape=[jax.ShapeDtypeStruct((message, cols), f32)] * 2,
        name="row_pack",
    )(t, t, s, s, u, u, v, v, spacing_lengths, spacing_lengths, ocean_layer_number, ocean_layer_number)

    axes = ("lon", "lat")

    def place(lat, lon):
        return lon * lats + lat

    swap1, swap2 = [], []
    for lon in range(lons):
        for lat in range(0, lats, 2):
            swap1 += [(place(lat, lon), place(lat + 1, lon)), (place(lat + 1, lon), place(lat, lon))]
        for lat in range(1, lats - 1, 2):
            swap2 += [(place(lat, lon), place(lat + 1, lon)), (place(lat + 1, lon), place(lat, lon))]
        swap2.append((place(lats - 1, lon), place(lats - 1, lons - 1 - lon)))
    got1 = lax.ppermute(first, axes, swap1)
    got2 = lax.ppermute(second, axes, swap2)

    group = 8
    slab = pl.BlockSpec((group, rows, cols), lambda i: (i, 0, 0))
    message_out = jax.ShapeDtypeStruct((rows + 8, LANES), f32)
    to_east, to_west = pl.pallas_call(
        lambda *refs: column_pack(group, *refs),
        grid=(levels // group,),
        in_specs=[slab] * 4
        + [pl.BlockSpec((2, rows, cols), lambda i: (1, 0, 0)), pl.BlockSpec((rows, cols), lambda i: (0, 0))],
        out_specs=[pl.BlockSpec((rows + 8, LANES), lambda i: (0, 0))] * 2,
        out_shape=[message_out] * 2,
        compiler_params=pltpu.CompilerParams(vmem_limit_bytes=64 * 2**20),
        cost_estimate=pl.CostEstimate(flops=20 * t.size, bytes_accessed=16 * t.size, transcendentals=0),
        name="column_pack",
    )(t, s, u, v, spacing_lengths, ocean_layer_number)

    seam = seam_partner_index.reshape(-1, LANES)
    fixed = lambda *shape: pl.BlockSpec(shape, lambda i: (0,) * len(shape))
    high_edge = pl.BlockSpec((8, LANES), lambda i: (rows // 8, 0))
    low_edge = pl.BlockSpec((8, LANES), lambda i: (0, 0))
    tight = pltpu.CompilerParams(vmem_limit_bytes=64 * 2**20)
    u_rows = pl.BlockSpec((levels, cols), lambda i: (ZONAL, 0))
    v_rows = pl.BlockSpec((levels, cols), lambda i: (MERID, 0))
    to_east, to_west = pl.pallas_call(
        corners,
        grid=(1,),
        in_specs=[u_rows, u_rows, v_rows, v_rows, fixed(*seam.shape), high_edge, low_edge],
        out_specs=[high_edge, low_edge],
        out_shape=[message_out] * 2,
        input_output_aliases={5: 0, 6: 1},
        compiler_params=tight,
        name="corners",
    )(got1, got2, got1, got2, seam, to_east, to_west)

    from_west = lax.ppermute(to_east, "lon", [(i, (i + 1) % lons) for i in range(lons)])
    from_east = lax.ppermute(to_west, "lon", [((i + 1) % lons, i) for i in range(lons)])

    north, south = pl.pallas_call(
        halo_rows,
        grid=(1,),
        in_specs=[fixed(message, cols)] * 4 + [fixed(*seam.shape)],
        out_specs=[fixed(message, cols), fixed(4 * levels, cols)],
        out_shape=[jax.ShapeDtypeStruct((message, cols), f32), jax.ShapeDtypeStruct((4 * levels, cols), f32)],
        compiler_params=tight,
        cost_estimate=pl.CostEstimate(flops=4 * t.size, bytes_accessed=2 * t.size, transcendentals=0),
        name="halo_rows",
    )(first, second, got1, got2, seam)

    halves = cols // LANES
    held = (halves, levels, rows + 2 * TILE, LANES)
    anywhere = pl.BlockSpec(memory_space=pl.ANY)
    out = jax.ShapeDtypeStruct((levels, rows, cols), f32)
    return pl.pallas_call(
        step_kernel,
        in_specs=[anywhere] * 12,
        out_specs=[anywhere] * 3,
        out_shape=[out] * 3,
        scratch_shapes=[
            pltpu.VMEM((message, cols), f32),
            pltpu.VMEM((4 * levels, cols), f32),
        ]
        + [pltpu.VMEM((rows + 8, LANES), f32)] * 3
        + [pltpu.VMEM(held, f32)] * 6
        + [
            pltpu.VMEM((5, halves, levels, TILE, LANES), f32),
            pltpu.VMEM((halves, levels, 2 * TILE, LANES), f32),
            pltpu.VMEM((halves, levels, 2 * TILE, LANES), f32),
        ]
        * 2
        + [
            pltpu.VMEM(spacing_lengths.shape, f32),
            pltpu.VMEM(planetary_spin.shape, f32),
            pltpu.VMEM((rows, cols), jnp.int32),
            pltpu.VMEM((halves, rows + TILE, LANES), f32),
        ]
        + [pltpu.VMEM((levels, rows, cols), f32)] * 3
        + [
            pltpu.VMEM((3, cols, cols), jnp.bfloat16),
            pltpu.VMEM((3, cols, cols), jnp.bfloat16),
            pltpu.VMEM((4, levels // 2, 2 * TILE, LANES), jnp.bfloat16),
            pltpu.VMEM((21, halves, rows, LANES), f32),
            pltpu.SemaphoreType.DMA((rows // TILE // 2 + 1,)),
            pltpu.SemaphoreType.DMA((8,)),
            pltpu.SemaphoreType.DMA((3,)),
        ],
        compiler_params=pltpu.CompilerParams(vmem_limit_bytes=60 * 2**20),
        name="ocean_step",
    )(t, s, u, v, spacing_lengths, planetary_spin, ocean_layer_number, north, south, to_west, from_east, from_west)


def solution(mesh):
    in_specs = (
        P(None, "lat", "lon"),
        P(None, "lat", "lon"),
        P(None, "lat", "lon"),
        P(None, "lat", "lon"),
        P(None, "lat", "lon"),
        P(None, "lat", "lon"),
        P("lat", "lon"),
        P(),
    )
    out_specs = (P(None, "lat", "lon"), P(None, "lat", "lon"), P(None, "lat", "lon"))
    return jax.shard_map(body, mesh=mesh, in_specs=in_specs, out_specs=out_specs, check_vma=False)
```

```python
import jax
import jax.numpy as jnp
from jax import lax
from jax.experimental import pallas as pl
from jax.experimental.pallas import tpu as pltpu
from jax.sharding import PartitionSpec as P

LANES = 128
TILE = 8

step_duration = 0.25
viscosity = 0.05
diffusivity = 0.3
expansion_coefficient = 0.6
haline_contraction = 0.8
gravity = 0.1

NEAR, FAR, SALT, ZONAL, MERID = 0, 1, 2, 3, 4
E1V_AT, E2V_AT, WET_AT = 0, 1, 2
HEAT_LANE, SALT_LANE, ZONAL_LANE, MERID_LANE = 0, 40, 56, 72
E1U_LANE, E2U_LANE, WET_LANE = 96, 97, 98


def density_of(salinity, heat):
    return haline_contraction * salinity - expansion_coefficient * heat


def inverse_of(x):
    return pltpu.reciprocal(x, approx=True)


def row_pack(t_lo, t_hi, s_lo, s_hi, u_lo, u_hi, v_lo, v_hi, e_lo, e_hi, n_lo, n_hi, first, second):
    levels = t_lo.shape[0]
    even = lax.rem(lax.axis_index("lat"), 2) == 0

    def put(slot, high, low):
        rows = pl.ds(slot * levels, levels)
        first[rows] = jnp.where(even, high, low)
        second[rows] = jnp.where(even, low, high)

    near_hi, near_lo = t_hi[:, 7, :], t_lo[:, 0, :]
    put(NEAR, near_hi, near_lo)
    put(FAR, t_hi[:, 6, :], t_lo[:, 1, :])
    put(SALT, s_hi[:, 7, :], s_lo[:, 0, :])
    put(ZONAL, u_hi[:, 7, :], u_lo[:, 0, :])
    put(MERID, v_hi[:, 7, :], v_lo[:, 0, :])
    base = 5 * levels
    high = jnp.concatenate([e_hi[4, 7:8], e_hi[5, 7:8], n_hi[7:8].astype(jnp.float32), jnp.zeros((5, e_hi.shape[2]), jnp.float32)], axis=0)
    low = jnp.concatenate([e_lo[4, 0:1], e_lo[5, 0:1], n_lo[0:1].astype(jnp.float32), jnp.zeros((5, e_lo.shape[2]), jnp.float32)], axis=0)
    first[base : base + 8] = jnp.where(even, high, low)
    second[base : base + 8] = jnp.where(even, low, high)


def vertical_span(x):
    return jnp.concatenate([x[1:], x[-1:]], axis=0) - jnp.concatenate([x[:1], x[:-1]], axis=0)


def corners(u1, u2, v1, v2, seam, east_in, west_in, east_out, west_out):
    levels, cols = u1.shape
    lat, lon = lax.axis_index("lat"), lax.axis_index("lon")
    lats, lons = lax.axis_size("lat"), lax.axis_size("lon")
    even = lax.rem(lat, 2) == 0
    is_top = lat == lats - 1
    per = cols // LANES
    pick = seam[pl.ds(lon * per + per - 1, 1), LANES - 1 : LANES] - (lons - 1 - lon) * cols
    pick = jnp.where(is_top, pick, cols - 1)
    u = jnp.where(even, u1[...], u2[...])
    u = jnp.where(is_top, -u, u)
    here = lax.broadcasted_iota(jnp.int32, (levels, cols), 1) == pick
    u = jnp.sum(jnp.where(here, u, 0.0), axis=1, keepdims=True)
    v = jnp.where(lat == 0, 0.0, jnp.where(even, v2[:, 0:1], v1[:, 0:1]))
    sub16 = lax.broadcasted_iota(jnp.int32, (levels, LANES), 0)
    lane16 = lax.broadcasted_iota(jnp.int32, (levels, LANES), 1)

    def line(x, base):
        return jnp.sum(jnp.where(lane16 == sub16 + base, x, 0.0), axis=0, keepdims=True)

    east_out[...] = jnp.broadcast_to(line(u, ZONAL_LANE), (8, LANES))
    west_out[...] = jnp.broadcast_to(line(v, MERID_LANE + 1), (8, LANES))


def halo_rows(mine1, mine2, got1, got2, seam, north_out, south_out):
    levels = (mine1.shape[0] - 8) // 5
    cols = mine1.shape[1]
    lat, lon = lax.axis_index("lat"), lax.axis_index("lon")
    lats, lons = lax.axis_size("lat"), lax.axis_size("lon")
    even = lax.rem(lat, 2) == 0
    is_top = lat == lats - 1
    is_bottom = lat == 0
    north_rows = got1.shape[0]
    for h in range(cols // LANES):
        span = slice(h * LANES, (h + 1) * LANES)
        pick = seam[pl.ds(lon * (cols // LANES) + h, 1), :] - (lons - 1 - lon) * cols
        pick = jnp.where(is_top, pick, lax.broadcasted_iota(jnp.int32, (1, LANES), 1) + h * LANES)
        pick = jnp.broadcast_to(pick, (TILE, LANES))
        inner = jnp.bitwise_and(pick, LANES - 1)
        for row in range(0, north_rows, TILE):
            total = None
            for g in range(cols // LANES):
                piece = slice(g * LANES, (g + 1) * LANES)
                source = jnp.where(even, got1[row : row + TILE, piece], got2[row : row + TILE, piece])
                taken = jnp.take_along_axis(source, inner, axis=1, mode="promise_in_bounds")
                taken = jnp.where(pick >= g * LANES, taken, 0.0) if g == 0 else taken
                total = taken if total is None else jnp.where(pick >= g * LANES, taken, total)
            if ZONAL * levels <= row < (MERID + 1) * levels:
                total = jnp.where(is_top, -total, total)
            north_out[row : row + TILE, span] = total
    def south(slot):
        part = slice(slot * levels, (slot + 1) * levels)
        return jnp.where(is_bottom, 0.0, jnp.where(even, got2[part], got1[part]))

    def own(slot):
        part = slice(slot * levels, (slot + 1) * levels)
        return jnp.where(even, mine2[part], mine1[part])

    tail = slice(5 * levels, 5 * levels + 8)
    coef = jnp.where(even, got2[tail], got1[tail])
    own_wet = jnp.where(even, mine2[tail], mine1[tail])[WET_AT : WET_AT + 1]
    e1v = jnp.where(is_bottom, 1.0, coef[E1V_AT : E1V_AT + 1])
    e2v = jnp.where(is_bottom, 1.0, coef[E2V_AT : E2V_AT + 1])
    wet = jnp.where(is_bottom, 0.0, coef[WET_AT : WET_AT + 1])
    t_near, t_far, v_near = south(NEAR), south(FAR), south(MERID)
    t_own, t_next = own(NEAR), own(FAR)
    d_near, d_own = density_of(south(SALT), t_near), density_of(own(SALT), t_own)
    t_sum = t_near + t_own
    adv = (e1v / 12.0) * v_near * (7.0 * t_sum - (t_far + t_next))
    d_span = vertical_span(d_near + d_own)
    tilt = (d_own - d_near) * d_span * vertical_span(t_sum) / (d_span * d_span + 16.0)
    iso = (diffusivity * e1v / e2v) * (t_own - t_near - tilt)
    level = lax.broadcasted_iota(jnp.int32, (levels, cols), 0).astype(jnp.float32)
    flux = jnp.where(level < jnp.minimum(wet, own_wet), iso - adv, 0.0)
    south_out[0:levels] = t_near
    south_out[levels : 2 * levels] = flux
    south_out[2 * levels : 3 * levels] = south(ZONAL)
    south_out[3 * levels : 4 * levels] = v_near


def column_pack(group, t, s, u, v, e, n, east_out, west_out):
    rows, cols = t.shape[1:]
    step = pl.program_id(0)
    lane = lax.broadcasted_iota(jnp.int32, (rows, LANES), 1)
    pair = lax.shift_right_logical(lane, 1)
    first = slice(0, LANES)
    last = slice(cols - LANES, cols)

    @pl.when(step == 0)
    def _():
        n_f = n[...].astype(jnp.float32)
        hi = jnp.where(lane == E1U_LANE, pltpu.roll(e[0, :, last], (E1U_LANE + 1) % LANES, 1), 0.0)
        hi = jnp.where(lane == E2U_LANE, pltpu.roll(e[1, :, last], (E2U_LANE + 1) % LANES, 1), hi)
        east_out[0:rows] = jnp.where(lane == WET_LANE, pltpu.roll(n_f[:, last], (WET_LANE + 1) % LANES, 1), hi)
        west_out[8 : rows + 8] = jnp.where(lane == WET_LANE, pltpu.roll(n_f[:, first], WET_LANE, 1), 0.0)
        east_out[rows : rows + 8] = jnp.zeros((8, LANES), jnp.float32)
        west_out[0:8] = jnp.zeros((8, LANES), jnp.float32)

    hi = east_out[0:rows]
    lo = west_out[8 : rows + 8]
    for kk in range(group):
        k = step * group + kk
        for field, base in ((t, HEAT_LANE), (s, SALT_LANE), (u, ZONAL_LANE), (v, MERID_LANE)):
            ends = jnp.where(lane < LANES // 2, field[kk, :, first], field[kk, :, last])
            if field is t:
                ends = pltpu.roll(ends, 2 * k + 2, 1)
                hi = jnp.where(pair == k, ends, hi)
                lo = jnp.where(pair == k + 1, ends, lo)
            else:
                ends = pltpu.roll(ends, base + 1 + k, 1)
                hi = jnp.where(lane == base + k, ends, hi)
                lo = jnp.where(lane == base + 1 + k, ends, lo)
    east_out[0:rows] = hi
    west_out[8 : rows + 8] = lo


def step_kernel(
    t_hbm, s_hbm, u_hbm, v_hbm, e_hbm, f_hbm, n_hbm, north_hbm, south_hbm, own_hbm, from_east_hbm, from_west_hbm,
    u_out, v_out, t_out,
    north, south, own_west, from_east, from_west, t_s, s_s, u_s, v_s, g_s, mixed_a, uw_a, ve_a, den_a, coef_a, mixed_b, uw_b, ve_b, den_b, coef_b, e_s, f_s, n_s, nf_s, uo_s, vo_s, to_s, move_s, rim_s, mask_s,
    in_sem, flat_sem, out_sem,
):
    levels, rows, cols = t_hbm.shape
    tiles = rows // TILE
    halves = cols // LANES
    both = range(halves)
    pairs = (tiles - 1) // 2
    assert tiles == 2 * pairs + 1

    fields = ((t_hbm, t_s), (s_hbm, s_s), (u_hbm, u_s), (v_hbm, v_s))

    def load(first, count, unit):
        span = pl.ds(first * TILE, count * TILE)
        held = pl.ds(first * TILE + TILE, count * TILE)
        for hbm, vmem in fields:
            for h in both:
                pltpu.make_async_copy(
                    hbm.at[:, span, pl.ds(h * LANES, LANES)], vmem.at[h, :, held, :], in_sem.at[unit]
                ).start()

    def loaded(count, unit):
        span = pl.ds(0, len(fields) * halves * count * TILE)
        pltpu.make_async_copy(t_hbm.at[:, span, pl.ds(0, LANES)], t_s.at[0, :, span, :], in_sem.at[unit]).wait()

    outs = ((uo_s, u_out), (vo_s, v_out), (to_s, t_out))

    def store(row, count):
        span = pl.ds(row, count * TILE)
        for i, (vmem, hbm) in enumerate(outs):
            pltpu.make_async_copy(vmem.at[:, span, :], hbm.at[:, span, :], out_sem.at[i]).start()

    flat = [
        pltpu.make_async_copy(hbm, vmem, flat_sem.at[i])
        for i, (hbm, vmem) in enumerate(
            (
                (e_hbm, e_s),
                (f_hbm, f_s),
                (n_hbm, n_s),
                (north_hbm, north),
                (south_hbm, south),
                (own_hbm, own_west),
                (from_east_hbm, from_east),
                (from_west_hbm, from_west),
            )
        )
    ]
    for copy in flat[2:]:
        copy.start()
    load(0, 1, 0)
    for copy in flat[:2]:
        copy.start()
    load(1, 2, 1)
    for unit in range(2, pairs + 1):
        load(2 * unit - 1, 2, unit)

    source = lax.broadcasted_iota(jnp.int32, (cols, cols), 0)
    target = lax.broadcasted_iota(jnp.int32, (cols, cols), 1)
    apart = source - target

    def matrix(*terms):
        total = jnp.zeros((cols, cols), jnp.float32)
        for where, value in terms:
            total = jnp.where(where, value, total)
        return total.astype(jnp.bfloat16)

    at = [apart == i for i in range(-1, 3)]
    move_s[0] = matrix((at[0], -1.0), (at[1], 7.0), (at[2], 7.0), (at[3], -1.0))
    move_s[1] = matrix((at[0], 1.0))
    move_s[2] = matrix((at[2], 1.0))
    origin = jnp.bitwise_and(source, LANES - 1)
    odd = jnp.bitwise_and(origin, 1) == 1
    west_end, east_end = target == 0, target == cols - 1
    heat_east, heat_west = origin < 32, (origin >= 32) & (origin < 64) & odd
    rim_s[0] = matrix(
        (heat_east & ~odd & (target == cols - 2), -1.0),
        (heat_east & ~odd & east_end, 7.0),
        (heat_east & odd & east_end, -1.0),
        (heat_west & west_end, -1.0),
    )
    western = jnp.bitwise_and(origin, 16) == 16
    rim_s[1] = matrix(((origin >= 64) & western & west_end, 1.0))
    rim_s[2] = matrix(
        ((origin >= 64) & ~western & east_end, 1.0),
        (heat_east & ~odd & east_end, 1.0),
        ((origin >= 32) & (origin < 64) & ~odd & east_end, 1.0),
    )

    for copy in flat[2:]:
        copy.wait()
    low, high = TILE - 1, TILE + rows
    north_density = density_of(
        north[SALT * levels : (SALT + 1) * levels, :], north[NEAR * levels : (NEAR + 1) * levels, :]
    )
    for h in both:
        span = slice(h * LANES, (h + 1) * LANES)
        for k in range(levels):
            t_s[h, k, low : low + 1, :] = south[k : k + 1, span]
            g_s[h, k, low : low + 1, :] = south[levels + k : levels + k + 1, span]
            u_s[h, k, low : low + 1, :] = south[2 * levels + k : 2 * levels + k + 1, span]
            v_s[h, k, low : low + 1, :] = south[3 * levels + k : 3 * levels + k + 1, span]
            t_s[h, k, high : high + 1, :] = north[NEAR * levels + k : NEAR * levels + k + 1, span]
            t_s[h, k, high + 1 : high + 2, :] = north[FAR * levels + k : FAR * levels + k + 1, span]
            u_s[h, k, high : high + 1, :] = north[ZONAL * levels + k : ZONAL * levels + k + 1, span]
            v_s[h, k, high : high + 1, :] = north[MERID * levels + k : MERID * levels + k + 1, span]
        nf_s[h, rows : rows + 1, :] = north[5 * levels + WET_AT : 5 * levels + WET_AT + 1, span]
    for h in both:
        nf_s[h, 0:rows, :] = n_s[:, h * LANES : (h + 1) * LANES].astype(jnp.float32)

    lane = lax.broadcasted_iota(jnp.int32, (TILE, LANES), 1)
    is_last = lane == LANES - 1
    is_first = lane == 0
    from_rim_west = ((lane >= 32) & (lane < 64)) | ((lane >= 80) & (lane < 96)) | (lane >= 112)
    rim_source = jnp.where(
        lane < 32,
        lane + 2,
        jnp.where(
            lane < 64,
            lane - 32,
            jnp.where(
                lane < 80,
                lane - 64 + ZONAL_LANE + 1,
                jnp.where(
                    lane < 96,
                    lane - 80 + ZONAL_LANE,
                    jnp.where(lane < 112, lane - 96 + MERID_LANE + 1, lane - 112 + MERID_LANE),
                ),
            ),
        ),
    )
    lane2 = lax.broadcasted_iota(jnp.int32, (2 * TILE, LANES), 1)
    second = lax.broadcasted_iota(jnp.int32, (2 * TILE, LANES), 0) >= TILE
    level2 = jnp.where(lane2 < 64, lax.shift_right_logical(jnp.bitwise_and(lane2, 31), 1), jnp.bitwise_and(lane2, 15))
    level2 = level2 - jnp.where(second, 1, 0)
    for_density = (lane2 >= 32) & (lane2 < 64) & (jnp.bitwise_and(lane2, 1) == 0)
    kinds = ((lane2 < 64) & ~for_density, (lane2 >= 64) & (lane2 < 96), lane2 >= 96, for_density)
    for i, kind in enumerate(kinds):
        for p in range(levels // 2):
            mask_s[i, p] = jnp.where(kind & (level2 == 2 * p), 1.0, 0.0).astype(jnp.bfloat16)
    density_lane = (lane >= 32) & (lane < 64) & (jnp.bitwise_and(lane, 1) == 0)
    salt_source = jnp.bitwise_and(SALT_LANE + 1 + lax.shift_right_logical(lane - 32, 1), LANES - 1)
    heat_source = jnp.bitwise_and(lane - 30, LANES - 1)

    def to_lane(x, source, target):
        return pltpu.roll(x, (target - source) % LANES, 1)

    def east_of(x, halo, source):
        turned = [pltpu.roll(p, LANES - 1, 1) for p in x] + [to_lane(halo, source, LANES - 1)]
        return [jnp.where(is_last, turned[h + 1], turned[h]) for h in both]

    def west_of(x, halo, source):
        turned = [to_lane(halo, source, 0)] + [pltpu.roll(p, 1, 1) for p in x]
        return [jnp.where(is_first, turned[h], turned[h + 1]) for h in both]

    def two_parts(x):
        high_part = x.astype(jnp.bfloat16)
        return [high_part, (x - high_part.astype(jnp.float32)).astype(jnp.bfloat16)]

    def moved(parts, edges, i):
        y = jnp.dot(edges, rim_s[i], preferred_element_type=jnp.float32) if edges is not None else 0.0
        for p in parts:
            y = y + jnp.dot(p, move_s[i], preferred_element_type=jnp.float32)
        return y

    def prepare(r, coef_s):
        flat_at = pl.ds(pl.multiple_of(r * TILE, TILE), TILE)
        dt = step_duration
        wet = [nf_s[h, flat_at, :] for h in both]
        wet_e = east_of(wet, from_east[pl.ds(pl.multiple_of(r * TILE, TILE) + TILE, TILE), :], WET_LANE)
        for h in both:
            e1t, e2t, e1u, e2u, e1v, e2v = (e_s[i, flat_at, h * LANES : (h + 1) * LANES] for i in range(6))
            fu, fv = (f_s[i, flat_at, h * LANES : (h + 1) * LANES] for i in range(2))
            wet_n = nf_s[h, pl.ds(pl.multiple_of(r * TILE, TILE) + 1, TILE), :]
            iu1, iu2, iv1, iv2 = (inverse_of(x) for x in (e1u, e2u, e1v, e2v))

            def speeds(spin, along, across, a, b):
                c4, c5 = dt * viscosity * a * a, dt * viscosity * b * b
                return 0.25 * dt * spin, 0.125 * dt * across, 0.5 * dt * along, c4, c5, 2.0 * (c4 + c5)

            values = speeds(fu, iu1, iu2, iu1, iu2) + (0.5 * gravity * dt * iu1, diffusivity * e2u * iu1, e2u * (1.0 / 12.0))
            values += speeds(-fv, iv2, iv1, iv1, iv2) + (0.5 * gravity * dt * iv2, diffusivity * e1v * iv2, e1v * (1.0 / 12.0))
            values += (dt * inverse_of(e1t * e2t), jnp.minimum(wet[h], wet_e[h]), jnp.minimum(wet[h], wet_n))
            for i, value in enumerate(values):
                coef_s[i, h] = value

    def mix(r, kept, previous):
        mixed, uw_s, ve_s, den_s, coef_s = kept
        row = pl.multiple_of(r * TILE, TILE)
        prepare(r, coef_s)

        def turned(x, order):
            return jnp.take_along_axis(x, order, axis=1, mode="promise_in_bounds")

        east = from_east[pl.ds(row + TILE, TILE), :]
        x = jnp.where(from_rim_west, turned(from_west[pl.ds(row, TILE), :], rim_source), turned(east, rim_source))
        x = jnp.where(density_lane, density_of(turned(east, salt_source), turned(east, heat_source)), x)
        twice = [jnp.concatenate([p, p], axis=0) for p in two_parts(x)]

        def spread(kind):
            split = [[p * mask_s[kind, i] for i in range(levels // 2)] for p in twice]
            return jnp.concatenate([jnp.concatenate(q, axis=0) for q in split], axis=1)

        rim_t, rim_u, rim_v, rim_d = (spread(kind) for kind in range(4))

        def of(values):
            return two_parts(jnp.concatenate(values, axis=-1).reshape(levels * TILE, cols))

        def held_in(ref):
            return [ref[h, :, pl.ds(row + TILE, TILE), :] for h in both]

        def piece(y, i, h):
            count = levels * TILE
            return y[i * count : (i + 1) * count, h * LANES : (h + 1) * LANES].reshape(levels, TILE, LANES)

        d = [density_of(salt, heat) for salt, heat in zip(held_in(s_s), held_in(t_s))]
        for h in both:
            den_s[h, :, 0:TILE, :] = d[h]
            previous[3][h, :, TILE : TILE + 1, :] = d[h][:, 0:1, :]
        parts = [of(held_in(u_s)), of(held_in(v_s)), of(held_in(t_s)), of(d)]
        y = moved([jnp.concatenate(p, axis=0) for p in zip(*parts)], jnp.concatenate([rim_u, rim_v, rim_t, rim_d], axis=0), 2)
        for h in both:
            mixed[0, h] = piece(y, 0, h)
            ve_s[h, :, TILE : 2 * TILE, :] = piece(y, 1, h)
            mixed[3, h] = piece(y, 2, h)
            mixed[4, h] = piece(y, 3, h)
        y = moved(parts[2], rim_t, 0)
        for h in both:
            mixed[2, h] = piece(y, 0, h)
        y = moved([jnp.concatenate(p, axis=0) for p in zip(*parts[:2])], jnp.concatenate([rim_u, rim_v], axis=0), 1)
        for h in both:
            uw = piece(y, 0, h)
            uw_s[h, :, 0:TILE, :] = uw
            previous[1][h, :, TILE : TILE + 1, :] = uw[:, 0:1, :]
            mixed[1, h] = piece(y, 1, h)

    sub16 = lax.broadcasted_iota(jnp.int32, (levels, LANES), 0)
    lane16 = lax.broadcasted_iota(jnp.int32, (levels, LANES), 1)

    def corner(line, base):
        wide = jnp.broadcast_to(line, (levels, LANES))
        return jnp.sum(jnp.where(lane16 == sub16 + base, wide, 0.0), axis=1, keepdims=True)

    edge = moved(two_parts(south[3 * levels : 4 * levels, :]), None, 2)
    edge = [edge[:, h * LANES : (h + 1) * LANES] for h in both]
    edge[-1] = jnp.where(lane16 == LANES - 1, corner(from_east[TILE - 1 : TILE, :], MERID_LANE + 1), edge[-1])
    for h in both:
        for k in range(levels):
            ve_a[h, k, TILE - 1 : TILE, :] = edge[h][k : k + 1]

    def advance(r, kept, following):
        mixed, uw_s, ve_s, den_s, coef_s = kept
        for h in both:
            following[2][h, :, TILE - 1 : TILE, :] = ve_s[h, :, 2 * TILE - 1 : 2 * TILE, :]
        row = pl.multiple_of(r * TILE, TILE)
        flat_at = pl.ds(row, TILE)

        def rows_of(ref, k, shift):
            return [ref[h, k, pl.ds(row + TILE + shift, TILE), :] for h in both]

        east = from_east[pl.ds(row + TILE, TILE), :]
        west = from_west[flat_at, :]
        own = own_west[pl.ds(row + TILE, TILE), :]

        def span_of(x):
            up = jnp.where(lane < levels - 1, pltpu.roll(x, LANES - 1, 1), x)
            down = jnp.where(lane > 0, pltpu.roll(x, 1, 1), x)
            return up - down

        def heat_lane(x, offset):
            order = jnp.bitwise_and(2 * lane + offset, LANES - 1)
            return jnp.take_along_axis(x, order, axis=1, mode="promise_in_bounds")

        t_near, t_own = heat_lane(west, 1), heat_lane(own, 2)
        t_sum, t_far = t_near + t_own, heat_lane(west, 0) + heat_lane(own, 3)
        d_near = density_of(to_lane(west, SALT_LANE, 0), t_near)
        d_own = density_of(to_lane(own, SALT_LANE + 1, 0), t_own)
        e1 = jnp.broadcast_to(west[:, E1U_LANE : E1U_LANE + 1], (TILE, LANES))
        e2 = jnp.broadcast_to(west[:, E2U_LANE : E2U_LANE + 1], (TILE, LANES))
        wet_w = jnp.broadcast_to(jnp.minimum(west, own)[:, WET_LANE : WET_LANE + 1], (TILE, LANES))
        d_span = span_of(d_near + d_own)
        tilt = (d_own - d_near) * d_span * span_of(t_sum) * inverse_of(d_span * d_span + 16.0)
        flux_w = diffusivity * e2 * inverse_of(e1) * (t_own - t_near - tilt)
        flux_w = flux_w - e2 * (1.0 / 12.0) * to_lane(west, ZONAL_LANE, 0) * (7.0 * t_sum - t_far)
        flux_w = jnp.where(lane.astype(jnp.float32) < wet_w, flux_w, 0.0)

        def coefficient(i):
            return [coef_s[i, h] for h in both]

        store_at = lambda h: (flat_at, pl.ds(h * LANES, LANES))
        zero = jnp.zeros((TILE, LANES), jnp.float32)

        run = [zero for _ in both]

        def east_parts(k):
            t, u = rows_of(t_s, k, 0), rows_of(u_s, k, 0)
            d = [den_s[h, k, 0:TILE, :] for h in both]
            un, us = rows_of(u_s, k, 1), rows_of(u_s, k, -1)
            ue, wide, te, de = ([mixed[i, h, k] for h in both] for i in (0, 2, 3, 4))
            uw = [uw_s[h, k, 0:TILE, :] for h in both]
            v, vs = rows_of(v_s, k, 0), rows_of(v_s, k, -1)
            vbar = [
                (v[h] + vs[h]) + (ve_s[h, k, TILE : 2 * TILE, :] + ve_s[h, k, TILE - 1 : 2 * TILE - 1, :]) for h in both
            ]
            c1, c2, c3, c4, c5, c6, pu, iso_e, adv_e = (coefficient(i) for i in range(9))
            u_wet = coefficient(19)
            out = []
            for h in both:
                rise = de[h] - d[h]
                direct = iso_e[h] * (te[h] - t[h]) - adv_e[h] * u[h] * wide[h]
                out.append((t[h] + te[h], d[h] + de[h], direct, iso_e[h] * rise))
                press = run[h] + rise
                run[h] = press + rise
                du = (
                    vbar[h] * (c1[h] - c2[h] * (un[h] - us[h]))
                    - u[h] * (c3[h] * (ue[h] - uw[h]) + c6[h])
                    + c4[h] * (ue[h] + uw[h])
                    + c5[h] * (un[h] + us[h])
                    - pu[h] * press
                )
                uo_s[(k,) + store_at(h)] = u[h] + jnp.where(u_wet[h] > k, du, 0.0)
            return out

        def flux_of(below, here, above, open_face):
            t_span, d_span = above[0] - below[0], above[1] - below[1]
            flux = here[2] - here[3] * d_span * t_span * inverse_of(d_span * d_span + 16.0)
            return jnp.where(open_face, flux, 0.0)

        def east_finish(k, below, here, above):
            u_wet = coefficient(19)
            fe = [flux_of(below[h], here[h], above[h], u_wet[h] > k) for h in both]
            fw = west_of(fe, flux_w, k)
            for h in both:
                to_s[(k,) + store_at(h)] = fe[h] - fw[h]

        below = here = east_parts(0)
        for k in range(1, levels):
            above = east_parts(k)
            east_finish(k - 1, below, here, above)
            below, here = here, above
        east_finish(levels - 1, below, here, here)

        run = [zero for _ in both]

        def north_parts(k):
            t, tn, ts, tnn = (rows_of(t_s, k, i) for i in (0, 1, -1, 2))
            d, dn = [den_s[h, k, 0:TILE, :] for h in both], [den_s[h, k, 1 : TILE + 1, :] for h in both]
            v, vn, vs = (rows_of(v_s, k, i) for i in (0, 1, -1))
            ve, vw = [ve_s[h, k, TILE : 2 * TILE, :] for h in both], [mixed[1, h, k] for h in both]
            u, un = rows_of(u_s, k, 0), rows_of(u_s, k, 1)
            ubar = [(u[h] + un[h]) + (uw_s[h, k, 0:TILE, :] + uw_s[h, k, 1 : TILE + 1, :]) for h in both]
            c1, c2, c3, c4, c5, c6, pv, iso_n, adv_n = (coefficient(i) for i in range(9, 18))
            v_wet = coefficient(20)
            out = []
            for h in both:
                rise, pair = dn[h] - d[h], t[h] + tn[h]
                direct = iso_n[h] * (tn[h] - t[h]) - adv_n[h] * v[h] * (7.0 * pair - (ts[h] + tnn[h]))
                out.append((pair, d[h] + dn[h], direct, iso_n[h] * rise))
                press = run[h] + rise
                run[h] = press + rise
                dv = (
                    ubar[h] * (c1[h] - c2[h] * (ve[h] - vw[h]))
                    - v[h] * (c3[h] * (vn[h] - vs[h]) + c6[h])
                    + c4[h] * (ve[h] + vw[h])
                    + c5[h] * (vn[h] + vs[h])
                    - pv[h] * press
                )
                vo_s[(k,) + store_at(h)] = v[h] + jnp.where(v_wet[h] > k, dv, 0.0)
            return out

        def north_finish(k, below, here, above):
            area, v_wet, wet = coefficient(18), coefficient(20), [nf_s[h, flat_at, :] for h in both]
            for h in both:
                fn = flux_of(below[h], here[h], above[h], v_wet[h] > k)
                g_s[h, k, pl.ds(row + TILE, TILE), :] = fn
                fs = g_s[h, k, pl.ds(row + TILE - 1, TILE), :]
                at_h = (k,) + store_at(h)
                change = area[h] * (to_s[at_h] + (fn - fs))
                to_s[at_h] = t_s[h, k, pl.ds(row + TILE, TILE), :] + jnp.where(wet[h] > k, change, 0.0)

        below = here = north_parts(0)
        for k in range(1, levels):
            above = north_parts(k)
            north_finish(k - 1, below, here, above)
            below, here = here, above
        north_finish(levels - 1, below, here, here)

    set_a, set_b = (mixed_a, uw_a, ve_a, den_a, coef_a), (mixed_b, uw_b, ve_b, den_b, coef_b)
    flat[0].wait()
    flat[1].wait()
    loaded(1, 0)
    loaded(2, 1)
    mix(0, set_a, set_b)

    def two_tiles(i, carry):
        @pl.when(i + 2 <= pairs)
        def _():
            loaded(2, i + 2)

        mix(2 * i + 1, set_b, set_a)
        advance(2 * i, set_a, set_b)
        mix(2 * i + 2, set_a, set_b)
        advance(2 * i + 1, set_b, set_a)
        store(pl.multiple_of(i * 2 * TILE, 2 * TILE), 2)
        return carry

    lax.fori_loop(0, pairs, two_tiles, 0)
    edge = moved(two_parts(north[ZONAL * levels : (ZONAL + 1) * levels, :]), None, 1)
    edge = [edge[:, h * LANES : (h + 1) * LANES] for h in both]
    edge[0] = jnp.where(lane16 == 0, corner(from_west[rows : rows + 1, :], ZONAL_LANE), edge[0])
    for h in both:
        for k in range(levels):
            uw_a[h, k, TILE : TILE + 1, :] = edge[h][k : k + 1]
            den_a[h, k, TILE : TILE + 1, :] = north_density[k : k + 1, h * LANES : (h + 1) * LANES]
    advance(jnp.int32(2 * pairs), set_a, set_b)
    store(2 * pairs * TILE, 1)
    for i, (vmem, hbm) in enumerate(outs):
        pltpu.make_async_copy(vmem, hbm, out_sem.at[i]).wait()


def body(
    east_velocity,
    north_velocity,
    heat_anomaly,
    haline_anomaly,
    spacing_lengths,
    planetary_spin,
    ocean_layer_number,
    seam_partner_index,
):
    t, s, u, v = heat_anomaly, haline_anomaly, east_velocity, north_velocity
    levels, rows, cols = t.shape
    lats, lons = lax.axis_size("lat"), lax.axis_size("lon")
    f32 = jnp.float32
    top = rows // TILE - 1
    message = 5 * levels + 8

    low3 = pl.BlockSpec((levels, TILE, cols), lambda i: (0, 0, 0))
    high3 = pl.BlockSpec((levels, TILE, cols), lambda i: (0, top, 0))
    whole = pl.BlockSpec((message, cols), lambda i: (0, 0))
    count = spacing_lengths.shape[0]
    first, second = pl.pallas_call(
        row_pack,
        grid=(1,),
        in_specs=[low3, high3] * 4
        + [
            pl.BlockSpec((count, TILE, cols), lambda i: (0, 0, 0)),
            pl.BlockSpec((count, TILE, cols), lambda i: (0, top, 0)),
            pl.BlockSpec((TILE, cols), lambda i: (0, 0)),
            pl.BlockSpec((TILE, cols), lambda i: (top, 0)),
        ],
        out_specs=[whole, whole],
        out_shape=[jax.ShapeDtypeStruct((message, cols), f32)] * 2,
        name="row_pack",
    )(t, t, s, s, u, u, v, v, spacing_lengths, spacing_lengths, ocean_layer_number, ocean_layer_number)

    axes = ("lon", "lat")

    def place(lat, lon):
        return lon * lats + lat

    swap1, swap2 = [], []
    for lon in range(lons):
        for lat in range(0, lats, 2):
            swap1 += [(place(lat, lon), place(lat + 1, lon)), (place(lat + 1, lon), place(lat, lon))]
        for lat in range(1, lats - 1, 2):
            swap2 += [(place(lat, lon), place(lat + 1, lon)), (place(lat + 1, lon), place(lat, lon))]
        swap2.append((place(lats - 1, lon), place(lats - 1, lons - 1 - lon)))
        swap2.append((place(0, lon), place(0, lon)))
    got1 = lax.ppermute(first, axes, swap1)
    got2 = lax.ppermute(second, axes, swap2)

    group = 8
    slab = pl.BlockSpec((group, rows, cols), lambda i: (i, 0, 0))
    message_out = jax.ShapeDtypeStruct((rows + 8, LANES), f32)
    to_east, to_west = pl.pallas_call(
        lambda *refs: column_pack(group, *refs),
        grid=(levels // group,),
        in_specs=[slab] * 4
        + [pl.BlockSpec((2, rows, cols), lambda i: (1, 0, 0)), pl.BlockSpec((rows, cols), lambda i: (0, 0))],
        out_specs=[pl.BlockSpec((rows + 8, LANES), lambda i: (0, 0))] * 2,
        out_shape=[message_out] * 2,
        compiler_params=pltpu.CompilerParams(vmem_limit_bytes=64 * 2**20),
        cost_estimate=pl.CostEstimate(flops=20 * t.size, bytes_accessed=16 * t.size, transcendentals=0),
        name="column_pack",
    )(t, s, u, v, spacing_lengths, ocean_layer_number)

    seam = seam_partner_index.reshape(-1, LANES)
    fixed = lambda *shape: pl.BlockSpec(shape, lambda i: (0,) * len(shape))
    high_edge = pl.BlockSpec((8, LANES), lambda i: (rows // 8, 0))
    low_edge = pl.BlockSpec((8, LANES), lambda i: (0, 0))
    tight = pltpu.CompilerParams(vmem_limit_bytes=64 * 2**20)
    u_rows = pl.BlockSpec((levels, cols), lambda i: (ZONAL, 0))
    v_rows = pl.BlockSpec((levels, cols), lambda i: (MERID, 0))
    to_east, to_west = pl.pallas_call(
        corners,
        grid=(1,),
        in_specs=[u_rows, u_rows, v_rows, v_rows, fixed(*seam.shape), high_edge, low_edge],
        out_specs=[high_edge, low_edge],
        out_shape=[message_out] * 2,
        input_output_aliases={5: 0, 6: 1},
        compiler_params=tight,
        name="corners",
    )(got1, got2, got1, got2, seam, to_east, to_west)

    from_west = lax.ppermute(to_east, "lon", [(i, (i + 1) % lons) for i in range(lons)])
    from_east = lax.ppermute(to_west, "lon", [((i + 1) % lons, i) for i in range(lons)])

    north, south = pl.pallas_call(
        halo_rows,
        grid=(1,),
        in_specs=[fixed(message, cols)] * 4 + [fixed(*seam.shape)],
        out_specs=[fixed(message, cols), fixed(4 * levels, cols)],
        out_shape=[jax.ShapeDtypeStruct((message, cols), f32), jax.ShapeDtypeStruct((4 * levels, cols), f32)],
        compiler_params=tight,
        cost_estimate=pl.CostEstimate(flops=4 * t.size, bytes_accessed=2 * t.size, transcendentals=0),
        name="halo_rows",
    )(first, second, got1, got2, seam)

    halves = cols // LANES
    held = (halves, levels, rows + 2 * TILE, LANES)
    anywhere = pl.BlockSpec(memory_space=pl.ANY)
    out = jax.ShapeDtypeStruct((levels, rows, cols), f32)
    return pl.pallas_call(
        step_kernel,
        in_specs=[anywhere] * 12,
        out_specs=[anywhere] * 3,
        out_shape=[out] * 3,
        scratch_shapes=[
            pltpu.VMEM((message, cols), f32),
            pltpu.VMEM((4 * levels, cols), f32),
        ]
        + [pltpu.VMEM((rows + 8, LANES), f32)] * 3
        + [pltpu.VMEM(held, f32)] * 5
        + [
            pltpu.VMEM((5, halves, levels, TILE, LANES), f32),
            pltpu.VMEM((halves, levels, 2 * TILE, LANES), f32),
            pltpu.VMEM((halves, levels, 2 * TILE, LANES), f32),
            pltpu.VMEM((halves, levels, 2 * TILE, LANES), f32),
            pltpu.VMEM((21, halves, TILE, LANES), f32),
        ]
        * 2
        + [
            pltpu.VMEM(spacing_lengths.shape, f32),
            pltpu.VMEM(planetary_spin.shape, f32),
            pltpu.VMEM((rows, cols), jnp.int32),
            pltpu.VMEM((halves, rows + TILE, LANES), f32),
        ]
        + [pltpu.VMEM((levels, rows, cols), f32)] * 3
        + [
            pltpu.VMEM((3, cols, cols), jnp.bfloat16),
            pltpu.VMEM((3, cols, cols), jnp.bfloat16),
            pltpu.VMEM((4, levels // 2, 2 * TILE, LANES), jnp.bfloat16),
            pltpu.SemaphoreType.DMA((rows // TILE // 2 + 1,)),
            pltpu.SemaphoreType.DMA((8,)),
            pltpu.SemaphoreType.DMA((3,)),
        ],
        compiler_params=pltpu.CompilerParams(vmem_limit_bytes=60 * 2**20),
        name="ocean_step",
    )(t, s, u, v, spacing_lengths, planetary_spin, ocean_layer_number, north, south, to_west, from_east, from_west)


def solution(mesh):
    in_specs = (
        P(None, "lat", "lon"),
        P(None, "lat", "lon"),
        P(None, "lat", "lon"),
        P(None, "lat", "lon"),
        P(None, "lat", "lon"),
        P(None, "lat", "lon"),
        P("lat", "lon"),
        P(),
    )
    out_specs = (P(None, "lat", "lon"), P(None, "lat", "lon"), P(None, "lat", "lon"))
    return jax.shard_map(body, mesh=mesh, in_specs=in_specs, out_specs=out_specs, check_vma=False)
```

```python
import jax
import jax.numpy as jnp
from jax import lax
from jax.experimental import pallas as pl
from jax.experimental.pallas import tpu as pltpu
from jax.sharding import PartitionSpec as P

LANES = 128
TILE = 8

step_duration = 0.25
viscosity = 0.05
diffusivity = 0.3
expansion_coefficient = 0.6
haline_contraction = 0.8
gravity = 0.1

NEAR, FAR, SALT, ZONAL, MERID = 0, 1, 2, 3, 4
E1V_AT, E2V_AT, WET_AT = 0, 1, 2
HEAT_LANE, SALT_LANE, ZONAL_LANE, MERID_LANE = 0, 40, 56, 72
E1U_LANE, E2U_LANE, WET_LANE = 96, 97, 98


def density_of(salinity, heat):
    return haline_contraction * salinity - expansion_coefficient * heat


def inverse_of(x):
    return pltpu.reciprocal(x, approx=True)


def row_pack(t_lo, t_hi, s_lo, s_hi, u_lo, u_hi, v_lo, v_hi, e_lo, e_hi, n_lo, n_hi, first, second):
    levels = t_lo.shape[0]
    even = lax.rem(lax.axis_index("lat"), 2) == 0

    def put(slot, high, low):
        rows = pl.ds(slot * levels, levels)
        first[rows] = jnp.where(even, high, low)
        second[rows] = jnp.where(even, low, high)

    near_hi, near_lo = t_hi[:, 7, :], t_lo[:, 0, :]
    put(NEAR, near_hi, near_lo)
    put(FAR, t_hi[:, 6, :], t_lo[:, 1, :])
    put(SALT, s_hi[:, 7, :], s_lo[:, 0, :])
    put(ZONAL, u_hi[:, 7, :], u_lo[:, 0, :])
    put(MERID, v_hi[:, 7, :], v_lo[:, 0, :])
    base = 5 * levels
    high = jnp.concatenate([e_hi[4, 7:8], e_hi[5, 7:8], n_hi[7:8].astype(jnp.float32), jnp.zeros((5, e_hi.shape[2]), jnp.float32)], axis=0)
    low = jnp.concatenate([e_lo[4, 0:1], e_lo[5, 0:1], n_lo[0:1].astype(jnp.float32), jnp.zeros((5, e_lo.shape[2]), jnp.float32)], axis=0)
    first[base : base + 8] = jnp.where(even, high, low)
    second[base : base + 8] = jnp.where(even, low, high)


def vertical_span(x):
    return jnp.concatenate([x[1:], x[-1:]], axis=0) - jnp.concatenate([x[:1], x[:-1]], axis=0)


def corners(u1, u2, v1, v2, seam, east_in, west_in, east_out, west_out):
    levels, cols = u1.shape
    lat, lon = lax.axis_index("lat"), lax.axis_index("lon")
    lats, lons = lax.axis_size("lat"), lax.axis_size("lon")
    even = lax.rem(lat, 2) == 0
    is_top = lat == lats - 1
    per = cols // LANES
    pick = seam[pl.ds(lon * per + per - 1, 1), LANES - 1 : LANES] - (lons - 1 - lon) * cols
    pick = jnp.where(is_top, pick, cols - 1)
    u = jnp.where(even, u1[...], u2[...])
    u = jnp.where(is_top, -u, u)
    here = lax.broadcasted_iota(jnp.int32, (levels, cols), 1) == pick
    u = jnp.sum(jnp.where(here, u, 0.0), axis=1, keepdims=True)
    v = jnp.where(lat == 0, 0.0, jnp.where(even, v2[:, 0:1], v1[:, 0:1]))
    sub16 = lax.broadcasted_iota(jnp.int32, (levels, LANES), 0)
    lane16 = lax.broadcasted_iota(jnp.int32, (levels, LANES), 1)

    def line(x, base):
        return jnp.sum(jnp.where(lane16 == sub16 + base, x, 0.0), axis=0, keepdims=True)

    east_out[...] = jnp.broadcast_to(line(u, ZONAL_LANE), (8, LANES))
    west_out[...] = jnp.broadcast_to(line(v, MERID_LANE + 1), (8, LANES))


def halo_rows(mine1, mine2, got1, got2, seam, north_out, south_out):
    levels = (mine1.shape[0] - 8) // 5
    cols = mine1.shape[1]
    lat, lon = lax.axis_index("lat"), lax.axis_index("lon")
    lats, lons = lax.axis_size("lat"), lax.axis_size("lon")
    even = lax.rem(lat, 2) == 0
    is_top = lat == lats - 1
    is_bottom = lat == 0
    north_rows = got1.shape[0]
    for h in range(cols // LANES):
        span = slice(h * LANES, (h + 1) * LANES)
        pick = seam[pl.ds(lon * (cols // LANES) + h, 1), :] - (lons - 1 - lon) * cols
        pick = jnp.where(is_top, pick, lax.broadcasted_iota(jnp.int32, (1, LANES), 1) + h * LANES)
        pick = jnp.broadcast_to(pick, (TILE, LANES))
        inner = jnp.bitwise_and(pick, LANES - 1)
        for row in range(0, north_rows, TILE):
            total = None
            for g in range(cols // LANES):
                piece = slice(g * LANES, (g + 1) * LANES)
                source = jnp.where(even, got1[row : row + TILE, piece], got2[row : row + TILE, piece])
                taken = jnp.take_along_axis(source, inner, axis=1, mode="promise_in_bounds")
                taken = jnp.where(pick >= g * LANES, taken, 0.0) if g == 0 else taken
                total = taken if total is None else jnp.where(pick >= g * LANES, taken, total)
            if ZONAL * levels <= row < (MERID + 1) * levels:
                total = jnp.where(is_top, -total, total)
            north_out[row : row + TILE, span] = total
    def south(slot):
        part = slice(slot * levels, (slot + 1) * levels)
        return jnp.where(is_bottom, 0.0, jnp.where(even, got2[part], got1[part]))

    def own(slot):
        part = slice(slot * levels, (slot + 1) * levels)
        return jnp.where(even, mine2[part], mine1[part])

    tail = slice(5 * levels, 5 * levels + 8)
    coef = jnp.where(even, got2[tail], got1[tail])
    own_wet = jnp.where(even, mine2[tail], mine1[tail])[WET_AT : WET_AT + 1]
    e1v = jnp.where(is_bottom, 1.0, coef[E1V_AT : E1V_AT + 1])
    e2v = jnp.where(is_bottom, 1.0, coef[E2V_AT : E2V_AT + 1])
    wet = jnp.where(is_bottom, 0.0, coef[WET_AT : WET_AT + 1])
    t_near, t_far, v_near = south(NEAR), south(FAR), south(MERID)
    t_own, t_next = own(NEAR), own(FAR)
    d_near, d_own = density_of(south(SALT), t_near), density_of(own(SALT), t_own)
    t_sum = t_near + t_own
    adv = (e1v / 12.0) * v_near * (7.0 * t_sum - (t_far + t_next))
    d_span = vertical_span(d_near + d_own)
    tilt = (d_own - d_near) * d_span * vertical_span(t_sum) / (d_span * d_span + 16.0)
    iso = (diffusivity * e1v / e2v) * (t_own - t_near - tilt)
    level = lax.broadcasted_iota(jnp.int32, (levels, cols), 0).astype(jnp.float32)
    flux = jnp.where(level < jnp.minimum(wet, own_wet), iso - adv, 0.0)
    south_out[0:levels] = t_near
    south_out[levels : 2 * levels] = flux
    south_out[2 * levels : 3 * levels] = south(ZONAL)
    south_out[3 * levels : 4 * levels] = v_near


def column_pack(group, t, s, u, v, e, n, east_out, west_out):
    rows, cols = t.shape[1:]
    step = pl.program_id(0)
    lane = lax.broadcasted_iota(jnp.int32, (rows, LANES), 1)
    pair = lax.shift_right_logical(lane, 1)
    first = slice(0, LANES)
    last = slice(cols - LANES, cols)

    @pl.when(step == 0)
    def _():
        n_f = n[...].astype(jnp.float32)
        hi = jnp.where(lane == E1U_LANE, pltpu.roll(e[0, :, last], (E1U_LANE + 1) % LANES, 1), 0.0)
        hi = jnp.where(lane == E2U_LANE, pltpu.roll(e[1, :, last], (E2U_LANE + 1) % LANES, 1), hi)
        east_out[0:rows] = jnp.where(lane == WET_LANE, pltpu.roll(n_f[:, last], (WET_LANE + 1) % LANES, 1), hi)
        west_out[8 : rows + 8] = jnp.where(lane == WET_LANE, pltpu.roll(n_f[:, first], WET_LANE, 1), 0.0)
        east_out[rows : rows + 8] = jnp.zeros((8, LANES), jnp.float32)
        west_out[0:8] = jnp.zeros((8, LANES), jnp.float32)

    hi = east_out[0:rows]
    lo = west_out[8 : rows + 8]
    for kk in range(group):
        k = step * group + kk
        for field, base in ((t, HEAT_LANE), (s, SALT_LANE), (u, ZONAL_LANE), (v, MERID_LANE)):
            ends = jnp.where(lane < LANES // 2, field[kk, :, first], field[kk, :, last])
            if field is t:
                ends = pltpu.roll(ends, 2 * k + 2, 1)
                hi = jnp.where(pair == k, ends, hi)
                lo = jnp.where(pair == k + 1, ends, lo)
            else:
                ends = pltpu.roll(ends, base + 1 + k, 1)
                hi = jnp.where(lane == base + k, ends, hi)
                lo = jnp.where(lane == base + 1 + k, ends, lo)
    east_out[0:rows] = hi
    west_out[8 : rows + 8] = lo


def step_kernel(
    t_hbm, s_hbm, u_hbm, v_hbm, e_hbm, f_hbm, n_hbm, north_hbm, south_hbm, own_hbm, from_east_hbm, from_west_hbm,
    u_out, v_out, t_out,
    north, south, own_west, from_east, from_west, t_s, s_s, u_s, v_s, d_s, g_s, mixed_a, uw_a, ve_a, mixed_b, uw_b, ve_b, e_s, f_s, n_s, nf_s, uo_s, vo_s, to_s, move_s, rim_s, mask_s, coef_s,
    in_sem, flat_sem, out_sem,
):
    levels, rows, cols = t_hbm.shape
    tiles = rows // TILE
    halves = cols // LANES
    both = range(halves)
    pairs = (tiles - 1) // 2
    assert tiles == 2 * pairs + 1

    fields = ((t_hbm, t_s), (s_hbm, s_s), (u_hbm, u_s), (v_hbm, v_s))

    def load(first, count, unit):
        span = pl.ds(first * TILE, count * TILE)
        held = pl.ds(first * TILE + TILE, count * TILE)
        for hbm, vmem in fields:
            for h in both:
                pltpu.make_async_copy(
                    hbm.at[:, span, pl.ds(h * LANES, LANES)], vmem.at[h, :, held, :], in_sem.at[unit]
                ).start()

    def loaded(count, unit):
        span = pl.ds(0, len(fields) * halves * count * TILE)
        pltpu.make_async_copy(t_hbm.at[:, span, pl.ds(0, LANES)], t_s.at[0, :, span, :], in_sem.at[unit]).wait()

    outs = ((uo_s, u_out), (vo_s, v_out), (to_s, t_out))

    def store(row, count):
        span = pl.ds(row, count * TILE)
        for i, (vmem, hbm) in enumerate(outs):
            pltpu.make_async_copy(vmem.at[:, span, :], hbm.at[:, span, :], out_sem.at[i]).start()

    flat = [
        pltpu.make_async_copy(hbm, vmem, flat_sem.at[i])
        for i, (hbm, vmem) in enumerate(
            (
                (e_hbm, e_s),
                (f_hbm, f_s),
                (n_hbm, n_s),
                (north_hbm, north),
                (south_hbm, south),
                (own_hbm, own_west),
                (from_east_hbm, from_east),
                (from_west_hbm, from_west),
            )
        )
    ]
    for copy in flat[2:]:
        copy.start()
    load(0, 1, 0)
    for copy in flat[:2]:
        copy.start()
    load(1, 2, 1)
    for unit in range(2, pairs + 1):
        load(2 * unit - 1, 2, unit)

    source = lax.broadcasted_iota(jnp.int32, (cols, cols), 0)
    target = lax.broadcasted_iota(jnp.int32, (cols, cols), 1)
    apart = source - target

    def matrix(*terms):
        total = jnp.zeros((cols, cols), jnp.float32)
        for where, value in terms:
            total = jnp.where(where, value, total)
        return total.astype(jnp.bfloat16)

    at = [apart == i for i in range(-1, 3)]
    move_s[0] = matrix((at[0], -1.0), (at[1], 7.0), (at[2], 7.0), (at[3], -1.0))
    move_s[1] = matrix((at[0], 1.0))
    move_s[2] = matrix((at[2], 1.0))
    origin = jnp.bitwise_and(source, LANES - 1)
    odd = jnp.bitwise_and(origin, 1) == 1
    west_end, east_end = target == 0, target == cols - 1
    heat_east, heat_west = origin < 32, (origin >= 32) & (origin < 64) & odd
    rim_s[0] = matrix(
        (heat_east & ~odd & (target == cols - 2), -1.0),
        (heat_east & ~odd & east_end, 7.0),
        (heat_east & odd & east_end, -1.0),
        (heat_west & west_end, -1.0),
    )
    western = jnp.bitwise_and(origin, 16) == 16
    rim_s[1] = matrix(((origin >= 64) & western & west_end, 1.0))
    rim_s[2] = matrix(
        ((origin >= 64) & ~western & east_end, 1.0),
        (heat_east & ~odd & east_end, 1.0),
        ((origin >= 32) & (origin < 64) & ~odd & east_end, 1.0),
    )

    for copy in flat[2:]:
        copy.wait()
    low, high = TILE - 1, TILE + rows
    north_density = density_of(
        north[SALT * levels : (SALT + 1) * levels, :], north[NEAR * levels : (NEAR + 1) * levels, :]
    )
    for h in both:
        span = slice(h * LANES, (h + 1) * LANES)
        for k in range(levels):
            t_s[h, k, low : low + 1, :] = south[k : k + 1, span]
            g_s[h, k, low : low + 1, :] = south[levels + k : levels + k + 1, span]
            u_s[h, k, low : low + 1, :] = south[2 * levels + k : 2 * levels + k + 1, span]
            v_s[h, k, low : low + 1, :] = south[3 * levels + k : 3 * levels + k + 1, span]
            t_s[h, k, high : high + 1, :] = north[NEAR * levels + k : NEAR * levels + k + 1, span]
            t_s[h, k, high + 1 : high + 2, :] = north[FAR * levels + k : FAR * levels + k + 1, span]
            d_s[h, k, high : high + 1, :] = north_density[k : k + 1, span]
            u_s[h, k, high : high + 1, :] = north[ZONAL * levels + k : ZONAL * levels + k + 1, span]
            v_s[h, k, high : high + 1, :] = north[MERID * levels + k : MERID * levels + k + 1, span]
        nf_s[h, rows : rows + 1, :] = north[5 * levels + WET_AT : 5 * levels + WET_AT + 1, span]
    for h in both:
        nf_s[h, 0:rows, :] = n_s[:, h * LANES : (h + 1) * LANES].astype(jnp.float32)

    lane = lax.broadcasted_iota(jnp.int32, (TILE, LANES), 1)
    is_last = lane == LANES - 1
    is_first = lane == 0
    from_rim_west = ((lane >= 32) & (lane < 64)) | ((lane >= 80) & (lane < 96)) | (lane >= 112)
    rim_source = jnp.where(
        lane < 32,
        lane + 2,
        jnp.where(
            lane < 64,
            lane - 32,
            jnp.where(
                lane < 80,
                lane - 64 + ZONAL_LANE + 1,
                jnp.where(
                    lane < 96,
                    lane - 80 + ZONAL_LANE,
                    jnp.where(lane < 112, lane - 96 + MERID_LANE + 1, lane - 112 + MERID_LANE),
                ),
            ),
        ),
    )
    lane2 = lax.broadcasted_iota(jnp.int32, (2 * TILE, LANES), 1)
    second = lax.broadcasted_iota(jnp.int32, (2 * TILE, LANES), 0) >= TILE
    level2 = jnp.where(lane2 < 64, lax.shift_right_logical(jnp.bitwise_and(lane2, 31), 1), jnp.bitwise_and(lane2, 15))
    level2 = level2 - jnp.where(second, 1, 0)
    for_density = (lane2 >= 32) & (lane2 < 64) & (jnp.bitwise_and(lane2, 1) == 0)
    kinds = ((lane2 < 64) & ~for_density, (lane2 >= 64) & (lane2 < 96), lane2 >= 96, for_density)
    for i, kind in enumerate(kinds):
        for p in range(levels // 2):
            mask_s[i, p] = jnp.where(kind & (level2 == 2 * p), 1.0, 0.0).astype(jnp.bfloat16)
    density_lane = (lane >= 32) & (lane < 64) & (jnp.bitwise_and(lane, 1) == 0)
    salt_source = jnp.bitwise_and(SALT_LANE + 1 + lax.shift_right_logical(lane - 32, 1), LANES - 1)
    heat_source = jnp.bitwise_and(lane - 30, LANES - 1)

    def to_lane(x, source, target):
        return pltpu.roll(x, (target - source) % LANES, 1)

    def east_of(x, halo, source):
        turned = [pltpu.roll(p, LANES - 1, 1) for p in x] + [to_lane(halo, source, LANES - 1)]
        return [jnp.where(is_last, turned[h + 1], turned[h]) for h in both]

    def west_of(x, halo, source):
        turned = [to_lane(halo, source, 0)] + [pltpu.roll(p, 1, 1) for p in x]
        return [jnp.where(is_first, turned[h], turned[h + 1]) for h in both]

    def two_parts(x):
        high_part = x.astype(jnp.bfloat16)
        return [high_part, (x - high_part.astype(jnp.float32)).astype(jnp.bfloat16)]

    def moved(parts, edges, i):
        y = jnp.dot(edges, rim_s[i], preferred_element_type=jnp.float32) if edges is not None else 0.0
        for p in parts:
            y = y + jnp.dot(p, move_s[i], preferred_element_type=jnp.float32)
        return y

    def prepare(r):
        flat_at = pl.ds(pl.multiple_of(r * TILE, TILE), TILE)
        dt = step_duration
        wet = [nf_s[h, flat_at, :] for h in both]
        wet_e = east_of(wet, from_east[pl.ds(pl.multiple_of(r * TILE, TILE) + TILE, TILE), :], WET_LANE)
        for h in both:
            e1t, e2t, e1u, e2u, e1v, e2v = (e_s[i, flat_at, h * LANES : (h + 1) * LANES] for i in range(6))
            fu, fv = (f_s[i, flat_at, h * LANES : (h + 1) * LANES] for i in range(2))
            wet_n = nf_s[h, pl.ds(pl.multiple_of(r * TILE, TILE) + 1, TILE), :]
            iu1, iu2, iv1, iv2 = (inverse_of(x) for x in (e1u, e2u, e1v, e2v))

            def speeds(spin, along, across, a, b):
                c4, c5 = dt * viscosity * a * a, dt * viscosity * b * b
                return 0.25 * dt * spin, 0.125 * dt * across, 0.5 * dt * along, c4, c5, 2.0 * (c4 + c5)

            values = speeds(fu, iu1, iu2, iu1, iu2) + (0.5 * gravity * dt * iu1, diffusivity * e2u * iu1, e2u * (1.0 / 12.0))
            values += speeds(-fv, iv2, iv1, iv1, iv2) + (0.5 * gravity * dt * iv2, diffusivity * e1v * iv2, e1v * (1.0 / 12.0))
            values += (dt * inverse_of(e1t * e2t), jnp.minimum(wet[h], wet_e[h]), jnp.minimum(wet[h], wet_n))
            for i, value in enumerate(values):
                coef_s[i, h, flat_at, :] = value

    def mix(r, kept, previous):
        mixed, uw_s, ve_s = kept
        row = pl.multiple_of(r * TILE, TILE)
        prepare(r)

        def turned(x, order):
            return jnp.take_along_axis(x, order, axis=1, mode="promise_in_bounds")

        east = from_east[pl.ds(row + TILE, TILE), :]
        x = jnp.where(from_rim_west, turned(from_west[pl.ds(row, TILE), :], rim_source), turned(east, rim_source))
        x = jnp.where(density_lane, density_of(turned(east, salt_source), turned(east, heat_source)), x)
        twice = [jnp.concatenate([p, p], axis=0) for p in two_parts(x)]

        def spread(kind):
            split = [[p * mask_s[kind, i] for i in range(levels // 2)] for p in twice]
            return jnp.concatenate([jnp.concatenate(q, axis=0) for q in split], axis=1)

        rim_t, rim_u, rim_v, rim_d = (spread(kind) for kind in range(4))

        def of(values):
            return two_parts(jnp.concatenate(values, axis=-1).reshape(levels * TILE, cols))

        def held_in(ref):
            return [ref[h, :, pl.ds(row + TILE, TILE), :] for h in both]

        def piece(y, i, h):
            count = levels * TILE
            return y[i * count : (i + 1) * count, h * LANES : (h + 1) * LANES].reshape(levels, TILE, LANES)

        d = [density_of(salt, heat) for salt, heat in zip(held_in(s_s), held_in(t_s))]
        for h in both:
            d_s[h, :, pl.ds(row + TILE, TILE), :] = d[h]
        parts = [of(held_in(u_s)), of(held_in(v_s)), of(held_in(t_s)), of(d)]
        y = moved([jnp.concatenate(p, axis=0) for p in zip(*parts)], jnp.concatenate([rim_u, rim_v, rim_t, rim_d], axis=0), 2)
        for h in both:
            mixed[0, h] = piece(y, 0, h)
            ve_s[h, :, TILE : 2 * TILE, :] = piece(y, 1, h)
            mixed[3, h] = piece(y, 2, h)
            mixed[4, h] = piece(y, 3, h)
        y = moved(parts[2], rim_t, 0)
        for h in both:
            mixed[2, h] = piece(y, 0, h)
        y = moved([jnp.concatenate(p, axis=0) for p in zip(*parts[:2])], jnp.concatenate([rim_u, rim_v], axis=0), 1)
        for h in both:
            uw = piece(y, 0, h)
            uw_s[h, :, 0:TILE, :] = uw
            previous[1][h, :, TILE : TILE + 1, :] = uw[:, 0:1, :]
            mixed[1, h] = piece(y, 1, h)

    sub16 = lax.broadcasted_iota(jnp.int32, (levels, LANES), 0)
    lane16 = lax.broadcasted_iota(jnp.int32, (levels, LANES), 1)

    def corner(line, base):
        wide = jnp.broadcast_to(line, (levels, LANES))
        return jnp.sum(jnp.where(lane16 == sub16 + base, wide, 0.0), axis=1, keepdims=True)

    edge = moved(two_parts(south[3 * levels : 4 * levels, :]), None, 2)
    edge = [edge[:, h * LANES : (h + 1) * LANES] for h in both]
    edge[-1] = jnp.where(lane16 == LANES - 1, corner(from_east[TILE - 1 : TILE, :], MERID_LANE + 1), edge[-1])
    for h in both:
        for k in range(levels):
            ve_a[h, k, TILE - 1 : TILE, :] = edge[h][k : k + 1]

    def advance(r, kept, following):
        mixed, uw_s, ve_s = kept
        for h in both:
            following[2][h, :, TILE - 1 : TILE, :] = ve_s[h, :, 2 * TILE - 1 : 2 * TILE, :]
        row = pl.multiple_of(r * TILE, TILE)
        flat_at = pl.ds(row, TILE)

        def rows_of(ref, k, shift):
            return [ref[h, k, pl.ds(row + TILE + shift, TILE), :] for h in both]

        east = from_east[pl.ds(row + TILE, TILE), :]
        west = from_west[flat_at, :]
        own = own_west[pl.ds(row + TILE, TILE), :]

        def span_of(x):
            up = jnp.where(lane < levels - 1, pltpu.roll(x, LANES - 1, 1), x)
            down = jnp.where(lane > 0, pltpu.roll(x, 1, 1), x)
            return up - down

        def heat_lane(x, offset):
            order = jnp.bitwise_and(2 * lane + offset, LANES - 1)
            return jnp.take_along_axis(x, order, axis=1, mode="promise_in_bounds")

        t_near, t_own = heat_lane(west, 1), heat_lane(own, 2)
        t_sum, t_far = t_near + t_own, heat_lane(west, 0) + heat_lane(own, 3)
        d_near = density_of(to_lane(west, SALT_LANE, 0), t_near)
        d_own = density_of(to_lane(own, SALT_LANE + 1, 0), t_own)
        e1 = jnp.broadcast_to(west[:, E1U_LANE : E1U_LANE + 1], (TILE, LANES))
        e2 = jnp.broadcast_to(west[:, E2U_LANE : E2U_LANE + 1], (TILE, LANES))
        wet_w = jnp.broadcast_to(jnp.minimum(west, own)[:, WET_LANE : WET_LANE + 1], (TILE, LANES))
        d_span = span_of(d_near + d_own)
        tilt = (d_own - d_near) * d_span * span_of(t_sum) * inverse_of(d_span * d_span + 16.0)
        flux_w = diffusivity * e2 * inverse_of(e1) * (t_own - t_near - tilt)
        flux_w = flux_w - e2 * (1.0 / 12.0) * to_lane(west, ZONAL_LANE, 0) * (7.0 * t_sum - t_far)
        flux_w = jnp.where(lane.astype(jnp.float32) < wet_w, flux_w, 0.0)

        def coefficient(i):
            return [coef_s[i, h, flat_at, :] for h in both]

        store_at = lambda h: (flat_at, pl.ds(h * LANES, LANES))
        zero = jnp.zeros((TILE, LANES), jnp.float32)

        run = [zero for _ in both]

        def east_parts(k):
            t, d, u = rows_of(t_s, k, 0), rows_of(d_s, k, 0), rows_of(u_s, k, 0)
            un, us = rows_of(u_s, k, 1), rows_of(u_s, k, -1)
            ue, wide, te, de = ([mixed[i, h, k] for h in both] for i in (0, 2, 3, 4))
            uw = [uw_s[h, k, 0:TILE, :] for h in both]
            v, vs = rows_of(v_s, k, 0), rows_of(v_s, k, -1)
            vbar = [
                (v[h] + vs[h]) + (ve_s[h, k, TILE : 2 * TILE, :] + ve_s[h, k, TILE - 1 : 2 * TILE - 1, :]) for h in both
            ]
            c1, c2, c3, c4, c5, c6, pu, iso_e, adv_e = (coefficient(i) for i in range(9))
            u_wet = coefficient(19)
            out = []
            for h in both:
                rise = de[h] - d[h]
                direct = iso_e[h] * (te[h] - t[h]) - adv_e[h] * u[h] * wide[h]
                out.append((t[h] + te[h], d[h] + de[h], direct, iso_e[h] * rise))
                press = run[h] + rise
                run[h] = press + rise
                du = (
                    vbar[h] * (c1[h] - c2[h] * (un[h] - us[h]))
                    - u[h] * (c3[h] * (ue[h] - uw[h]) + c6[h])
                    + c4[h] * (ue[h] + uw[h])
                    + c5[h] * (un[h] + us[h])
                    - pu[h] * press
                )
                uo_s[(k,) + store_at(h)] = u[h] + jnp.where(u_wet[h] > k, du, 0.0)
            return out

        def flux_of(below, here, above, open_face):
            t_span, d_span = above[0] - below[0], above[1] - below[1]
            flux = here[2] - here[3] * d_span * t_span * inverse_of(d_span * d_span + 16.0)
            return jnp.where(open_face, flux, 0.0)

        def east_finish(k, below, here, above):
            u_wet = coefficient(19)
            fe = [flux_of(below[h], here[h], above[h], u_wet[h] > k) for h in both]
            fw = west_of(fe, flux_w, k)
            for h in both:
                to_s[(k,) + store_at(h)] = fe[h] - fw[h]

        below = here = east_parts(0)
        for k in range(1, levels):
            above = east_parts(k)
            east_finish(k - 1, below, here, above)
            below, here = here, above
        east_finish(levels - 1, below, here, here)

        run = [zero for _ in both]

        def north_parts(k):
            t, tn, ts, tnn = (rows_of(t_s, k, i) for i in (0, 1, -1, 2))
            d, dn = rows_of(d_s, k, 0), rows_of(d_s, k, 1)
            v, vn, vs = (rows_of(v_s, k, i) for i in (0, 1, -1))
            ve, vw = [ve_s[h, k, TILE : 2 * TILE, :] for h in both], [mixed[1, h, k] for h in both]
            u, un = rows_of(u_s, k, 0), rows_of(u_s, k, 1)
            ubar = [(u[h] + un[h]) + (uw_s[h, k, 0:TILE, :] + uw_s[h, k, 1 : TILE + 1, :]) for h in both]
            c1, c2, c3, c4, c5, c6, pv, iso_n, adv_n = (coefficient(i) for i in range(9, 18))
            v_wet = coefficient(20)
            out = []
            for h in both:
                rise, pair = dn[h] - d[h], t[h] + tn[h]
                direct = iso_n[h] * (tn[h] - t[h]) - adv_n[h] * v[h] * (7.0 * pair - (ts[h] + tnn[h]))
                out.append((pair, d[h] + dn[h], direct, iso_n[h] * rise))
                press = run[h] + rise
                run[h] = press + rise
                dv = (
                    ubar[h] * (c1[h] - c2[h] * (ve[h] - vw[h]))
                    - v[h] * (c3[h] * (vn[h] - vs[h]) + c6[h])
                    + c4[h] * (ve[h] + vw[h])
                    + c5[h] * (vn[h] + vs[h])
                    - pv[h] * press
                )
                vo_s[(k,) + store_at(h)] = v[h] + jnp.where(v_wet[h] > k, dv, 0.0)
            return out

        def north_finish(k, below, here, above):
            area, v_wet, wet = coefficient(18), coefficient(20), [nf_s[h, flat_at, :] for h in both]
            for h in both:
                fn = flux_of(below[h], here[h], above[h], v_wet[h] > k)
                g_s[h, k, pl.ds(row + TILE, TILE), :] = fn
                fs = g_s[h, k, pl.ds(row + TILE - 1, TILE), :]
                at_h = (k,) + store_at(h)
                change = area[h] * (to_s[at_h] + (fn - fs))
                to_s[at_h] = t_s[h, k, pl.ds(row + TILE, TILE), :] + jnp.where(wet[h] > k, change, 0.0)

        below = here = north_parts(0)
        for k in range(1, levels):
            above = north_parts(k)
            north_finish(k - 1, below, here, above)
            below, here = here, above
        north_finish(levels - 1, below, here, here)

    set_a, set_b = (mixed_a, uw_a, ve_a), (mixed_b, uw_b, ve_b)
    flat[0].wait()
    flat[1].wait()
    loaded(1, 0)
    loaded(2, 1)
    mix(0, set_a, set_b)

    def two_tiles(i, carry):
        @pl.when(i + 2 <= pairs)
        def _():
            loaded(2, i + 2)

        mix(2 * i + 1, set_b, set_a)
        advance(2 * i, set_a, set_b)
        mix(2 * i + 2, set_a, set_b)
        advance(2 * i + 1, set_b, set_a)
        store(pl.multiple_of(i * 2 * TILE, 2 * TILE), 2)
        return carry

    lax.fori_loop(0, pairs, two_tiles, 0)
    edge = moved(two_parts(north[ZONAL * levels : (ZONAL + 1) * levels, :]), None, 1)
    edge = [edge[:, h * LANES : (h + 1) * LANES] for h in both]
    edge[0] = jnp.where(lane16 == 0, corner(from_west[rows : rows + 1, :], ZONAL_LANE), edge[0])
    for h in both:
        for k in range(levels):
            uw_a[h, k, TILE : TILE + 1, :] = edge[h][k : k + 1]
    advance(jnp.int32(2 * pairs), set_a, set_b)
    store(2 * pairs * TILE, 1)
    for i, (vmem, hbm) in enumerate(outs):
        pltpu.make_async_copy(vmem, hbm, out_sem.at[i]).wait()


def body(
    east_velocity,
    north_velocity,
    heat_anomaly,
    haline_anomaly,
    spacing_lengths,
    planetary_spin,
    ocean_layer_number,
    seam_partner_index,
):
    t, s, u, v = heat_anomaly, haline_anomaly, east_velocity, north_velocity
    levels, rows, cols = t.shape
    lats, lons = lax.axis_size("lat"), lax.axis_size("lon")
    f32 = jnp.float32
    top = rows // TILE - 1
    message = 5 * levels + 8

    low3 = pl.BlockSpec((levels, TILE, cols), lambda i: (0, 0, 0))
    high3 = pl.BlockSpec((levels, TILE, cols), lambda i: (0, top, 0))
    whole = pl.BlockSpec((message, cols), lambda i: (0, 0))
    count = spacing_lengths.shape[0]
    first, second = pl.pallas_call(
        row_pack,
        grid=(1,),
        in_specs=[low3, high3] * 4
        + [
            pl.BlockSpec((count, TILE, cols), lambda i: (0, 0, 0)),
            pl.BlockSpec((count, TILE, cols), lambda i: (0, top, 0)),
            pl.BlockSpec((TILE, cols), lambda i: (0, 0)),
            pl.BlockSpec((TILE, cols), lambda i: (top, 0)),
        ],
        out_specs=[whole, whole],
        out_shape=[jax.ShapeDtypeStruct((message, cols), f32)] * 2,
        name="row_pack",
    )(t, t, s, s, u, u, v, v, spacing_lengths, spacing_lengths, ocean_layer_number, ocean_layer_number)

    axes = ("lon", "lat")

    def place(lat, lon):
        return lon * lats + lat

    swap1, swap2 = [], []
    for lon in range(lons):
        for lat in range(0, lats, 2):
            swap1 += [(place(lat, lon), place(lat + 1, lon)), (place(lat + 1, lon), place(lat, lon))]
        for lat in range(1, lats - 1, 2):
            swap2 += [(place(lat, lon), place(lat + 1, lon)), (place(lat + 1, lon), place(lat, lon))]
        swap2.append((place(lats - 1, lon), place(lats - 1, lons - 1 - lon)))
        swap2.append((place(0, lon), place(0, lons - 1 - lon)))
    got1 = lax.ppermute(first, axes, swap1)
    got2 = lax.ppermute(second, axes, swap2)

    group = 8
    slab = pl.BlockSpec((group, rows, cols), lambda i: (i, 0, 0))
    message_out = jax.ShapeDtypeStruct((rows + 8, LANES), f32)
    to_east, to_west = pl.pallas_call(
        lambda *refs: column_pack(group, *refs),
        grid=(levels // group,),
        in_specs=[slab] * 4
        + [pl.BlockSpec((2, rows, cols), lambda i: (1, 0, 0)), pl.BlockSpec((rows, cols), lambda i: (0, 0))],
        out_specs=[pl.BlockSpec((rows + 8, LANES), lambda i: (0, 0))] * 2,
        out_shape=[message_out] * 2,
        compiler_params=pltpu.CompilerParams(vmem_limit_bytes=64 * 2**20),
        cost_estimate=pl.CostEstimate(flops=20 * t.size, bytes_accessed=16 * t.size, transcendentals=0),
        name="column_pack",
    )(t, s, u, v, spacing_lengths, ocean_layer_number)

    seam = seam_partner_index.reshape(-1, LANES)
    fixed = lambda *shape: pl.BlockSpec(shape, lambda i: (0,) * len(shape))
    high_edge = pl.BlockSpec((8, LANES), lambda i: (rows // 8, 0))
    low_edge = pl.BlockSpec((8, LANES), lambda i: (0, 0))
    tight = pltpu.CompilerParams(vmem_limit_bytes=64 * 2**20)
    u_rows = pl.BlockSpec((levels, cols), lambda i: (ZONAL, 0))
    v_rows = pl.BlockSpec((levels, cols), lambda i: (MERID, 0))
    to_east, to_west = pl.pallas_call(
        corners,
        grid=(1,),
        in_specs=[u_rows, u_rows, v_rows, v_rows, fixed(*seam.shape), high_edge, low_edge],
        out_specs=[high_edge, low_edge],
        out_shape=[message_out] * 2,
        input_output_aliases={5: 0, 6: 1},
        compiler_params=tight,
        name="corners",
    )(got1, got2, got1, got2, seam, to_east, to_west)

    from_west = lax.ppermute(to_east, "lon", [(i, (i + 1) % lons) for i in range(lons)])
    from_east = lax.ppermute(to_west, "lon", [((i + 1) % lons, i) for i in range(lons)])

    north, south = pl.pallas_call(
        halo_rows,
        grid=(1,),
        in_specs=[fixed(message, cols)] * 4 + [fixed(*seam.shape)],
        out_specs=[fixed(message, cols), fixed(4 * levels, cols)],
        out_shape=[jax.ShapeDtypeStruct((message, cols), f32), jax.ShapeDtypeStruct((4 * levels, cols), f32)],
        compiler_params=tight,
        cost_estimate=pl.CostEstimate(flops=4 * t.size, bytes_accessed=2 * t.size, transcendentals=0),
        name="halo_rows",
    )(first, second, got1, got2, seam)

    halves = cols // LANES
    held = (halves, levels, rows + 2 * TILE, LANES)
    anywhere = pl.BlockSpec(memory_space=pl.ANY)
    out = jax.ShapeDtypeStruct((levels, rows, cols), f32)
    return pl.pallas_call(
        step_kernel,
        in_specs=[anywhere] * 12,
        out_specs=[anywhere] * 3,
        out_shape=[out] * 3,
        scratch_shapes=[
            pltpu.VMEM((message, cols), f32),
            pltpu.VMEM((4 * levels, cols), f32),
        ]
        + [pltpu.VMEM((rows + 8, LANES), f32)] * 3
        + [pltpu.VMEM(held, f32)] * 6
        + [
            pltpu.VMEM((5, halves, levels, TILE, LANES), f32),
            pltpu.VMEM((halves, levels, 2 * TILE, LANES), f32),
            pltpu.VMEM((halves, levels, 2 * TILE, LANES), f32),
        ]
        * 2
        + [
            pltpu.VMEM(spacing_lengths.shape, f32),
            pltpu.VMEM(planetary_spin.shape, f32),
            pltpu.VMEM((rows, cols), jnp.int32),
            pltpu.VMEM((halves, rows + TILE, LANES), f32),
        ]
        + [pltpu.VMEM((levels, rows, cols), f32)] * 3
        + [
            pltpu.VMEM((3, cols, cols), jnp.bfloat16),
            pltpu.VMEM((3, cols, cols), jnp.bfloat16),
            pltpu.VMEM((4, levels // 2, 2 * TILE, LANES), jnp.bfloat16),
            pltpu.VMEM((21, halves, rows, LANES), f32),
            pltpu.SemaphoreType.DMA((rows // TILE // 2 + 1,)),
            pltpu.SemaphoreType.DMA((8,)),
            pltpu.SemaphoreType.DMA((3,)),
        ],
        compiler_params=pltpu.CompilerParams(vmem_limit_bytes=60 * 2**20),
        name="ocean_step",
    )(t, s, u, v, spacing_lengths, planetary_spin, ocean_layer_number, north, south, to_west, from_east, from_west)


def solution(mesh):
    in_specs = (
        P(None, "lat", "lon"),
        P(None, "lat", "lon"),
        P(None, "lat", "lon"),
        P(None, "lat", "lon"),
        P(None, "lat", "lon"),
        P(None, "lat", "lon"),
        P("lat", "lon"),
        P(),
    )
    out_specs = (P(None, "lat", "lon"), P(None, "lat", "lon"), P(None, "lat", "lon"))
    return jax.shard_map(body, mesh=mesh, in_specs=in_specs, out_specs=out_specs, check_vma=False)
```
